128 devices in a mesh: grp: 2 (over core), dev: 64 (over y, x, z).
Axes of the slice: x: 4, y: 4, z: 4, core: 2. Of those that a mesh axis runs over, the one named last changes fastest.
Arguments:
- queries: bfloat16 [4096, 2048], P(('grp', 'dev')), may hold values from -400 to 400
- keys: bfloat16 [2048, 64, 2048], P(('grp', 'dev')), may hold values from -9 to 9
- values: bfloat16 [2048, 64, 2048], P(('grp', 'dev')), may hold values from -24 to 24
- counts: int32 [256], P(('grp', 'dev')), may hold values from 4 to 28, as said below
- passage_ids: int32 [256, 28], P(('grp', 'dev')), may hold values from 0 to 1023, as said below
- out_weight: bfloat16 [2048, 2048], P('grp'), may hold values from -0.125 to 0.125
Outputs:
- projected: bfloat16 [4096, 2048], P(('grp', 'dev'))
The draws below stay inside these ranges and needn't reach their ends.
Inputs may be any that keep to these rules, and one draw needn't show every extreme that they name: counts[n] is the number of live entries at the head of row n of passage_ids. `passage_ids`: an id i names passage row i % 16 of device i // 16 along dev in the question's group; the live ids of one question are distinct, entries past counts[n] are ignored. At most one of a device's questions has live passages on any one device of its group, and at most 2 live passages of one question lie on one device; in every draw some device holds live passages of exactly one question of every device of its group, and some question has 2 live passages on one device.
All inputs are finite; a program needn't handle non-finite values.
Results may differ from the reference program's by a relative error of at most 0.012.
Values may be sent and summed in bfloat16 or wider, within the bound.
A program may use at most 192 MiB of HBM per device.

```python
import math
import jax
import jax.numpy as jnp
from jax import lax

D = 2048
H = 32
HD = 64
QT = 16
PT = 64
MAXP = 28
MIN_P = 4
Q_DEV = 2
P_DEV = 16
OWNERS = 64
GROUPS = 2
QUESTIONS = 256
ROWS = 4096
PASSAGES = 2048
LANES = 1
SPREAD = 14


def routing(key):
    key_count, key_force, key_hot, key_lane, key_place, key_base = jax.random.split(key, 6)
    counts = jax.random.randint(key_count, (GROUPS, OWNERS, Q_DEV), MIN_P, MAXP + 1)
    flat_ids = jnp.arange(QUESTIONS).reshape(GROUPS, OWNERS, Q_DEV)
    forced = jax.random.randint(key_force, (), 0, QUESTIONS)
    counts = jnp.where(flat_ids == forced, MAXP, counts)
    hot_owner = jax.random.randint(key_hot, (GROUPS, 1, 1, 1), 0, OWNERS)
    lane_keys = jax.random.split(key_lane, GROUPS * OWNERS * LANES)
    orders = jax.vmap(lambda sub_key: jax.random.permutation(sub_key, OWNERS))(lane_keys)
    orders = orders.reshape(GROUPS, OWNERS, LANES, OWNERS)
    orders = jnp.where(orders == hot_owner, orders[..., :1], orders)
    at_front = jnp.arange(OWNERS)[None, None, None, :] == 0
    orders = jnp.where(at_front, hot_owner, orders)
    place_keys = jax.random.split(key_place, GROUPS * OWNERS)
    places = jax.vmap(lambda sub_key: jax.random.permutation(sub_key, Q_DEV))(place_keys)
    places = places.reshape(GROUPS, OWNERS, Q_DEV)
    lane_of = places // 2
    side_of = places % 2
    group_ids = jnp.arange(GROUPS)[:, None, None]
    device_ids = jnp.arange(OWNERS)[None, :, None]
    chosen = orders[group_ids, device_ids, lane_of]
    reach_of = jnp.minimum(counts, SPREAD)[..., None]
    column_ids = jnp.arange(MAXP)[None, None, None, :]
    column_of = column_ids % reach_of
    owner_of = jnp.take_along_axis(chosen, side_of[..., None] * SPREAD + column_of, axis=-1)
    base_slot = jax.random.randint(key_base, (GROUPS, OWNERS, Q_DEV, MAXP), 0, P_DEV)
    start_slot = jnp.take_along_axis(base_slot, column_of, axis=-1)
    local_slot = (start_slot + column_ids // reach_of) % P_DEV
    id_table = owner_of * P_DEV + local_slot
    return (counts.reshape(QUESTIONS).astype(jnp.int32), id_table.reshape(QUESTIONS, MAXP).astype(jnp.int32))


def draw_counts(key, part):
    counts, id_table = routing(key)
    return counts


def draw_passage_ids(key, part):
    counts, id_table = routing(key)
    return id_table


def draw_keys(key, part):
    key = jax.random.fold_in(key, 11)
    noise_key = jax.random.fold_in(key, 0)
    drawn = jnp.clip(1.5 * jax.random.normal(noise_key, (PASSAGES, PT, D), jnp.float32), -9.0, 9.0)
    return drawn.astype(jnp.bfloat16)


def draw_queries(key, part):
    key = jax.random.fold_in(key, 12)
    noise_key = jax.random.fold_in(key, 0)
    drawn = jnp.clip(jax.random.normal(noise_key, (ROWS, D), jnp.float32), -6.0, 6.0)
    return drawn.astype(jnp.bfloat16)


def steps_of(key, extent, cuts, low, top_value):
    level, own = 1.0, jax.random.fold_in(key, 6)
    for axis_at, shards_of in cuts:
        heights = jnp.exp(jax.random.uniform(jax.random.fold_in(own, axis_at), (shards_of,), jnp.float32, low / len(cuts), top_value / len(cuts)))
        level = level * jnp.repeat(heights, extent[axis_at] // shards_of).reshape([-1 if axis == axis_at else 1 for axis in range(len(extent))])
    return level


def gaussian(own_key, extent, width, most, cuts=(), kind=jnp.bfloat16):
    entries = width * jax.random.normal(own_key, extent, jnp.float32)
    if cuts:
        entries = entries * steps_of(own_key, extent, cuts, -0.22, 0.18)
    return jnp.clip(entries, -most, most).astype(kind)


def setup_inputs(seed: int = 0) -> dict:
    splits = jax.random.split(jax.random.key(seed), 7)
    queries = draw_queries(jax.random.fold_in(splits[6], 71), 0)
    keys = draw_keys(jax.random.fold_in(splits[6], 71), 0)
    values = gaussian(splits[2], (PASSAGES, PT, D), 4.0, 24.0, ((0, 128),))
    counts = draw_counts(jax.random.fold_in(splits[6], 71), 0)
    passage_ids = draw_passage_ids(jax.random.fold_in(splits[6], 71), 0)
    out_weight = gaussian(splits[5], (D, D), D ** -0.5, 0.125, ((0, 2),))
    return dict(queries=queries, keys=keys, values=values, counts=counts, passage_ids=passage_ids, out_weight=out_weight)


def reference(queries, keys, values, counts, passage_ids, out_weight):
    scale_factor = 1.0 / math.sqrt(HD)
    highest = lax.Precision.HIGHEST
    group_index = jnp.arange(QUESTIONS, dtype=jnp.int32) // (OWNERS * Q_DEV)
    key_rows = (passage_ids + (group_index * (OWNERS * P_DEV))[:, None]).astype(jnp.int32)
    query_heads = queries.reshape(QUESTIONS, QT, H, HD)

    def attend(packed):
        query_block, row_list, live_count = packed
        key_block = keys[row_list].astype(jnp.float32).reshape(MAXP, PT, H, HD)
        value_block = values[row_list].astype(jnp.float32).reshape(MAXP, PT, H, HD)
        scores = jnp.einsum('ahd,jthd->jhat', query_block.astype(jnp.float32), key_block, precision=highest) * scale_factor
        peak_scores = lax.optimization_barrier(jnp.max(scores, axis=-1))
        weights = jnp.exp(scores - peak_scores[..., None])
        totals = lax.optimization_barrier(jnp.sum(weights, axis=-1))
        rounded = lax.optimization_barrier(weights.astype(jnp.bfloat16)).astype(jnp.float32)
        partial_out = jnp.einsum('jhat,jthd->jahd', rounded, value_block, precision=highest)
        live_mask = (jnp.arange(MAXP) < live_count)[:, None, None]
        top_peak = lax.optimization_barrier(jnp.max(jnp.where(live_mask, peak_scores, -jnp.inf), axis=0))
        factors = jnp.where(live_mask, jnp.exp(jnp.minimum(peak_scores - top_peak, 0.0)), 0.0)
        denominator = lax.optimization_barrier(jnp.sum(factors * totals, axis=0))
        numerator = jnp.einsum('jha,jahd->ahd', factors, partial_out, precision=highest)
        attended = numerator / jnp.transpose(denominator)[:, :, None]
        return attended.astype(jnp.bfloat16).reshape(QT, D)
    attended_all = lax.map(attend, (query_heads, key_rows, counts))
    return jnp.dot(attended_all.reshape(ROWS, D), out_weight, preferred_element_type=jnp.float32).astype(jnp.bfloat16)
```

```python
import jax
import jax.numpy as jnp
from jax import lax
from jax.experimental import pallas as pl
from jax.experimental.pallas import tpu as pltpu
from jax.sharding import PartitionSpec as P

D = 2048
H = 32
HD = 64
QT = 16
PT = 64
GW = 256
GH = GW // HD
GROUPS = D // GW
LANE = 128
SIDE = 4
OWNERS = SIDE * SIDE * SIDE
HALVES = 2
HW = D // HALVES
HG = HW // GW
SPIN = 21
BATCH = 8
DEAD = -1e30
WIDE = D + LANE
CUTS = ((0, 384), (384, 384), (768, 256))
ORDERS = (("x", "y", "z"), ("y", "z", "x"), ("z", "x", "y"))
MESH = pl.DeviceIdType.MESH


def torus_kernel(
    ids_ref, mine_ref, k_hbm, v_hbm, w_hbm, out_ref,
    q0_ref, q1_ref, k_ref, v_ref, w_ref, part_ref, back_ref, stat_ref, ask_ref, told_ref, ask_smem, told_smem,
    lse_ref, factor_ref, wide_ref, sum_ref,
    load_sem, home_sem, code_send, code_recv, w_sem, ring_send, ring_recv, part_send, part_recv,
):
    me = lax.axis_index("dev")
    grp = lax.axis_index("grp")
    own = {"y": me // (SIDE * SIDE), "x": lax.rem(me // SIDE, SIDE), "z": lax.rem(me, SIDE)}
    q_refs = (q0_ref, q1_ref)

    def partner(i, sign):
        offset = lax.rem(i * SPIN, OWNERS)
        step = {"y": offset // (SIDE * SIDE), "x": lax.rem(offset // SIDE, SIDE), "z": lax.rem(offset, SIDE)}
        at = {a: lax.rem(own[a] + (step[a] if sign > 0 else SIDE - step[a]), SIDE) for a in own}
        return (at["y"] * SIDE + at["x"]) * SIDE + at["z"]

    def device(axis, at):
        spot = dict(own)
        spot[axis] = at
        return (grp, (spot["y"] * SIDE + spot["x"]) * SIDE + spot["z"])

    def moved(axis, by):
        return lax.rem(own[axis] + by, SIDE)

    loads = [
        pltpu.make_async_copy(k_hbm, k_ref, load_sem.at[0]),
        pltpu.make_async_copy(v_hbm, v_ref, load_sem.at[1]),
    ]
    for load in loads:
        load.start()
    barrier = pltpu.get_barrier_semaphore()

    def greet(i, carry):
        pl.semaphore_signal(barrier, inc=1, device_id=(grp, partner(i, 1)), device_id_type=MESH)
        return carry

    lax.fori_loop(1, OWNERS, greet, 0)
    pl.semaphore_signal(barrier, inc=1, device_id=(1 - grp, me), device_id_type=MESH)

    homes = [
        pltpu.make_async_copy(
            mine_ref.at[:, pl.ds(half * HW, HW)], q_refs[half].at[own["y"], own["x"], own["z"]], home_sem.at[half]
        )
        for half in range(HALVES)
    ]
    for home in homes:
        home.start()
    ids = jnp.broadcast_to(ids_ref[...], (OWNERS, LANE))
    owner_row = lax.broadcasted_iota(jnp.int32, (OWNERS, LANE), 0)
    key = lax.broadcasted_iota(jnp.int32, (OWNERS, LANE), 1) * 16 + (ids & 15)
    here = (ids >> 4) == owner_row
    first = jnp.min(jnp.where(here, key, 1 << 20), axis=1, keepdims=True)
    last = jnp.max(jnp.where(here, key, -1), axis=1, keepdims=True)
    code = jnp.where(last < 0, -1, (first >> 10) + ((first & 15) << 1) + ((last & 15) << 5))
    ask_ref[...] = jnp.broadcast_to(code, (OWNERS, LANE)).reshape(OWNERS, 1, LANE)

    pl.semaphore_wait(barrier, OWNERS)

    def ring_block(half, part, stage, at, rows):
        order = ORDERS[part]
        spot = {axis: own[axis] for axis in order}
        for axis in order[:stage]:
            spot[axis] = pl.ds(0, SIDE)
        spot[order[stage]] = at
        return q_refs[half].at[spot["y"], spot["x"], spot["z"], pl.ds(*rows), pl.ds(*CUTS[part])]

    whole, lower, upper = (0, 2 * QT), (0, QT), (QT, QT)
    both = ((0, 1, lower), (1, SIDE - 1, upper))

    def ring_copy(half, part, stage, kind, at, rows, to, source=None):
        dst = ring_block(half, part, stage, at, rows)
        return pltpu.make_async_remote_copy(
            src_ref=dst if source is None else source,
            dst_ref=dst,
            send_sem=ring_send.at[half, part, stage, kind],
            recv_sem=ring_recv.at[half, part, stage, kind],
            device_id=device(ORDERS[part][stage], to),
            device_id_type=MESH,
        )

    def ring_own(half, part, stage, kind, by):
        axis = ORDERS[part][stage]
        source = None
        if stage == 0:
            source = mine_ref.at[:, pl.ds(half * HW + CUTS[part][0], CUTS[part][1])]
        return ring_copy(half, part, stage, kind, own[axis], whole, moved(axis, by), source)

    def ring_pass(half, part, stage, kind, by, rows):
        axis = ORDERS[part][stage]
        return ring_copy(half, part, stage, 2 + kind, moved(axis, SIDE - by), rows, moved(axis, by))

    def ring_start(half, stage):
        for part in range(3):
            for kind, by, rows in both:
                ring_own(half, part, stage, kind, by).start()

    def ring_forward(half, stage):
        for kind, by, rows in both:
            for part in range(3):
                axis = ORDERS[part][stage]
                came = moved(axis, SIDE - by)
                ring_copy(half, part, stage, kind, came, whole, came).wait_recv()
                ring_pass(half, part, stage, kind, by, rows).start()

    def ring_end(half, stage):
        for part in range(3):
            axis = ORDERS[part][stage]
            for kind, by, rows in both:
                ring_copy(half, part, stage, 2 + kind, moved(axis, 2), rows, moved(axis, by)).wait_recv()

    def ring_sent(half):
        for stage in range(3):
            for part in range(3):
                for kind, by, rows in both:
                    ring_own(half, part, stage, kind, by).wait_send()
                    ring_pass(half, part, stage, kind, by, rows).wait_send()

    def tell(i, sign):
        to, source = partner(i, 1), partner(i, -1)
        return pltpu.make_async_remote_copy(
            src_ref=ask_ref.at[to],
            dst_ref=told_ref.at[me if sign > 0 else source],
            send_sem=code_send.at[i],
            recv_sem=code_recv.at[i],
            device_id=(grp, to),
            device_id_type=MESH,
        )

    def tell_start(i, carry):
        tell(i, 1).start()
        return carry

    def tell_wait(i, carry):
        tell(i, 1).wait_send()
        tell(i, -1).wait_recv()
        return carry

    half_rows = D // 2
    w_home = pltpu.make_async_copy(w_hbm, w_ref.at[pl.ds(grp * half_rows, half_rows)], home_sem.at[2])
    w_give = pltpu.make_async_remote_copy(
        src_ref=w_hbm,
        dst_ref=w_ref.at[pl.ds(grp * half_rows, half_rows)],
        send_sem=w_sem.at[0],
        recv_sem=w_sem.at[1],
        device_id=(1 - grp, me),
        device_id_type=MESH,
    )
    w_take = pltpu.make_async_remote_copy(
        src_ref=w_hbm,
        dst_ref=w_ref.at[pl.ds((1 - grp) * half_rows, half_rows)],
        send_sem=w_sem.at[0],
        recv_sem=w_sem.at[1],
        device_id=(1 - grp, me),
        device_id_type=MESH,
    )

    ring_start(0, 0)
    lax.fori_loop(1, OWNERS, tell_start, 0)
    told_home = pltpu.make_async_copy(ask_ref.at[me], told_ref.at[me], home_sem.at[3])
    told_home.start()
    homes[0].wait()
    ring_forward(0, 0)
    ring_end(0, 0)
    ring_start(0, 1)
    ring_forward(0, 1)
    ring_end(0, 1)
    ring_start(0, 2)
    ask_move = pltpu.make_async_copy(ask_ref, ask_smem, home_sem.at[4])
    ask_move.start()
    told_home.wait()
    lax.fori_loop(1, OWNERS, tell_wait, 0)
    told_move = pltpu.make_async_copy(told_ref, told_smem, home_sem.at[5])
    told_move.start()
    ring_forward(0, 2)
    w_home.start()
    w_give.start()
    for load in loads:
        load.wait()
    homes[1].wait()
    told_move.wait()
    ask_move.wait()
    ring_end(0, 2)
    ring_start(1, 0)

    row_head = lax.broadcasted_iota(jnp.int32, (GH * QT, GW), 0) // QT
    lane_head = lax.broadcasted_iota(jnp.int32, (GH * QT, GW), 1) // HD
    diag = (row_head == lane_head).astype(jnp.float32).astype(jnp.bfloat16)
    stat_lane = lax.broadcasted_iota(jnp.int32, (QT, LANE), 1)
    near = stat_lane < HD

    def answer(half, i, sign):
        cols = pl.ds(0, HW) if half == 0 else pl.ds(HW, WIDE - HW)
        return pltpu.make_async_remote_copy(
            src_ref=part_ref.at[i, :, cols],
            dst_ref=back_ref.at[me if sign > 0 else partner(i, -1), :, cols],
            send_sem=part_send.at[half, i],
            recv_sem=part_recv.at[half, i],
            device_id=(grp, partner(i, 1)),
            device_id_type=MESH,
        )

    def keep():
        return pltpu.make_async_copy(part_ref.at[0], back_ref.at[me], home_sem.at[3])

    def attend(half, b):
        base = b * BATCH
        slots, stats, spots = [], [], []
        for n in range(BATCH):
            s = partner(base + n, 1)
            told = jnp.maximum(told_smem[s, 0, 0], 0)
            slots.append((told & 1, (told >> 1) & 15, (told >> 5) & 15))
            spots.append((s // (SIDE * SIDE), lax.rem(s // SIDE, SIDE), lax.rem(s, SIDE)))
            stats.append(stat_ref[base + n] if half else jnp.zeros((QT, LANE), jnp.float32))
        items = [(n, g) for n in range(BATCH) for g in range(HG)]
        scores, weights = {}, {}

        def score(n, g):
            which, first, second = slots[n]
            near_cols = slice(g * GW, (g + 1) * GW)
            cols = slice(half * HW + g * GW, half * HW + (g + 1) * GW)
            q_ref = q_refs[half]
            q = jnp.where(which > 0, q_ref[(*spots[n], slice(QT, 2 * QT), near_cols)], q_ref[(*spots[n], slice(0, QT), near_cols)])
            lhs = jnp.concatenate([q * jnp.bfloat16(0.125)] * GH, axis=0) * diag
            k = jnp.concatenate([k_ref[first, :, cols], k_ref[second, :, cols]], axis=0)
            scores[n, g] = lax.dot_general(lhs, k, (((1,), (1,)), ((), ())), preferred_element_type=jnp.float32)

        def weigh(n, g):
            which, first, second = slots[n]
            values = scores.pop((n, g))
            peak = jnp.max(values, axis=1, keepdims=True)
            shaped = jnp.exp(values - peak)
            total = jnp.sum(shaped, axis=1, keepdims=True)
            lse = peak + jnp.log(total * jnp.where(first == second, 0.5, 1.0))
            for h in range(GH):
                head = (half * HG + g) * GH + h
                stats[n] = jnp.where(stat_lane % H == head, lse[h * QT : (h + 1) * QT], stats[n])
            weights[n, g] = (shaped.astype(jnp.bfloat16), 1.0 / total)

        def apply(n, g):
            which, first, second = slots[n]
            start = half * HW + g * GW
            cols = slice(start, start + GW)
            shaped, inverse = weights.pop((n, g))
            v = jnp.concatenate([v_ref[first, :, cols], v_ref[second, :, cols]], axis=0)
            full = jnp.dot(shaped, v, preferred_element_type=jnp.float32)
            for t in range(GW // LANE):
                lanes = slice(t * LANE, (t + 1) * LANE)
                a, b = (slice((2 * t + e) * QT, (2 * t + e + 1) * QT) for e in (0, 1))
                part = jnp.where(near, full[a, lanes] * inverse[a], full[b, lanes] * inverse[b])
                part_ref[base + n, :, start + t * LANE : start + (t + 1) * LANE] = part.astype(jnp.bfloat16)

        for at in range(len(items) + 4):
            if at < len(items):
                score(*items[at])
            if 2 <= at < len(items) + 2:
                weigh(*items[at - 2])
            if 4 <= at:
                apply(*items[at - 4])
        for n in range(BATCH):
            if half == 0:
                stat_ref[base + n] = stats[n]
                continue
            high = stats[n].astype(jnp.bfloat16).astype(jnp.float32)
            rest = stats[n] - high
            middle = rest.astype(jnp.bfloat16).astype(jnp.float32)
            low = rest - middle
            pieces = jnp.where(stat_lane < H, high, jnp.where(stat_lane < 2 * H, middle, low))
            part_ref[base + n, :, D:] = jnp.where(stat_lane < 3 * H, pieces, 0.0).astype(jnp.bfloat16)
        for n in range(BATCH):
            if n:
                answer(half, base + n, 1).start()
            else:

                @pl.when(b > 0)
                def _():
                    answer(half, base, 1).start()

    def attend_first(b, carry):
        attend(0, b)
        steps = (
            lambda: ring_forward(1, 0),
            lambda: (ring_end(1, 0), ring_start(1, 1)),
            lambda: ring_forward(1, 1),
            lambda: (ring_end(1, 1), ring_start(1, 2)),
            None,
            lambda: ring_forward(1, 2),
        )
        for at, step in enumerate(steps):
            if step is not None:
                pl.when(b == at)(lambda step=step: (step(), None)[1])
        return carry

    def attend_second(b, carry):
        attend(1, b)
        return carry

    lax.fori_loop(0, OWNERS // BATCH, attend_first, 0)
    ring_end(1, 2)
    lax.fori_loop(0, OWNERS // BATCH, attend_second, 0)
    keep().start()
    ring_sent(0)
    ring_sent(1)
    keep().wait()

    def finish(i, carry):
        for half in range(HALVES):
            answer(half, i, 1).wait_send()
            answer(half, i, -1).wait_recv()
        return carry

    lax.fori_loop(1, OWNERS, finish, 0)

    fold_row = lax.broadcasted_iota(jnp.int32, (LANE, LANE), 0)
    fold_lane = lax.broadcasted_iota(jnp.int32, (LANE, LANE), 1)
    fold = ((fold_row < 3 * H) & (fold_row % H == fold_lane % H)).astype(jnp.float32).astype(jnp.bfloat16)
    lse_ref[...] = jnp.dot(
        back_ref[:, :, D:].reshape(OWNERS * QT, LANE), fold, preferred_element_type=jnp.float32
    ).reshape(OWNERS, QT, LANE)

    def question(o):
        asked = ask_smem[o, 0, 0]
        return jnp.where(asked < 0, -1, asked & 1)

    def highest(o, tops):
        which, lse = question(o), lse_ref[o]
        return tuple(jnp.maximum(top, jnp.where(which == n, lse, DEAD)) for n, top in enumerate(tops))

    bottom = jnp.full((QT, LANE), DEAD, jnp.float32)
    tops = lax.fori_loop(0, OWNERS, highest, (bottom, bottom), unroll=8)

    def weigh_all(o, totals):
        which = question(o)
        factor = jnp.exp(jnp.minimum(lse_ref[o] - jnp.where(which == 1, tops[1], tops[0]), 0.0))
        factor = jnp.where(which < 0, 0.0, factor)
        lse_ref[o] = factor
        return tuple(total + jnp.where(which == n, factor, 0.0) for n, total in enumerate(totals))

    nothing = jnp.zeros((QT, LANE), jnp.float32)
    totals = lax.fori_loop(0, OWNERS, weigh_all, (nothing, nothing), unroll=8)
    shares = tuple(1.0 / total for total in totals)

    def scale(o, carry):
        factor = lse_ref[o] * jnp.where(question(o) == 1, shares[1], shares[0])
        high = factor.astype(jnp.bfloat16).astype(jnp.float32)
        pieces = jnp.where(stat_lane < H, high, jnp.where(stat_lane < 2 * H, factor - high, 0.0))
        factor_ref[o] = pieces.astype(jnp.bfloat16)
        return carry

    lax.fori_loop(0, OWNERS, scale, 0, unroll=8)
    w_home.wait()
    w_give.wait_send()
    w_take.wait_recv()
    sum_ref[...] = jnp.zeros(sum_ref.shape, jnp.float32)
    spread_row = lax.broadcasted_iota(jnp.int32, (LANE, GW), 0)
    spread_lane = lax.broadcasted_iota(jnp.int32, (LANE, GW), 1)

    def project(g, carry):
        cols = pl.ds(pl.multiple_of(g * GW, GW), GW)
        spread = (spread_row < 2 * H) & (spread_row % H == g * GH + spread_lane // HD)
        wide_ref[...] = jnp.dot(
            factor_ref[...].reshape(OWNERS * QT, LANE),
            spread.astype(jnp.float32).astype(jnp.bfloat16),
            preferred_element_type=jnp.float32,
        ).reshape(OWNERS, QT, GW)

        def add(o, sums):
            which = question(o)
            term = wide_ref[o] * back_ref[o, :, cols].astype(jnp.float32)
            return tuple(total + jnp.where(which == n, term, 0.0) for n, total in enumerate(sums))

        empty = jnp.zeros((QT, GW), jnp.float32)
        attended = jnp.concatenate(lax.fori_loop(0, OWNERS, add, (empty, empty), unroll=8), axis=0)
        sum_ref[...] += jnp.dot(attended.astype(jnp.bfloat16), w_ref[cols, :], preferred_element_type=jnp.float32)
        return carry

    lax.fori_loop(0, GROUPS, project, 0)
    out_ref[...] = sum_ref[...].astype(jnp.bfloat16)


def on_device(queries, keys, values, counts, passage_ids, out_weight):
    list_len = passage_ids.shape[1]
    listed = jnp.arange(list_len)[None, :] < counts[:, None]
    ids = jnp.where(listed, passage_ids, -1).astype(jnp.int32)
    ids = jnp.pad(ids, ((0, 0), (0, LANE // 2 - list_len)), constant_values=-1).reshape(1, LANE)
    half_shape = (SIDE, SIDE, SIDE, 2 * QT, HW)
    return pl.pallas_call(
        torus_kernel,
        out_shape=jax.ShapeDtypeStruct((2 * QT, D), jnp.bfloat16),
        in_specs=[pl.BlockSpec(memory_space=pltpu.VMEM)] * 2 + [pl.BlockSpec(memory_space=pl.ANY)] * 3,
        out_specs=pl.BlockSpec(memory_space=pltpu.VMEM),
        scratch_shapes=[
            pltpu.VMEM(half_shape, jnp.bfloat16),
            pltpu.VMEM(half_shape, jnp.bfloat16),
            pltpu.VMEM(keys.shape, jnp.bfloat16),
            pltpu.VMEM(values.shape, jnp.bfloat16),
            pltpu.VMEM((D, D), jnp.bfloat16),
            pltpu.VMEM((OWNERS, QT, WIDE), jnp.bfloat16),
            pltpu.VMEM((OWNERS, QT, WIDE), jnp.bfloat16),
            pltpu.VMEM((OWNERS, QT, LANE), jnp.float32),
            pltpu.VMEM((OWNERS, 1, LANE), jnp.int32),
            pltpu.VMEM((OWNERS, 1, LANE), jnp.int32),
            pltpu.SMEM((OWNERS, 1, LANE), jnp.int32),
            pltpu.SMEM((OWNERS, 1, LANE), jnp.int32),
            pltpu.VMEM((OWNERS, QT, LANE), jnp.float32),
            pltpu.VMEM((OWNERS, QT, LANE), jnp.bfloat16),
            pltpu.VMEM((OWNERS, QT, GW), jnp.float32),
            pltpu.VMEM((2 * QT, D), jnp.float32),
            pltpu.SemaphoreType.DMA((2,)),
            pltpu.SemaphoreType.DMA((6,)),
            pltpu.SemaphoreType.DMA((OWNERS,)),
            pltpu.SemaphoreType.DMA((OWNERS,)),
            pltpu.SemaphoreType.DMA((2,)),
            pltpu.SemaphoreType.DMA((HALVES, 3, 3, 4)),
            pltpu.SemaphoreType.DMA((HALVES, 3, 3, 4)),
            pltpu.SemaphoreType.DMA((HALVES, OWNERS)),
            pltpu.SemaphoreType.DMA((HALVES, OWNERS)),
        ],
        compiler_params=pltpu.CompilerParams(
            vmem_limit_bytes=60 * 2**20, collective_id=0, has_side_effects=True
        ),
        cost_estimate=pl.CostEstimate(flops=40 * 10**9, bytes_accessed=20 * 2**20, transcendentals=4 * 10**6),
        name="torus",
    )(ids, queries, keys, values, out_weight)


def solution(mesh):
    placed = (
        P(("grp", "dev"), None),
        P(("grp", "dev"), None, None),
        P(("grp", "dev"), None, None),
        P(("grp", "dev")),
        P(("grp", "dev"), None),
        P("grp", None),
    )
    return jax.shard_map(
        on_device, mesh=mesh, in_specs=placed, out_specs=P(("grp", "dev"), None), check_vma=False
    )
```

```python
import jax
import jax.numpy as jnp
from jax import lax
from jax.experimental import pallas as pl
from jax.experimental.pallas import tpu as pltpu
from jax.sharding import PartitionSpec as P

D = 2048
H = 32
HD = 64
QT = 16
PT = 64
GW = 256
GH = GW // HD
GROUPS = D // GW
LANE = 128
SIDE = 4
OWNERS = SIDE * SIDE * SIDE
WS = (768, 768, 512)
STARTS = (0, 768, 1536)
BATCH = 8
DEAD = -1e30
CUTS = (
    ((0, 256), (256, 256), (512, 256)),
    ((0, 256), (256, 256), (512, 256)),
    ((0, 256), (256, 128), (384, 128)),
)
ORDERS = (("x", "y", "z"), ("y", "z", "x"), ("z", "x", "y"))
MESH = pl.DeviceIdType.MESH


def torus_kernel(
    ids_ref, mine_ref, k_hbm, v_hbm, w_hbm, out_ref,
    q0_ref, q1_ref, q2_ref, part0_ref, part1_ref, part2_ref, near0_ref, near1_ref, near2_ref,
    mid0_ref, mid1_ref, mid2_ref, next0_ref, next1_ref, next2_ref,
    late0_ref, late1_ref, late2_ref, last0_ref, last1_ref, last2_ref,
    k_ref, v_ref, w_ref, list_ref, code_ref, code_smem, seen_ref, factor_ref, wide_ref, sum_ref,
    load_sem, home_sem, list_send, list_recv, w_sem, ring_send, ring_recv,
    one_send, one_recv, two_send, two_recv, three_send, three_recv,
):
    me = lax.axis_index("dev")
    grp = lax.axis_index("grp")
    own = {"y": me >> 4, "x": (me >> 2) & 3, "z": me & 3}
    stride = {"y": SIDE * SIDE, "x": SIDE, "z": 1}
    line = {
        axis: {by: (grp, me + ((((own[axis] + by) & 3) - own[axis]) * stride[axis])) for by in range(1, SIDE)}
        for axis in own
    }
    q_refs = (q0_ref, q1_ref, q2_ref)
    parts = (part0_ref, part1_ref, part2_ref)
    nears = (near0_ref, near1_ref, near2_ref)
    mids = (mid0_ref, mid1_ref, mid2_ref)
    nexts = (next0_ref, next1_ref, next2_ref)
    lates = (late0_ref, late1_ref, late2_ref)
    lasts = (last0_ref, last1_ref, last2_ref)

    loads = [
        pltpu.make_async_copy(k_hbm, k_ref, load_sem.at[0]),
        pltpu.make_async_copy(v_hbm, v_ref, load_sem.at[1]),
    ]
    for load in loads:
        load.start()
    barrier = pltpu.get_barrier_semaphore()
    for axis in line:
        for by in line[axis]:
            pl.semaphore_signal(barrier, inc=1, device_id=line[axis][by], device_id_type=MESH)
    pl.semaphore_signal(barrier, inc=1, device_id=(1 - grp, me), device_id_type=MESH)
    homes = [
        pltpu.make_async_copy(
            mine_ref.at[:, pl.ds(STARTS[phase], WS[phase])], q_refs[phase].at[0, 0, 0], home_sem.at[phase]
        )
        for phase in range(3)
    ]
    for home in homes:
        home.start()
    list_ref[0, 0, 0] = ids_ref[...]
    pl.semaphore_wait(barrier, 10)

    whole, lower, upper = (0, 2 * QT), (0, QT), (QT, QT)
    both = ((0, 1, 3, lower), (1, 3, 1, upper))

    def ring_block(phase, part, stage, at, rows):
        order = ORDERS[part]
        spot = {axis: 0 for axis in order}
        for axis in order[:stage]:
            spot[axis] = pl.ds(0, SIDE)
        spot[order[stage]] = at
        first, second, third = (spot[axis] for axis in ORDERS[phase])
        return q_refs[phase].at[first, second, third, pl.ds(*rows), pl.ds(*CUTS[phase][part])]

    def ring_own(phase, part, stage, kind, by, at):
        if stage == 0:
            cut = CUTS[phase][part]
            source = mine_ref.at[:, pl.ds(STARTS[phase] + cut[0], cut[1])]
        else:
            source = ring_block(phase, part, stage, 0, whole)
        return pltpu.make_async_remote_copy(
            src_ref=source,
            dst_ref=ring_block(phase, part, stage, at, whole),
            send_sem=ring_send.at[phase, part, stage, kind],
            recv_sem=ring_recv.at[phase, part, stage, kind],
            device_id=line[ORDERS[part][stage]][by],
            device_id_type=MESH,
        )

    def ring_pass(phase, part, stage, kind, by, at, rows):
        return pltpu.make_async_remote_copy(
            src_ref=ring_block(phase, part, stage, at, rows),
            dst_ref=ring_block(phase, part, stage, 2, rows),
            send_sem=ring_send.at[phase, part, stage, 2 + kind],
            recv_sem=ring_recv.at[phase, part, stage, 2 + kind],
            device_id=line[ORDERS[part][stage]][by],
            device_id_type=MESH,
        )

    def ring_start(phase, stage):
        for part in range(3):
            for kind, by, at, rows in both:
                ring_own(phase, part, stage, kind, by, at).start()

    def ring_forward(phase, stage):
        for kind, by, at, rows in both:
            for part in range(3):
                ring_own(phase, part, stage, kind, by, at).wait_recv()
                ring_pass(phase, part, stage, kind, by, at, rows).start()

    def ring_end(phase, stage):
        for part in range(3):
            for kind, by, at, rows in both:
                ring_pass(phase, part, stage, kind, by, at, rows).wait_recv()

    def ring_sent(phase):
        for stage in range(3):
            for part in range(3):
                for kind, by, at, rows in both:
                    ring_own(phase, part, stage, kind, by, at).wait_send()
                    ring_pass(phase, part, stage, kind, by, at, rows).wait_send()

    def list_copy(stage, by):
        order = ("x", "y", "z")
        spot = {axis: 0 for axis in order}
        for axis in order[:stage]:
            spot[axis] = pl.ds(0, SIDE)
        source = list_ref.at[spot["y"], spot["x"], spot["z"]]
        spot[order[stage]] = SIDE - by
        return pltpu.make_async_remote_copy(
            src_ref=source,
            dst_ref=list_ref.at[spot["y"], spot["x"], spot["z"]],
            send_sem=list_send.at[stage, by],
            recv_sem=list_recv.at[stage, by],
            device_id=line[order[stage]][by],
            device_id_type=MESH,
        )

    def list_start(stage):
        for by in range(1, SIDE):
            list_copy(stage, by).start()

    def list_end(stage):
        for by in range(1, SIDE):
            list_copy(stage, by).wait_recv()

    w_rows = D // 2
    w_home = pltpu.make_async_copy(w_hbm, w_ref.at[pl.ds(grp * w_rows, w_rows)], home_sem.at[3])
    w_give = pltpu.make_async_remote_copy(
        src_ref=w_hbm,
        dst_ref=w_ref.at[pl.ds(grp * w_rows, w_rows)],
        send_sem=w_sem.at[0],
        recv_sem=w_sem.at[1],
        device_id=(1 - grp, me),
        device_id_type=MESH,
    )
    w_take = pltpu.make_async_remote_copy(
        src_ref=w_hbm,
        dst_ref=w_ref.at[pl.ds((1 - grp) * w_rows, w_rows)],
        send_sem=w_sem.at[0],
        recv_sem=w_sem.at[1],
        device_id=(1 - grp, me),
        device_id_type=MESH,
    )

    list_start(0)
    ring_start(0, 0)
    for home in homes:
        home.wait()
    list_end(0)
    list_start(1)
    ring_forward(0, 0)
    list_end(1)
    list_start(2)
    ring_end(0, 0)
    ring_start(0, 1)
    ring_forward(0, 1)
    ring_end(0, 1)
    ring_start(0, 2)
    list_end(2)
    ids = list_ref[...].reshape(OWNERS, LANE)
    key = lax.broadcasted_iota(jnp.int32, (OWNERS, LANE), 1) * 16 + (ids & 15)
    here = (ids >> 4) == me
    first = jnp.min(jnp.where(here, key, 1 << 20), axis=1, keepdims=True)
    last = jnp.max(jnp.where(here, key, -1), axis=1, keepdims=True)
    code = jnp.where(last < 0, -1, (first >> 10) + ((first & 15) << 1) + ((last & 15) << 5))
    code_ref[...] = jnp.broadcast_to(code, (OWNERS, LANE)).reshape(OWNERS, 1, LANE)
    code_move = pltpu.make_async_copy(code_ref, code_smem, home_sem.at[4])
    code_move.start()
    ring_forward(0, 2)
    ring_start(1, 0)
    w_home.start()
    w_give.start()
    for load in loads:
        load.wait()
    code_move.wait()
    ring_end(0, 2)
    ring_forward(1, 0)

    row_head = lax.broadcasted_iota(jnp.int32, (GH * QT, GW), 0) // QT
    lane_head = lax.broadcasted_iota(jnp.int32, (GH * QT, GW), 1) // HD
    diag = (row_head == lane_head).astype(jnp.float32).astype(jnp.bfloat16)
    stat_lane = lax.broadcasted_iota(jnp.int32, (QT, LANE), 1)
    near = stat_lane < HD

    def tree(sources, targets, send_sem, recv_sem, phase, stage, by):
        return pltpu.make_async_remote_copy(
            src_ref=sources[phase].at[by],
            dst_ref=targets[phase].at[by - 1],
            send_sem=send_sem.at[phase, by],
            recv_sem=recv_sem.at[phase, by],
            device_id=line[ORDERS[phase][stage]][by],
            device_id_type=MESH,
        )

    def one(phase, by):
        return tree(parts, nears, one_send, one_recv, phase, 0, by)

    def two(phase, by):
        return tree(mids, nexts, two_send, two_recv, phase, 1, by)

    def three(phase, by):
        return tree(lates, lasts, three_send, three_recv, phase, 2, by)

    def split(value):
        high = value.astype(jnp.bfloat16).astype(jnp.float32)
        rest = value - high
        middle = rest.astype(jnp.bfloat16).astype(jnp.float32)
        return jnp.where(stat_lane < H, high, jnp.where(stat_lane < 2 * H, middle, rest - middle))

    def attend(phase, b):
        width = WS[phase]
        q_ref, part_ref = q_refs[phase], parts[phase]
        slots, stats, places, tags = [], [], [], []
        for n in range(BATCH):
            place = (((b >> 1) + 1) & 3, (b & 1) * 2 + n // SIDE, n % SIDE)
            at = dict(zip(ORDERS[phase], place))
            told = code_smem[(at["y"] << 4) + (at["x"] << 2) + at["z"], 0, 0]
            code = jnp.maximum(told, 0)
            slots.append((code & 1, (code >> 1) & 15, (code >> 5) & 15))
            tags.append(jnp.where(told < 0, -1.0, jnp.where((code & 1) > 0, 1.0, 0.0)))
            places.append(place)
            stats.append(jnp.zeros((QT, LANE), jnp.float32))
        items = [(n, g) for n in range(BATCH) for g in range(width // GW)]
        scores, weights = {}, {}

        def score(n, g):
            which, first, second = slots[n]
            near_cols = slice(g * GW, (g + 1) * GW)
            cols = slice(STARTS[phase] + g * GW, STARTS[phase] + (g + 1) * GW)
            q = jnp.where(
                which > 0, q_ref[(*places[n], slice(QT, 2 * QT), near_cols)], q_ref[(*places[n], slice(0, QT), near_cols)]
            )
            lhs = jnp.concatenate([q * jnp.bfloat16(0.125)] * GH, axis=0) * diag
            k = jnp.concatenate([k_ref[first, :, cols], k_ref[second, :, cols]], axis=0)
            scores[n, g] = lax.dot_general(lhs, k, (((1,), (1,)), ((), ())), preferred_element_type=jnp.float32)

        def weigh(n, g):
            which, first, second = slots[n]
            values = scores.pop((n, g))
            peak = jnp.max(values, axis=1, keepdims=True)
            shaped = jnp.exp(values - peak)
            total = jnp.sum(shaped, axis=1, keepdims=True)
            lse = peak + jnp.log(total * jnp.where(first == second, 0.5, 1.0))
            for h in range(GH):
                head = STARTS[phase] // HD + g * GH + h
                stats[n] = jnp.where(stat_lane % H == head, lse[h * QT : (h + 1) * QT], stats[n])
            weights[n, g] = (shaped.astype(jnp.bfloat16), 1.0 / total)

        def apply(n, g):
            which, first, second = slots[n]
            cols = slice(STARTS[phase] + g * GW, STARTS[phase] + (g + 1) * GW)
            shaped, inverse = weights.pop((n, g))
            v = jnp.concatenate([v_ref[first, :, cols], v_ref[second, :, cols]], axis=0)
            full = jnp.dot(shaped, v, preferred_element_type=jnp.float32)
            for t in range(GW // LANE):
                lanes = slice(t * LANE, (t + 1) * LANE)
                a, b = (slice((2 * t + e) * QT, (2 * t + e + 1) * QT) for e in (0, 1))
                part = jnp.where(near, full[a, lanes] * inverse[a], full[b, lanes] * inverse[b])
                start = g * GW + t * LANE
                part_ref[(*places[n], slice(None), slice(start, start + LANE))] = part.astype(jnp.bfloat16)

        for at in range(len(items) + 4):
            if at < len(items):
                score(*items[at])
            if 2 <= at < len(items) + 2:
                weigh(*items[at - 2])
            if 4 <= at:
                apply(*items[at - 4])
        for n in range(BATCH):
            pieces = jnp.where(stat_lane < 3 * H, split(stats[n]), tags[n])
            part_ref[(*places[n], slice(None), slice(width, width + LANE))] = pieces.astype(jnp.bfloat16)
    fold_row = lax.broadcasted_iota(jnp.int32, (LANE, 2 * LANE), 0)
    fold_lane = lax.broadcasted_iota(jnp.int32, (LANE, 2 * LANE), 1)
    fold = ((fold_lane < LANE) & (fold_row < 3 * H) & (fold_row % H == fold_lane % H)) | (
        (fold_lane >= LANE) & (fold_row == 3 * H)
    )
    fold = fold.astype(jnp.float32).astype(jnp.bfloat16)
    spread_row = lax.broadcasted_iota(jnp.int32, (LANE, GW), 0)
    spread_head = lax.broadcasted_iota(jnp.int32, (LANE, GW), 1) // HD

    def spread(phase, g):
        head = STARTS[phase] // HD + g * GH + spread_head
        chosen = (spread_row < 2 * H) & (spread_row % H == head)
        return chosen.astype(jnp.float32).astype(jnp.bfloat16)

    def merge_first(phase):
        width = WS[phase]
        part_ref, near_ref, mid_ref = parts[phase], nears[phase], mids[phase]

        for by in range(1, SIDE):
            one(phase, by).wait_send()
            one(phase, by).wait_recv()
        count = SIDE * SIDE
        for d in range(SIDE):
            stat = near_ref[d - 1, :, :, :, width:] if d else part_ref[0, :, :, :, width:]
            seen_ref[d] = jnp.dot(stat.reshape(count * QT, LANE), fold, preferred_element_type=jnp.float32)

        def weigh(j, carry):
            rows = pl.ds(pl.multiple_of(j * QT, QT), QT)
            lses = [seen_ref[d, rows, :LANE] for d in range(SIDE)]
            tags = [seen_ref[d, rows, LANE:] for d in range(SIDE)]
            tops = []
            for n in range(2):
                top = jnp.full((QT, LANE), DEAD, jnp.float32)
                for lse, tag in zip(lses, tags):
                    top = jnp.maximum(top, jnp.where(tag == n, lse, DEAD))
                tops.append(top)
            terms = [
                jnp.exp(jnp.minimum(lse - jnp.where(tag == 1.0, tops[1], tops[0]), 0.0)) for lse, tag in zip(lses, tags)
            ]
            inverses = []
            for n in range(2):
                kept = [jnp.where(tag == n, term, 0.0) for term, tag in zip(terms, tags)]
                total = kept[0] + kept[1] + kept[2] + kept[3]
                inverses.append(1.0 / jnp.maximum(total, 1e-30))
                lse = tops[n] + jnp.log(jnp.maximum(total, 1e-30))
                mid_ref[j >> 2, j & 3, n, :, width:] = jnp.where(
                    stat_lane < 3 * H, split(lse), 0.0
                ).astype(jnp.bfloat16)
            for d in range(SIDE):
                share = jnp.where(tags[d] < 0.0, 0.0, terms[d] * jnp.where(tags[d] == 1.0, inverses[1], inverses[0]))
                high = share.astype(jnp.bfloat16).astype(jnp.float32)
                pieces = jnp.where(stat_lane < H, high, jnp.where(stat_lane < 2 * H, share - high, 0.0))
                factor_ref[d, rows, :] = pieces.astype(jnp.bfloat16)
            return carry

        lax.fori_loop(0, count, weigh, 0, unroll=2)
        for g in range(width // GW):
            cols = slice(g * GW, (g + 1) * GW)
            wide_ref[...] = jnp.dot(
                factor_ref[...].reshape(SIDE * count * QT, LANE), spread(phase, g), preferred_element_type=jnp.float32
            ).reshape(SIDE, count * QT, GW)

            def add(j, carry):
                rows = pl.ds(pl.multiple_of(j * QT, QT), QT)
                second, third = j >> 2, j & 3
                blocks = [part_ref[0, second, third, :, cols]]
                blocks += [near_ref[d - 1, second, third, :, cols] for d in range(1, SIDE)]
                totals = [jnp.zeros((QT, GW), jnp.float32)] * 2
                for d in range(SIDE):
                    term = blocks[d].astype(jnp.float32) * wide_ref[d, rows, :]
                    tag = seen_ref[d, rows, LANE:]
                    tag = jnp.concatenate([tag, tag], axis=1)
                    totals = [total + jnp.where(tag == n, term, 0.0) for n, total in enumerate(totals)]
                for n in range(2):
                    mid_ref[second, third, n, :, cols] = totals[n].astype(jnp.bfloat16)
                return carry

            lax.fori_loop(0, count, add, 0, unroll=4)
        for by in range(1, SIDE):
            two(phase, by).start()

    def merge(phase, count, sources, stat_out, data_out):
        width = WS[phase]
        rows = count * QT
        lses = [
            jnp.dot(
                source(slice(width, width + LANE)).reshape(rows, LANE), fold[:, :LANE], preferred_element_type=jnp.float32
            )
            for source in sources
        ]
        top = jnp.maximum(jnp.maximum(lses[0], lses[1]), jnp.maximum(lses[2], lses[3]))
        terms = [jnp.exp(lse - top) for lse in lses]
        total = terms[0] + terms[1] + terms[2] + terms[3]
        inverse = 1.0 / total
        lane = lax.broadcasted_iota(jnp.int32, (rows, LANE), 1)
        for d in range(SIDE):
            share = terms[d] * inverse
            high = share.astype(jnp.bfloat16).astype(jnp.float32)
            pieces = jnp.where(lane < H, high, jnp.where(lane < 2 * H, share - high, 0.0))
            factor_ref[d, :rows, :] = pieces.astype(jnp.bfloat16)
        if stat_out is not None:
            value = top + jnp.log(total)
            high = value.astype(jnp.bfloat16).astype(jnp.float32)
            rest = value - high
            middle = rest.astype(jnp.bfloat16).astype(jnp.float32)
            pieces = jnp.where(lane < H, high, jnp.where(lane < 2 * H, middle, jnp.where(lane < 3 * H, rest - middle, 0.0)))
            stat_out(pieces.astype(jnp.bfloat16))
        for g in range(width // GW):
            cols = slice(g * GW, (g + 1) * GW)
            result = jnp.zeros((rows, GW), jnp.float32)
            for d in range(SIDE):
                wide = jnp.dot(factor_ref[d, :rows, :], spread(phase, g), preferred_element_type=jnp.float32)
                result = result + wide * sources[d](cols).reshape(rows, GW).astype(jnp.float32)
            data_out(cols, result.astype(jnp.bfloat16))

    def merge_second(phase):
        for by in range(1, SIDE):
            two(phase, by).wait_send()
            two(phase, by).wait_recv()
        width, count = WS[phase], 2 * SIDE
        mid_ref, next_ref, late_ref = mids[phase], nexts[phase], lates[phase]

        def source(d):
            if d:
                return lambda cols: next_ref[d - 1, :, :, :, cols].reshape(count, QT, cols.stop - cols.start)
            return lambda cols: mid_ref[0, :, :, :, cols].reshape(count, QT, cols.stop - cols.start)

        def stat_out(value):
            late_ref[:, :, :, width:] = value.reshape(SIDE, 2, QT, LANE)

        def data_out(cols, value):
            late_ref[:, :, :, cols] = value.reshape(SIDE, 2, QT, GW)

        merge(phase, count, [source(d) for d in range(SIDE)], stat_out, data_out)
        for by in range(1, SIDE):
            three(phase, by).start()

    def merge_third(phase):
        for by in range(1, SIDE):
            three(phase, by).wait_send()
            three(phase, by).wait_recv()
        late_ref, last_ref = lates[phase], lasts[phase]

        def source(d):
            return (lambda cols: last_ref[d - 1, :, :, cols]) if d else (lambda cols: late_ref[0, :, :, cols])

        def data_out(cols, value):
            rows = slice(STARTS[phase] + cols.start, STARTS[phase] + cols.stop)
            sum_ref[...] += jnp.dot(value, w_ref[rows, :], preferred_element_type=jnp.float32)

        merge(phase, 2, [source(d) for d in range(SIDE)], None, data_out)

    def run(phase, beside):
        def send(by):
            one(phase, by).start()

        beside = {at: list(acts) for at, acts in beside.items()}
        for by in range(1, SIDE):
            beside.setdefault(2 * by - 1, []).insert(0, (send, by))

        def body(b, carry):
            attend(phase, b)
            for at, acts in beside.items():

                @pl.when(b == at)
                def _():
                    for act, *args in acts:
                        act(*args)

            return carry

        lax.fori_loop(0, OWNERS // BATCH, body, 0)

    def ring_beside(phase):
        return {
            0: [(ring_end, phase, 0), (ring_start, phase, 1)],
            1: [(ring_forward, phase, 1)],
            2: [(ring_end, phase, 1), (ring_start, phase, 2)],
            4: [(ring_forward, phase, 2)],
        }

    run(0, ring_beside(1) | {6: [(ring_start, 2, 0)]})
    ring_end(1, 2)
    ring_forward(2, 0)
    run(1, ring_beside(2))
    ring_end(2, 2)
    merge_first(0)
    run(2, {})
    merge_first(1)
    merge_second(0)
    merge_first(2)
    merge_second(1)
    sum_ref[...] = jnp.zeros(sum_ref.shape, jnp.float32)
    w_home.wait()
    w_give.wait_send()
    w_take.wait_recv()
    merge_third(0)
    merge_second(2)
    merge_third(1)
    for phase in range(3):
        ring_sent(phase)
    for stage in range(3):
        for by in range(1, SIDE):
            list_copy(stage, by).wait_send()
    merge_third(2)
    out_ref[...] = sum_ref[...].astype(jnp.bfloat16)


def on_device(queries, keys, values, counts, passage_ids, out_weight):
    list_len = passage_ids.shape[1]
    listed = jnp.arange(list_len)[None, :] < counts[:, None]
    ids = jnp.where(listed, passage_ids, -1).astype(jnp.int32)
    ids = jnp.pad(ids, ((0, 0), (0, LANE // 2 - list_len)), constant_values=-1).reshape(1, LANE)
    bf16 = [pltpu.VMEM((SIDE, SIDE, SIDE, 2 * QT, width), jnp.bfloat16) for width in WS]
    for lead in (
        (SIDE, SIDE, SIDE),
        (SIDE - 1, SIDE, SIDE),
        (SIDE, SIDE, 2),
        (SIDE - 1, SIDE, 2),
        (SIDE, 2),
        (SIDE - 1, 2),
    ):
        bf16 += [pltpu.VMEM((*lead, QT, width + LANE), jnp.bfloat16) for width in WS]
    plane = SIDE * SIDE * QT
    return pl.pallas_call(
        torus_kernel,
        out_shape=jax.ShapeDtypeStruct((2 * QT, D), jnp.bfloat16),
        in_specs=[pl.BlockSpec(memory_space=pltpu.VMEM)] * 2 + [pl.BlockSpec(memory_space=pl.ANY)] * 3,
        out_specs=pl.BlockSpec(memory_space=pltpu.VMEM),
        scratch_shapes=bf16
        + [
            pltpu.VMEM(keys.shape, jnp.bfloat16),
            pltpu.VMEM(values.shape, jnp.bfloat16),
            pltpu.VMEM((D, D), jnp.bfloat16),
            pltpu.VMEM((SIDE, SIDE, SIDE, 1, LANE), jnp.int32),
            pltpu.VMEM((OWNERS, 1, LANE), jnp.int32),
            pltpu.SMEM((OWNERS, 1, LANE), jnp.int32),
            pltpu.VMEM((SIDE, plane, 2 * LANE), jnp.float32),
            pltpu.VMEM((SIDE, plane, LANE), jnp.bfloat16),
            pltpu.VMEM((SIDE, plane, GW), jnp.float32),
            pltpu.VMEM((2 * QT, D), jnp.float32),
            pltpu.SemaphoreType.DMA((2,)),
            pltpu.SemaphoreType.DMA((5,)),
            pltpu.SemaphoreType.DMA((3, SIDE)),
            pltpu.SemaphoreType.DMA((3, SIDE)),
            pltpu.SemaphoreType.DMA((2,)),
            pltpu.SemaphoreType.DMA((3, 3, 3, 4)),
            pltpu.SemaphoreType.DMA((3, 3, 3, 4)),
        ]
        + [pltpu.SemaphoreType.DMA((3, SIDE))] * 6,
        compiler_params=pltpu.CompilerParams(
            vmem_limit_bytes=60 * 2**20, collective_id=0, has_side_effects=True
        ),
        cost_estimate=pl.CostEstimate(flops=40 * 10**9, bytes_accessed=20 * 2**20, transcendentals=4 * 10**6),
        name="torus",
    )(ids, queries, keys, values, out_weight)


def solution(mesh):
    placed = (
        P(("grp", "dev"), None),
        P(("grp", "dev"), None, None),
        P(("grp", "dev"), None, None),
        P(("grp", "dev")),
        P(("grp", "dev"), None),
        P("grp", None),
    )
    return jax.shard_map(
        on_device, mesh=mesh, in_specs=placed, out_specs=P(("grp", "dev"), None), check_vma=False
    )
```

```python
import jax
import jax.numpy as jnp
from jax import lax
from jax.experimental import pallas as pl
from jax.experimental.pallas import tpu as pltpu
from jax.sharding import PartitionSpec as P

D = 2048
H = 32
HD = 64
QT = 16
PT = 64
GW = 256
GH = GW // HD
GROUPS = D // GW
LANE = 128
SIDE = 4
OWNERS = SIDE * SIDE * SIDE
PHASES = ((0, 1, 2), (3, 4, 5), (6, 7))
BATCH = 8
DEAD = -1e30
ORDERS = (("x", "y", "z"), ("y", "z", "x"), ("z", "x", "y"))
MESH = pl.DeviceIdType.MESH


def torus_kernel(
    ids_ref, mine_ref, k_hbm, v_hbm, w_hbm, out_ref,
    q_ref, part_ref, near_ref, mid_ref, next_ref, late_ref, last_ref,
    part_stat, near_stat, mid_stat, next_stat, late_stat, last_stat,
    k_ref, v_ref, w_ref, list_ref, code_ref, code_smem, spread_one, spread_two, spread_three, attended_ref, sum_ref,
    load_sem, home_sem, list_send, list_recv, w_sem, ring_send, ring_recv, tree_send, tree_recv,
):
    me = lax.axis_index("dev")
    grp = lax.axis_index("grp")
    own = {"y": me >> 4, "x": (me >> 2) & 3, "z": me & 3}
    stride = {"y": SIDE * SIDE, "x": SIDE, "z": 1}
    line = {
        axis: {by: (grp, me + ((((own[axis] + by) & 3) - own[axis]) * stride[axis])) for by in range(1, SIDE)}
        for axis in own
    }
    loads = [
        pltpu.make_async_copy(k_hbm, k_ref, load_sem.at[0]),
        pltpu.make_async_copy(v_hbm, v_ref, load_sem.at[1]),
    ]
    for load in loads:
        load.start()
    barrier = pltpu.get_barrier_semaphore()
    for axis in line:
        for by in line[axis]:
            pl.semaphore_signal(barrier, inc=1, device_id=line[axis][by], device_id_type=MESH)
    pl.semaphore_signal(barrier, inc=1, device_id=(1 - grp, me), device_id_type=MESH)
    homes = [
        pltpu.make_async_copy(mine_ref.at[:, pl.ds(g * GW, GW)], q_ref.at[g, 0, 0, 0], home_sem.at[g])
        for g in range(GROUPS)
    ]
    for home in homes:
        home.start()
    list_ref[0, 0, 0] = ids_ref[...]
    pl.semaphore_wait(barrier, 10)

    whole, lower, upper = (0, 2 * QT), (0, QT), (QT, QT)
    both = ((0, 1, 3, lower), (1, 3, 1, upper))

    def order_of(g):
        return ORDERS[g % 3]

    def ring_block(g, stage, at, rows):
        spot = [pl.ds(0, SIDE) if n < stage else at if n == stage else 0 for n in range(3)]
        return q_ref.at[g, spot[0], spot[1], spot[2], pl.ds(*rows), :]

    def ring_own(g, stage, kind, by, at):
        source = ring_block(g, stage, 0, whole) if stage else mine_ref.at[:, pl.ds(g * GW, GW)]
        return pltpu.make_async_remote_copy(
            src_ref=source,
            dst_ref=ring_block(g, stage, at, whole),
            send_sem=ring_send.at[g, stage, kind],
            recv_sem=ring_recv.at[g, stage, kind],
            device_id=line[order_of(g)[stage]][by],
            device_id_type=MESH,
        )

    def ring_pass(g, stage, kind, by, at, rows):
        return pltpu.make_async_remote_copy(
            src_ref=ring_block(g, stage, at, rows),
            dst_ref=ring_block(g, stage, 2, rows),
            send_sem=ring_send.at[g, stage, 2 + kind],
            recv_sem=ring_recv.at[g, stage, 2 + kind],
            device_id=line[order_of(g)[stage]][by],
            device_id_type=MESH,
        )

    def ring_start(phase, stage):
        for g in PHASES[phase]:
            for kind, by, at, rows in both:
                ring_own(g, stage, kind, by, at).start()

    def ring_forward(phase, stage):
        for kind, by, at, rows in both:
            for g in PHASES[phase]:
                ring_own(g, stage, kind, by, at).wait_recv()
                ring_pass(g, stage, kind, by, at, rows).start()

    def ring_end(phase, stage):
        for g in PHASES[phase]:
            for kind, by, at, rows in both:
                ring_pass(g, stage, kind, by, at, rows).wait_recv()

    def ring_sent():
        for g in range(GROUPS):
            for stage in range(3):
                for kind, by, at, rows in both:
                    ring_own(g, stage, kind, by, at).wait_send()
                    ring_pass(g, stage, kind, by, at, rows).wait_send()

    def list_copy(stage, by):
        order = ("x", "y", "z")
        spot = {axis: 0 for axis in order}
        for axis in order[:stage]:
            spot[axis] = pl.ds(0, SIDE)
        source = list_ref.at[spot["y"], spot["x"], spot["z"]]
        spot[order[stage]] = SIDE - by
        return pltpu.make_async_remote_copy(
            src_ref=source,
            dst_ref=list_ref.at[spot["y"], spot["x"], spot["z"]],
            send_sem=list_send.at[stage, by],
            recv_sem=list_recv.at[stage, by],
            device_id=line[order[stage]][by],
            device_id_type=MESH,
        )

    def list_start(stage):
        for by in range(1, SIDE):
            list_copy(stage, by).start()

    def list_end(stage):
        for by in range(1, SIDE):
            list_copy(stage, by).wait_recv()

    w_rows = D // 2
    w_home = pltpu.make_async_copy(w_hbm, w_ref.at[pl.ds(grp * w_rows, w_rows)], load_sem.at[2])
    w_give = pltpu.make_async_remote_copy(
        src_ref=w_hbm,
        dst_ref=w_ref.at[pl.ds(grp * w_rows, w_rows)],
        send_sem=w_sem.at[0],
        recv_sem=w_sem.at[1],
        device_id=(1 - grp, me),
        device_id_type=MESH,
    )
    w_take = pltpu.make_async_remote_copy(
        src_ref=w_hbm,
        dst_ref=w_ref.at[pl.ds((1 - grp) * w_rows, w_rows)],
        send_sem=w_sem.at[0],
        recv_sem=w_sem.at[1],
        device_id=(1 - grp, me),
        device_id_type=MESH,
    )

    list_start(0)
    ring_start(0, 0)
    part_stat[...] = jnp.zeros(part_stat.shape, jnp.float32)
    spread_row = lax.broadcasted_iota(jnp.int32, (LANE, GW), 0)
    spread_head = lax.broadcasted_iota(jnp.int32, (LANE, GW), 1) >> 6
    in_half = spread_row & 63

    def as_matrix(chosen):
        return chosen.astype(jnp.float32).astype(jnp.bfloat16)

    for n in range(SIDE * SIDE):
        spread_one[n] = as_matrix(in_half == n * GH + spread_head)
    for n in range(2 * SIDE):
        chosen = (in_half < 32) & ((in_half & 15) == (n >> 1) * GH + spread_head)
        spread_two[n] = as_matrix(chosen & ((spread_row >> 6) == (n & 1)))
    for n in range(2):
        chosen = (in_half < 8) & ((in_half & 3) == spread_head)
        spread_three[n] = as_matrix(chosen & ((spread_row >> 6) == n))
    for home in homes:
        home.wait()
    list_end(0)
    list_start(1)
    ring_forward(0, 0)
    list_end(1)
    list_start(2)
    ring_end(0, 0)
    ring_start(0, 1)
    ring_forward(0, 1)
    ring_end(0, 1)
    ring_start(0, 2)
    list_end(2)
    ids = list_ref[...].reshape(OWNERS, LANE)
    key = lax.broadcasted_iota(jnp.int32, (OWNERS, LANE), 1) * 16 + (ids & 15)
    here = (ids >> 4) == me
    first = jnp.min(jnp.where(here, key, 1 << 20), axis=1, keepdims=True)
    last = jnp.max(jnp.where(here, key, -1), axis=1, keepdims=True)
    code = jnp.where(last < 0, -1, (first >> 10) + ((first & 15) << 1) + ((last & 15) << 5))
    code_ref[...] = jnp.broadcast_to(code, (OWNERS, LANE)).reshape(OWNERS, 1, LANE)
    code_move = pltpu.make_async_copy(code_ref, code_smem, load_sem.at[3])
    code_move.start()
    ring_forward(0, 2)
    ring_start(1, 0)
    w_home.start()
    w_give.start()
    for load in loads:
        load.wait()
    code_move.wait()
    ring_end(0, 2)
    ring_forward(1, 0)

    row_head = lax.broadcasted_iota(jnp.int32, (GH * QT, GW), 0) // QT
    lane_head = lax.broadcasted_iota(jnp.int32, (GH * QT, GW), 1) // HD
    diag = (row_head == lane_head).astype(jnp.float32).astype(jnp.bfloat16)
    stat_lane = lax.broadcasted_iota(jnp.int32, (QT, LANE), 1)
    near = stat_lane < HD

    def tree(sources, targets, g, stage, by):
        return [
            pltpu.make_async_remote_copy(
                src_ref=source,
                dst_ref=target,
                send_sem=tree_send.at[stage, g, by, n],
                recv_sem=tree_recv.at[stage, g, by, n],
                device_id=line[order_of(g)[stage]][by],
                device_id_type=MESH,
            )
            for n, (source, target) in enumerate(zip(sources, targets))
        ]

    def one(g, by):
        return tree(
            (part_ref.at[g, by], part_stat.at[g, by]), (near_ref.at[g, by - 1], near_stat.at[g, by - 1]), g, 0, by
        )

    def two(g, by):
        return tree((mid_ref.at[g, by], mid_stat.at[g]), (next_ref.at[g, by - 1], next_stat.at[g, by - 1]), g, 1, by)

    def three(g, by):
        return tree((late_ref.at[g, by], late_stat.at[g]), (last_ref.at[g, by - 1], last_stat.at[g, by - 1]), g, 2, by)

    def tree_start(stage, g):
        for by in range(1, SIDE):
            for copy in stage(g, by):
                copy.start()

    def tree_wait(stage, g):
        for by in range(1, SIDE):
            for copy in stage(g, by):
                copy.wait_send()
                copy.wait_recv()

    stride = {"y": SIDE * SIDE, "x": SIDE, "z": 1}

    def attend(phase, b):
        delta, part_half = ((b >> 1) + 1) & 3, b & 1
        items = [(n, g) for n in range(BATCH) for g in PHASES[phase]]
        slots, tags, scores, weights = {}, {}, {}, {}
        lane = stat_lane - part_half * (BATCH * GH)
        stats = {g: part_stat[g, delta] for g in PHASES[phase]}

        def place(n):
            return delta, part_half * 2 + n // SIDE, n % SIDE

        for n, g in items:
            told = code_smem[sum(at * stride[axis] for axis, at in zip(order_of(g), place(n))), 0, 0]
            code = jnp.maximum(told, 0)
            slots[n, g] = (code & 1, (code >> 1) & 15, (code >> 5) & 15)
            tags[n, g] = jnp.where(told < 0, -1.0, jnp.where((code & 1) > 0, 1.0, 0.0))

        def score(n, g):
            which, first, second = slots[n, g]
            cols = slice(g * GW, (g + 1) * GW)
            q = jnp.where(which > 0, q_ref[(g, *place(n), slice(QT, 2 * QT))], q_ref[(g, *place(n), slice(0, QT))])
            lhs = jnp.concatenate([q * jnp.bfloat16(0.125)] * GH, axis=0) * diag
            k = jnp.concatenate([k_ref[first, :, cols], k_ref[second, :, cols]], axis=0)
            scores[n, g] = lax.dot_general(lhs, k, (((1,), (1,)), ((), ())), preferred_element_type=jnp.float32)

        def weigh(n, g):
            which, first, second = slots[n, g]
            values = scores.pop((n, g))
            peak = jnp.max(values, axis=1, keepdims=True)
            shaped = jnp.exp(values - peak)
            total = jnp.sum(shaped, axis=1, keepdims=True)
            lse = peak + jnp.log(total * jnp.where(first == second, 0.5, 1.0))
            for h in range(GH):
                stats[g] = jnp.where(lane == n * GH + h, lse[h * QT : (h + 1) * QT], stats[g])
            stats[g] = jnp.where(((lane - LANE // 2) >> 2) == n, tags[n, g], stats[g])
            weights[n, g] = (shaped.astype(jnp.bfloat16), 1.0 / total)

        def apply(n, g):
            which, first, second = slots[n, g]
            cols = slice(g * GW, (g + 1) * GW)
            shaped, inverse = weights.pop((n, g))
            v = jnp.concatenate([v_ref[first, :, cols], v_ref[second, :, cols]], axis=0)
            full = jnp.dot(shaped, v, preferred_element_type=jnp.float32)
            for t in range(GW // LANE):
                lanes = slice(t * LANE, (t + 1) * LANE)
                a, c = (slice((2 * t + e) * QT, (2 * t + e + 1) * QT) for e in (0, 1))
                part = jnp.where(near, full[a, lanes] * inverse[a], full[c, lanes] * inverse[c])
                part_ref[(g, *place(n), slice(None), lanes)] = part.astype(jnp.bfloat16)

        for at in range(len(items) + 4):
            if at < len(items):
                score(*items[at])
            if 2 <= at < len(items) + 2:
                weigh(*items[at - 2])
            if 4 <= at:
                apply(*items[at - 4])
        for g in PHASES[phase]:
            part_stat[g, delta] = stats[g]

    def rounded(value):
        return value.astype(jnp.bfloat16).astype(jnp.float32)

    def blend(factors, matrix, blocks):
        wide = jnp.dot(factors, matrix, preferred_element_type=jnp.float32)
        sums = []
        for at in range(0, factors.shape[0] // QT, SIDE):
            total = blocks[0] * wide[at * QT : (at + 1) * QT]
            for d in range(1, SIDE):
                total = total + blocks[d] * wide[(at + d) * QT : (at + d + 1) * QT]
            sums.append(total)
        return sums

    def merge_one(g):
        tree_wait(one, g)
        packed = [part_stat[g, 0]] + [near_stat[g, d - 1] for d in range(1, SIDE)]
        tags = [pltpu.roll(stat, LANE // 2, 1) for stat in packed]
        tops = []
        for n in range(2):
            kept = [jnp.where(tag == n, stat, DEAD) for stat, tag in zip(packed, tags)]
            tops.append(jnp.maximum(jnp.maximum(kept[0], kept[1]), jnp.maximum(kept[2], kept[3])))
        terms = [
            jnp.exp(jnp.minimum(stat - jnp.where(tag == 1.0, tops[1], tops[0]), 0.0)) for stat, tag in zip(packed, tags)
        ]
        factors, results = [], []
        for n in range(2):
            kept = [jnp.where(tag == n, term, 0.0) for term, tag in zip(terms, tags)]
            total = jnp.maximum(kept[0] + kept[1] + kept[2] + kept[3], 1e-30)
            results.append(tops[n] + jnp.log(total))
            for term in kept:
                share = term / total
                high = rounded(share)
                factors.append(jnp.where(stat_lane < LANE // 2, high, pltpu.roll(share - high, LANE // 2, 1)))
        mid_stat[g] = jnp.where(stat_lane < LANE // 2, results[0], pltpu.roll(results[1], LANE // 2, 1))
        factors = jnp.concatenate(factors, axis=0).astype(jnp.bfloat16)

        def body(j, carry):
            second, third = j >> 2, j & 3
            blocks = [part_ref[g, 0, second, third]] + [near_ref[g, d - 1, second, third] for d in range(1, SIDE)]
            sums = blend(factors, spread_one[j], [block.astype(jnp.float32) for block in blocks])
            for n in range(2):
                mid_ref[g, second, third, n] = sums[n].astype(jnp.bfloat16)
            return carry

        lax.fori_loop(0, SIDE * SIDE, body, 0, unroll=4)
        tree_start(two, g)

    def shares_of(packed, span):
        top = jnp.maximum(jnp.maximum(packed[0], packed[1]), jnp.maximum(packed[2], packed[3]))
        terms = [jnp.exp(stat - top) for stat in packed]
        total = terms[0] + terms[1] + terms[2] + terms[3]
        factors = []
        for term in terms:
            share = term / total
            high = rounded(share)
            low = pltpu.roll(share - high, span, 1)
            in_lane = stat_lane & 63
            factors.append(jnp.where(in_lane < span, high, jnp.where(in_lane < 2 * span, low, 0.0)))
        return top + jnp.log(total), jnp.concatenate(factors, axis=0).astype(jnp.bfloat16)

    def merge_two(g):
        tree_wait(two, g)
        packed = [mid_stat[g]] + [pltpu.roll(next_stat[g, d - 1], LANE - 16 * d, 1) for d in range(1, SIDE)]
        late_stat[g], factors = shares_of(packed, 16)
        for third in range(SIDE):
            for n in range(2):
                blocks = [mid_ref[g, 0, third, n]] + [next_ref[g, d - 1, third, n] for d in range(1, SIDE)]
                sums = blend(factors, spread_two[third * 2 + n], [block.astype(jnp.float32) for block in blocks])
                late_ref[g, third, n] = sums[0].astype(jnp.bfloat16)
        tree_start(three, g)

    def merge_three(g):
        tree_wait(three, g)
        packed = [late_stat[g]] + [pltpu.roll(last_stat[g, d - 1], LANE - 4 * d, 1) for d in range(1, SIDE)]
        value, factors = shares_of(packed, 4)
        for n in range(2):
            blocks = [late_ref[g, 0, n]] + [last_ref[g, d - 1, n] for d in range(1, SIDE)]
            sums = blend(factors, spread_three[n], [block.astype(jnp.float32) for block in blocks])
            attended_ref[n * QT : (n + 1) * QT, g * GW : (g + 1) * GW] = sums[0].astype(jnp.bfloat16)

    def project(phase):
        rows = slice(PHASES[phase][0] * GW, (PHASES[phase][-1] + 1) * GW)
        product = jnp.dot(attended_ref[:, rows], w_ref[rows, :], preferred_element_type=jnp.float32)
        if phase == 0:
            sum_ref[...] = product
        elif phase == 1:
            sum_ref[...] += product
        else:
            out_ref[...] = (sum_ref[...] + product).astype(jnp.bfloat16)

    def run(phase, beside):
        def send(by):
            for g in PHASES[phase]:
                for copy in one(g, by):
                    copy.start()

        beside = {at: list(acts) for at, acts in beside.items()}
        for by in range(1, SIDE):
            beside.setdefault(2 * by - 1, []).insert(0, (send, by))

        def body(b, carry):
            attend(phase, b)
            for at, acts in beside.items():

                @pl.when(b == at)
                def _():
                    for act, *args in acts:
                        act(*args)

            return carry

        lax.fori_loop(0, OWNERS // BATCH, body, 0)

    def ring_beside(phase):
        return {
            0: [(ring_end, phase, 0), (ring_start, phase, 1)],
            1: [(ring_forward, phase, 1)],
            2: [(ring_end, phase, 1), (ring_start, phase, 2)],
            4: [(ring_forward, phase, 2)],
        }

    def each(merge, phase):
        for g in PHASES[phase]:
            merge(g)

    run(0, ring_beside(1) | {6: [(ring_start, 2, 0)]})
    ring_end(1, 2)
    ring_forward(2, 0)
    run(1, ring_beside(2))
    ring_end(2, 2)
    each(merge_one, 0)
    run(2, {})
    each(merge_one, 1)
    each(merge_two, 0)
    each(merge_one, 2)
    each(merge_two, 1)
    each(merge_three, 0)
    w_home.wait()
    w_give.wait_send()
    w_take.wait_recv()
    project(0)
    each(merge_two, 2)
    each(merge_three, 1)
    project(1)
    ring_sent()
    for stage in range(3):
        for by in range(1, SIDE):
            list_copy(stage, by).wait_send()
    each(merge_three, 2)
    project(2)


def on_device(queries, keys, values, counts, passage_ids, out_weight):
    list_len = passage_ids.shape[1]
    listed = jnp.arange(list_len)[None, :] < counts[:, None]
    ids = jnp.where(listed, passage_ids, -1).astype(jnp.int32)
    ids = jnp.pad(ids, ((0, 0), (0, LANE // 2 - list_len)), constant_values=-1).reshape(1, LANE)
    leads = (
        (SIDE, SIDE, SIDE),
        (SIDE - 1, SIDE, SIDE),
        (SIDE, SIDE, 2),
        (SIDE - 1, SIDE, 2),
        (SIDE, 2),
        (SIDE - 1, 2),
    )
    blocks = [pltpu.VMEM((GROUPS, SIDE, SIDE, SIDE, 2 * QT, GW), jnp.bfloat16)]
    blocks += [pltpu.VMEM((GROUPS, *lead, QT, GW), jnp.bfloat16) for lead in leads]
    for lead in ((SIDE,), (SIDE - 1,), (), (SIDE - 1,), (), (SIDE - 1,)):
        blocks.append(pltpu.VMEM((GROUPS, *lead, QT, LANE), jnp.float32))
    return pl.pallas_call(
        torus_kernel,
        out_shape=jax.ShapeDtypeStruct((2 * QT, D), jnp.bfloat16),
        in_specs=[pl.BlockSpec(memory_space=pltpu.VMEM)] * 2 + [pl.BlockSpec(memory_space=pl.ANY)] * 3,
        out_specs=pl.BlockSpec(memory_space=pltpu.VMEM),
        scratch_shapes=blocks
        + [
            pltpu.VMEM(keys.shape, jnp.bfloat16),
            pltpu.VMEM(values.shape, jnp.bfloat16),
            pltpu.VMEM((D, D), jnp.bfloat16),
            pltpu.VMEM((SIDE, SIDE, SIDE, 1, LANE), jnp.int32),
            pltpu.VMEM((OWNERS, 1, LANE), jnp.int32),
            pltpu.SMEM((OWNERS, 1, LANE), jnp.int32),
            pltpu.VMEM((SIDE * SIDE, LANE, GW), jnp.bfloat16),
            pltpu.VMEM((2 * SIDE, LANE, GW), jnp.bfloat16),
            pltpu.VMEM((2, LANE, GW), jnp.bfloat16),
            pltpu.VMEM((2 * QT, D), jnp.bfloat16),
            pltpu.VMEM((2 * QT, D), jnp.float32),
            pltpu.SemaphoreType.DMA((4,)),
            pltpu.SemaphoreType.DMA((GROUPS,)),
            pltpu.SemaphoreType.DMA((3, SIDE)),
            pltpu.SemaphoreType.DMA((3, SIDE)),
            pltpu.SemaphoreType.DMA((2,)),
            pltpu.SemaphoreType.DMA((GROUPS, 3, 4)),
            pltpu.SemaphoreType.DMA((GROUPS, 3, 4)),
            pltpu.SemaphoreType.DMA((3, GROUPS, SIDE, 2)),
            pltpu.SemaphoreType.DMA((3, GROUPS, SIDE, 2)),
        ],
        compiler_params=pltpu.CompilerParams(
            vmem_limit_bytes=60 * 2**20, collective_id=0, has_side_effects=True
        ),
        cost_estimate=pl.CostEstimate(flops=40 * 10**9, bytes_accessed=20 * 2**20, transcendentals=4 * 10**6),
        name="torus",
    )(ids, queries, keys, values, out_weight)


def solution(mesh):
    placed = (
        P(("grp", "dev"), None),
        P(("grp", "dev"), None, None),
        P(("grp", "dev"), None, None),
        P(("grp", "dev")),
        P(("grp", "dev"), None),
        P("grp", None),
    )
    return jax.shard_map(
        on_device, mesh=mesh, in_specs=placed, out_specs=P(("grp", "dev"), None), check_vma=False
    )
```

```python
import jax
import jax.numpy as jnp
from jax import lax
from jax.experimental import pallas as pl
from jax.experimental.pallas import tpu as pltpu
from jax.sharding import PartitionSpec as P

D = 2048
H = 32
HD = 64
QT = 16
PT = 64
GW = 256
GH = GW // HD
GROUPS = D // GW
LANE = 128
SIDE = 4
OWNERS = SIDE * SIDE * SIDE
PHASES = ((0, 1, 2), (3, 4, 5), (6, 7))
BATCH = 8
DEAD = -1e30
ORDERS = (("x", "y", "z"), ("y", "z", "x"), ("z", "x", "y"))
MESH = pl.DeviceIdType.MESH


def torus_kernel(
    counts_ref, ids_ref, mine_ref, k_hbm, v_hbm, w_hbm, out_ref,
    q_ref, part_ref, near_ref, mid_ref, next_ref, late_ref, last_ref,
    part_stat, near_stat, mid_stat, next_stat, late_stat, last_stat,
    k_ref, v_ref, w_ref, list_ref, code_ref, code_smem, attended_ref, sum_ref,
    load_sem, home_sem, list_send, list_recv, w_sem, ring_send, ring_recv, tree_send, tree_recv,
):
    me = lax.axis_index("dev")
    grp = lax.axis_index("grp")
    own = {"y": me >> 4, "x": (me >> 2) & 3, "z": me & 3}
    stride = {"y": SIDE * SIDE, "x": SIDE, "z": 1}
    line = {
        axis: {by: (grp, me + ((((own[axis] + by) & 3) - own[axis]) * stride[axis])) for by in range(1, SIDE)}
        for axis in own
    }
    loads = [
        pltpu.make_async_copy(k_hbm, k_ref, load_sem.at[0]),
        pltpu.make_async_copy(v_hbm, v_ref, load_sem.at[1]),
    ]
    for load in loads:
        load.start()
    barrier = pltpu.get_barrier_semaphore()
    for axis in line:
        for by in line[axis]:
            pl.semaphore_signal(barrier, inc=1, device_id=line[axis][by], device_id_type=MESH)
    pl.semaphore_signal(barrier, inc=1, device_id=(1 - grp, me), device_id_type=MESH)
    homes = [
        pltpu.make_async_copy(mine_ref.at[:, pl.ds(g * GW, GW)], q_ref.at[g, 0, 0, 0], home_sem.at[g])
        for g in range(GROUPS)
    ]
    for home in homes:
        home.start()
    list_len = ids_ref.shape[1]
    place = lax.broadcasted_iota(jnp.int32, (2, list_len), 1)
    row = lax.broadcasted_iota(jnp.int32, (2, list_len), 0)
    live = place < jnp.where(row == 0, counts_ref[0], counts_ref[1])
    list_ref[0, 0, 0] = jnp.full((2, LANE), -1, jnp.int32)
    list_ref[0, 0, 0, :, :list_len] = jnp.where(live, ids_ref[...], -1)
    pl.semaphore_wait(barrier, 10)

    whole, lower, upper = (0, 2 * QT), (0, QT), (QT, QT)
    both = ((0, 1, 3, lower), (1, 3, 1, upper))
    straight = both + ((2, 2, 2, whole),)

    def sends(stage):
        return both if stage == 2 else straight

    def order_of(g):
        return ORDERS[g % 3]

    def ring_block(g, stage, at, rows):
        spot = [pl.ds(0, SIDE) if n < stage else at if n == stage else 0 for n in range(3)]
        return q_ref.at[g, spot[0], spot[1], spot[2], pl.ds(*rows), :]

    def ring_own(g, stage, kind, by, at):
        source = ring_block(g, stage, 0, whole) if stage else mine_ref.at[:, pl.ds(g * GW, GW)]
        return pltpu.make_async_remote_copy(
            src_ref=source,
            dst_ref=ring_block(g, stage, at, whole),
            send_sem=ring_send.at[g, stage, kind],
            recv_sem=ring_recv.at[g, stage, kind],
            device_id=line[order_of(g)[stage]][by],
            device_id_type=MESH,
        )

    def ring_pass(g, stage, kind, by, at, rows):
        return pltpu.make_async_remote_copy(
            src_ref=ring_block(g, stage, at, rows),
            dst_ref=ring_block(g, stage, 2, rows),
            send_sem=ring_send.at[g, stage, 2 + kind],
            recv_sem=ring_recv.at[g, stage, 2 + kind],
            device_id=line[order_of(g)[stage]][by],
            device_id_type=MESH,
        )

    def ring_start(phase, stage):
        for g in PHASES[phase]:
            for kind, by, at, rows in sends(stage):
                ring_own(g, stage, kind, by, at).start()

    def ring_forward(phase, stage):
        for kind, by, at, rows in both:
            for g in PHASES[phase]:
                ring_own(g, stage, kind, by, at).wait_recv()
                ring_pass(g, stage, kind, by, at, rows).start()

    def ring_end(phase, stage):
        for g in PHASES[phase]:
            for kind, by, at, rows in sends(stage):
                if stage == 2:
                    ring_pass(g, stage, kind, by, at, rows).wait_recv()
                else:
                    ring_own(g, stage, kind, by, at).wait_recv()

    def ring_sent():
        for g in range(GROUPS):
            for stage in range(3):
                for kind, by, at, rows in sends(stage):
                    ring_own(g, stage, kind, by, at).wait_send()
                    if stage == 2:
                        ring_pass(g, stage, kind, by, at, rows).wait_send()

    def list_copy(stage, by):
        order = ("x", "y", "z")
        spot = {axis: 0 for axis in order}
        for axis in order[:stage]:
            spot[axis] = pl.ds(0, SIDE)
        source = list_ref.at[spot["y"], spot["x"], spot["z"]]
        spot[order[stage]] = SIDE - by
        return pltpu.make_async_remote_copy(
            src_ref=source,
            dst_ref=list_ref.at[spot["y"], spot["x"], spot["z"]],
            send_sem=list_send.at[stage, by],
            recv_sem=list_recv.at[stage, by],
            device_id=line[order[stage]][by],
            device_id_type=MESH,
        )

    def list_start(stage):
        for by in range(1, SIDE):
            list_copy(stage, by).start()

    def list_end(stage):
        for by in range(1, SIDE):
            list_copy(stage, by).wait_recv()

    w_rows = D // 2
    w_home = pltpu.make_async_copy(w_hbm, w_ref.at[pl.ds(grp * w_rows, w_rows)], load_sem.at[2])
    w_give = pltpu.make_async_remote_copy(
        src_ref=w_hbm,
        dst_ref=w_ref.at[pl.ds(grp * w_rows, w_rows)],
        send_sem=w_sem.at[0],
        recv_sem=w_sem.at[1],
        device_id=(1 - grp, me),
        device_id_type=MESH,
    )
    w_take = pltpu.make_async_remote_copy(
        src_ref=w_hbm,
        dst_ref=w_ref.at[pl.ds((1 - grp) * w_rows, w_rows)],
        send_sem=w_sem.at[0],
        recv_sem=w_sem.at[1],
        device_id=(1 - grp, me),
        device_id_type=MESH,
    )

    list_start(0)
    ring_start(0, 0)
    part_stat[...] = jnp.zeros(part_stat.shape, jnp.float32)
    for home in homes:
        home.wait()
    list_end(0)
    list_start(1)
    ring_end(0, 0)
    ring_start(0, 1)
    list_end(1)
    list_start(2)
    ring_end(0, 1)
    ring_start(0, 2)
    list_end(2)
    firsts, lasts = [], []
    for n in range(2):
        ids = list_ref[:, :, :, n, :].reshape(OWNERS, LANE)
        key = n * 1024 + lax.broadcasted_iota(jnp.int32, (OWNERS, LANE), 1) * 16 + (ids & 15)
        here = (ids >> 4) == me
        firsts.append(jnp.min(jnp.where(here, key, 1 << 20), axis=1, keepdims=True))
        lasts.append(jnp.max(jnp.where(here, key, -1), axis=1, keepdims=True))
    first, last = jnp.minimum(*firsts), jnp.maximum(*lasts)
    code = jnp.where(last < 0, -1, (first >> 10) + ((first & 15) << 1) + ((last & 15) << 5))
    code_ref[...] = jnp.broadcast_to(code, (OWNERS, LANE)).reshape(OWNERS, 1, LANE)
    code_move = pltpu.make_async_copy(code_ref, code_smem, load_sem.at[3])
    code_move.start()
    ring_forward(0, 2)
    ring_start(1, 0)
    w_home.start()
    w_give.start()
    for load in loads:
        load.wait()
    code_move.wait()
    ring_end(0, 2)
    ring_end(1, 0)
    ring_start(1, 1)

    row_head = lax.broadcasted_iota(jnp.int32, (GH * QT, GW), 0) // QT
    lane_head = lax.broadcasted_iota(jnp.int32, (GH * QT, GW), 1) // HD
    diag = (row_head == lane_head).astype(jnp.float32).astype(jnp.bfloat16)
    stat_lane = lax.broadcasted_iota(jnp.int32, (QT, LANE), 1)
    near = stat_lane < HD

    def tree(sources, targets, g, stage, by):
        return [
            pltpu.make_async_remote_copy(
                src_ref=source,
                dst_ref=target,
                send_sem=tree_send.at[stage, g, by, n],
                recv_sem=tree_recv.at[stage, g, by, n],
                device_id=line[order_of(g)[stage]][by],
                device_id_type=MESH,
            )
            for n, (source, target) in enumerate(zip(sources, targets))
        ]

    def one(g, by):
        return tree(
            (part_ref.at[g, by], part_stat.at[g, by]), (near_ref.at[g, by - 1], near_stat.at[g, by - 1]), g, 0, by
        )

    def two(g, by):
        return tree((mid_ref.at[g, by], mid_stat.at[g]), (next_ref.at[g, by - 1], next_stat.at[g, by - 1]), g, 1, by)

    def three(g, by):
        return tree((late_ref.at[g, by], late_stat.at[g]), (last_ref.at[g, by - 1], last_stat.at[g, by - 1]), g, 2, by)

    def tree_start(stage, g):
        for by in range(1, SIDE):
            for copy in stage(g, by):
                copy.start()

    def tree_wait(stage, g):
        for by in range(1, SIDE):
            for copy in stage(g, by):
                copy.wait_send()
                copy.wait_recv()

    stride = {"y": SIDE * SIDE, "x": SIDE, "z": 1}

    def attend(phase, b):
        delta, part_half = ((b >> 1) + 1) & 3, b & 1
        items = [(n, g) for n in range(BATCH) for g in PHASES[phase]]
        slots, tags, scores, weights = {}, {}, {}, {}
        lane = stat_lane - part_half * (BATCH * GH)
        stats = {g: part_stat[g, delta] for g in PHASES[phase]}

        def place(n):
            return delta, part_half * 2 + n // SIDE, n % SIDE

        for n, g in items:
            told = code_smem[sum(at * stride[axis] for axis, at in zip(order_of(g), place(n))), 0, 0]
            code = jnp.maximum(told, 0)
            slots[n, g] = (code & 1, (code >> 1) & 15, (code >> 5) & 15)
            tags[n, g] = jnp.where(told < 0, -1.0, jnp.where((code & 1) > 0, 1.0, 0.0))

        def score(n, g):
            which, first, second = slots[n, g]
            cols = slice(g * GW, (g + 1) * GW)
            q = jnp.where(which > 0, q_ref[(g, *place(n), slice(QT, 2 * QT))], q_ref[(g, *place(n), slice(0, QT))])
            lhs = jnp.concatenate([q * jnp.bfloat16(0.125)] * GH, axis=0) * diag
            k = jnp.concatenate([k_ref[first, :, cols], k_ref[second, :, cols]], axis=0)
            scores[n, g] = lax.dot_general(lhs, k, (((1,), (1,)), ((), ())), preferred_element_type=jnp.float32)

        def weigh(n, g):
            which, first, second = slots[n, g]
            values = scores.pop((n, g))
            peak = jnp.max(values, axis=1, keepdims=True)
            shaped = jnp.exp(values - peak)
            total = jnp.sum(shaped, axis=1, keepdims=True)
            lse = peak + jnp.log(total * jnp.where(first == second, 0.5, 1.0))
            for h in range(GH):
                stats[g] = jnp.where(lane == n * GH + h, lse[h * QT : (h + 1) * QT], stats[g])
            stats[g] = jnp.where(((lane - LANE // 2) >> 2) == n, tags[n, g], stats[g])
            weights[n, g] = (shaped.astype(jnp.bfloat16), 1.0 / total)

        def apply(n, g):
            which, first, second = slots[n, g]
            cols = slice(g * GW, (g + 1) * GW)
            shaped, inverse = weights.pop((n, g))
            v = jnp.concatenate([v_ref[first, :, cols], v_ref[second, :, cols]], axis=0)
            full = jnp.dot(shaped, v, preferred_element_type=jnp.float32)
            for t in range(GW // LANE):
                lanes = slice(t * LANE, (t + 1) * LANE)
                a, c = (slice((2 * t + e) * QT, (2 * t + e + 1) * QT) for e in (0, 1))
                part = jnp.where(near, full[a, lanes] * inverse[a], full[c, lanes] * inverse[c])
                part_ref[(g, *place(n), slice(None), lanes)] = part.astype(jnp.bfloat16)

        for at in range(len(items) + 4):
            if at < len(items):
                score(*items[at])
            if 2 <= at < len(items) + 2:
                weigh(*items[at - 2])
            if 4 <= at:
                apply(*items[at - 4])
        for g in PHASES[phase]:
            part_stat[g, delta] = stats[g]

    def widen(share, at, t):
        pair = [jnp.broadcast_to(share[:, c : c + 1], (QT, LANE)) for c in (at + 2 * t, at + 2 * t + 1)]
        return jnp.where(near, pair[0], pair[1])

    def tiles(block):
        return [block[:, t * LANE : (t + 1) * LANE].astype(jnp.float32) for t in range(GW // LANE)]

    def blend(shares, at, blocks):
        sums = []
        for t in range(GW // LANE):
            total = widen(shares[0], at, t) * tiles(blocks[0])[t]
            for d in range(1, SIDE):
                total = total + widen(shares[d], at, t) * tiles(blocks[d])[t]
            sums.append(total)
        return jnp.concatenate(sums, axis=1).astype(jnp.bfloat16)

    def merge_one(g):
        tree_wait(one, g)
        packed = [part_stat[g, 0]] + [near_stat[g, d - 1] for d in range(1, SIDE)]
        tags = [pltpu.roll(stat, LANE // 2, 1) for stat in packed]
        tops = []
        for n in range(2):
            kept = [jnp.where(tag == n, stat, DEAD) for stat, tag in zip(packed, tags)]
            tops.append(jnp.maximum(jnp.maximum(kept[0], kept[1]), jnp.maximum(kept[2], kept[3])))
        terms = [
            jnp.exp(jnp.minimum(stat - jnp.where(tag == 1.0, tops[1], tops[0]), 0.0)) for stat, tag in zip(packed, tags)
        ]
        results, inverses = [], []
        for n in range(2):
            kept = [jnp.where(tag == n, term, 0.0) for term, tag in zip(terms, tags)]
            total = jnp.maximum(kept[0] + kept[1] + kept[2] + kept[3], 1e-30)
            results.append(tops[n] + jnp.log(total))
            inverses.append(1.0 / total)
        mid_stat[g] = jnp.where(stat_lane < LANE // 2, results[0], pltpu.roll(results[1], LANE // 2, 1))
        shares = [
            term * jnp.where(tag == 1.0, -inverses[1], jnp.where(tag == 0.0, inverses[0], 0.0))
            for term, tag in zip(terms, tags)
        ]

        def body(j, carry):
            second, third = j >> 2, j & 3
            blocks = [part_ref[g, 0, second, third]] + [near_ref[g, d - 1, second, third] for d in range(1, SIDE)]
            turned = [pltpu.roll(share, (LANE - GH * j) & (LANE - 1), 1) for share in shares]
            for t in range(GW // LANE):
                totals = [jnp.zeros((QT, LANE), jnp.float32)] * 2
                for d in range(SIDE):
                    factor, block = widen(turned[d], 0, t), tiles(blocks[d])[t]
                    totals = [
                        totals[0] + jnp.maximum(factor, 0.0) * block,
                        totals[1] - jnp.minimum(factor, 0.0) * block,
                    ]
                for n in range(2):
                    mid_ref[g, second, third, n, :, t * LANE : (t + 1) * LANE] = totals[n].astype(jnp.bfloat16)
            return carry

        lax.fori_loop(0, SIDE * SIDE, body, 0, unroll=4)
        tree_start(two, g)

    def shares_of(packed):
        top = jnp.maximum(jnp.maximum(packed[0], packed[1]), jnp.maximum(packed[2], packed[3]))
        terms = [jnp.exp(stat - top) for stat in packed]
        total = terms[0] + terms[1] + terms[2] + terms[3]
        inverse = 1.0 / total
        return top + jnp.log(total), [term * inverse for term in terms]

    def merge_two(g):
        tree_wait(two, g)
        packed = [mid_stat[g]] + [pltpu.roll(next_stat[g, d - 1], LANE - 16 * d, 1) for d in range(1, SIDE)]
        late_stat[g], shares = shares_of(packed)
        for third in range(SIDE):
            for n in range(2):
                blocks = [mid_ref[g, 0, third, n]] + [next_ref[g, d - 1, third, n] for d in range(1, SIDE)]
                late_ref[g, third, n] = blend(shares, n * LANE // 2 + third * GH, blocks)
        tree_start(three, g)

    def merge_three(g):
        tree_wait(three, g)
        packed = [late_stat[g]] + [pltpu.roll(last_stat[g, d - 1], LANE - 4 * d, 1) for d in range(1, SIDE)]
        value, shares = shares_of(packed)
        for n in range(2):
            blocks = [late_ref[g, 0, n]] + [last_ref[g, d - 1, n] for d in range(1, SIDE)]
            attended_ref[n * QT : (n + 1) * QT, g * GW : (g + 1) * GW] = blend(shares, n * LANE // 2, blocks)

    def project(phase):
        rows = slice(PHASES[phase][0] * GW, (PHASES[phase][-1] + 1) * GW)
        product = jnp.dot(attended_ref[:, rows], w_ref[rows, :], preferred_element_type=jnp.float32)
        if phase == 0:
            sum_ref[...] = product
        elif phase == 1:
            sum_ref[...] += product
        else:
            out_ref[...] = (sum_ref[...] + product).astype(jnp.bfloat16)

    def run(phase, beside):
        def send(by):
            for g in PHASES[phase]:
                for copy in one(g, by):
                    copy.start()

        beside = {at: list(acts) for at, acts in beside.items()}
        for by in range(1, SIDE):
            beside.setdefault(2 * by - 1, []).insert(0, (send, by))

        def body(b, carry):
            attend(phase, b)
            for at, acts in beside.items():

                @pl.when(b == at)
                def _():
                    for act, *args in acts:
                        act(*args)

            return carry

        lax.fori_loop(0, OWNERS // BATCH, body, 0)

    def ring_beside(phase):
        return {0: [(ring_end, phase, 1), (ring_start, phase, 2)], 4: [(ring_forward, phase, 2)]}

    def each(merge, phase):
        for g in PHASES[phase]:
            merge(g)

    run(0, ring_beside(1) | {5: [(ring_start, 2, 0)], 7: [(ring_end, 2, 0), (ring_start, 2, 1)]})
    ring_end(1, 2)
    run(1, ring_beside(2))
    each(merge_one, 0)
    ring_end(2, 2)
    run(2, {})
    each(merge_one, 1)
    each(merge_two, 0)
    each(merge_one, 2)
    each(merge_two, 1)
    each(merge_three, 0)
    w_home.wait()
    w_give.wait_send()
    w_take.wait_recv()
    project(0)
    each(merge_two, 2)
    each(merge_three, 1)
    project(1)
    ring_sent()
    for stage in range(3):
        for by in range(1, SIDE):
            list_copy(stage, by).wait_send()
    each(merge_three, 2)
    project(2)


def on_device(queries, keys, values, counts, passage_ids, out_weight):
    leads = (
        (SIDE, SIDE, SIDE),
        (SIDE - 1, SIDE, SIDE),
        (SIDE, SIDE, 2),
        (SIDE - 1, SIDE, 2),
        (SIDE, 2),
        (SIDE - 1, 2),
    )
    blocks = [pltpu.VMEM((GROUPS, SIDE, SIDE, SIDE, 2 * QT, GW), jnp.bfloat16)]
    blocks += [pltpu.VMEM((GROUPS, *lead, QT, GW), jnp.bfloat16) for lead in leads]
    for lead in ((SIDE,), (SIDE - 1,), (), (SIDE - 1,), (), (SIDE - 1,)):
        blocks.append(pltpu.VMEM((GROUPS, *lead, QT, LANE), jnp.float32))
    return pl.pallas_call(
        torus_kernel,
        out_shape=jax.ShapeDtypeStruct((2 * QT, D), jnp.bfloat16),
        in_specs=[pl.BlockSpec(memory_space=pltpu.SMEM)]
        + [pl.BlockSpec(memory_space=pltpu.VMEM)] * 2
        + [pl.BlockSpec(memory_space=pl.ANY)] * 3,
        out_specs=pl.BlockSpec(memory_space=pltpu.VMEM),
        scratch_shapes=blocks
        + [
            pltpu.VMEM(keys.shape, jnp.bfloat16),
            pltpu.VMEM(values.shape, jnp.bfloat16),
            pltpu.VMEM((D, D), jnp.bfloat16),
            pltpu.VMEM((SIDE, SIDE, SIDE, 2, LANE), jnp.int32),
            pltpu.VMEM((OWNERS, 1, LANE), jnp.int32),
            pltpu.SMEM((OWNERS, 1, LANE), jnp.int32),
            pltpu.VMEM((2 * QT, D), jnp.bfloat16),
            pltpu.VMEM((2 * QT, D), jnp.float32),
            pltpu.SemaphoreType.DMA((4,)),
            pltpu.SemaphoreType.DMA((GROUPS,)),
            pltpu.SemaphoreType.DMA((3, SIDE)),
            pltpu.SemaphoreType.DMA((3, SIDE)),
            pltpu.SemaphoreType.DMA((2,)),
            pltpu.SemaphoreType.DMA((GROUPS, 3, 4)),
            pltpu.SemaphoreType.DMA((GROUPS, 3, 4)),
            pltpu.SemaphoreType.DMA((3, GROUPS, SIDE, 2)),
            pltpu.SemaphoreType.DMA((3, GROUPS, SIDE, 2)),
        ],
        compiler_params=pltpu.CompilerParams(
            vmem_limit_bytes=60 * 2**20, collective_id=0, has_side_effects=True
        ),
        cost_estimate=pl.CostEstimate(flops=40 * 10**9, bytes_accessed=20 * 2**20, transcendentals=4 * 10**6),
        name="torus",
    )(counts, passage_ids, queries, keys, values, out_weight)


def solution(mesh):
    placed = (
        P(("grp", "dev"), None),
        P(("grp", "dev"), None, None),
        P(("grp", "dev"), None, None),
        P(("grp", "dev")),
        P(("grp", "dev"), None),
        P("grp", None),
    )
    return jax.shard_map(
        on_device, mesh=mesh, in_specs=placed, out_specs=P(("grp", "dev"), None), check_vma=False
    )
```

```python
import jax
import jax.numpy as jnp
from jax import lax
from jax.experimental import pallas as pl
from jax.experimental.pallas import tpu as pltpu
from jax.sharding import PartitionSpec as P

D = 2048
H = 32
HD = 64
QT = 16
PT = 64
GW = 256
GH = GW // HD
GROUPS = D // GW
LANE = 128
SIDE = 4
OWNERS = SIDE * SIDE * SIDE
PHASES = ((0, 1, 2), (3, 4, 5), (6, 7))
BATCH = 8
DEAD = -1e30
ORDERS = (("x", "y", "z"), ("y", "z", "x"), ("z", "x", "y"))
MESH = pl.DeviceIdType.MESH


def torus_kernel(
    counts_ref, ids_ref, mine_ref, k_hbm, v_hbm, w_hbm, out_ref,
    q_ref, part_ref, near_ref, mid_ref, next_ref, late_ref, last_ref,
    part_stat, near_stat, mid_stat, next_stat, late_stat, last_stat,
    k_ref, v_ref, w_ref, list_ref, code_ref, code_smem, attended_ref, sum_ref,
    load_sem, home_sem, list_send, list_recv, w_sem, ring_send, ring_recv, tree_send, tree_recv,
):
    me = lax.axis_index("dev")
    grp = lax.axis_index("grp")
    own = {"y": me >> 4, "x": (me >> 2) & 3, "z": me & 3}
    stride = {"y": SIDE * SIDE, "x": SIDE, "z": 1}
    line = {
        axis: {by: (grp, me + ((((own[axis] + by) & 3) - own[axis]) * stride[axis])) for by in range(1, SIDE)}
        for axis in own
    }
    loads = [
        pltpu.make_async_copy(k_hbm, k_ref, load_sem.at[0]),
        pltpu.make_async_copy(v_hbm, v_ref, load_sem.at[1]),
    ]
    for load in loads:
        load.start()
    barrier = pltpu.get_barrier_semaphore()
    for axis in line:
        for by in line[axis]:
            pl.semaphore_signal(barrier, inc=1, device_id=line[axis][by], device_id_type=MESH)
    pl.semaphore_signal(barrier, inc=1, device_id=(1 - grp, me), device_id_type=MESH)
    homes = [
        pltpu.make_async_copy(mine_ref.at[:, pl.ds(g * GW, GW)], q_ref.at[g, 0, 0, 0], home_sem.at[g])
        for g in range(GROUPS)
    ]
    for home in homes:
        home.start()
    list_len = ids_ref.shape[1]
    place = lax.broadcasted_iota(jnp.int32, (2, list_len), 1)
    row = lax.broadcasted_iota(jnp.int32, (2, list_len), 0)
    live = place < jnp.where(row == 0, counts_ref[0], counts_ref[1])
    list_ref[0, 0, 0] = jnp.full((2, LANE), -1, jnp.int32)
    list_ref[0, 0, 0, :, :list_len] = jnp.where(live, ids_ref[...], -1)
    pl.semaphore_wait(barrier, 10)

    whole, lower, upper = (0, 2 * QT), (0, QT), (QT, QT)
    both = ((0, 1, 3, lower), (1, 3, 1, upper))
    straight = both + ((2, 2, 2, whole),)

    def sends(stage):
        return both if stage == 2 else straight

    def order_of(g):
        return ORDERS[g % 3]

    def ring_block(g, stage, at, rows):
        spot = [pl.ds(0, SIDE) if n < stage else at if n == stage else 0 for n in range(3)]
        return q_ref.at[g, spot[0], spot[1], spot[2], pl.ds(*rows), :]

    def ring_own(g, stage, kind, by, at):
        source = ring_block(g, stage, 0, whole) if stage else mine_ref.at[:, pl.ds(g * GW, GW)]
        return pltpu.make_async_remote_copy(
            src_ref=source,
            dst_ref=ring_block(g, stage, at, whole),
            send_sem=ring_send.at[g, stage, kind],
            recv_sem=ring_recv.at[g, stage, kind],
            device_id=line[order_of(g)[stage]][by],
            device_id_type=MESH,
        )

    def ring_pass(g, stage, kind, by, at, rows):
        return pltpu.make_async_remote_copy(
            src_ref=ring_block(g, stage, at, rows),
            dst_ref=ring_block(g, stage, 2, rows),
            send_sem=ring_send.at[g, stage, 2 + kind],
            recv_sem=ring_recv.at[g, stage, 2 + kind],
            device_id=line[order_of(g)[stage]][by],
            device_id_type=MESH,
        )

    def ring_start(phase, stage):
        for g in PHASES[phase]:
            for kind, by, at, rows in sends(stage):
                ring_own(g, stage, kind, by, at).start()

    def ring_forward(phase, stage):
        for kind, by, at, rows in both:
            for g in PHASES[phase]:
                ring_own(g, stage, kind, by, at).wait_recv()
                ring_pass(g, stage, kind, by, at, rows).start()

    def ring_end(phase, stage):
        for g in PHASES[phase]:
            for kind, by, at, rows in sends(stage):
                if stage == 2:
                    ring_pass(g, stage, kind, by, at, rows).wait_recv()
                else:
                    ring_own(g, stage, kind, by, at).wait_recv()

    def ring_sent():
        for g in range(GROUPS):
            for stage in range(3):
                for kind, by, at, rows in sends(stage):
                    ring_own(g, stage, kind, by, at).wait_send()
                    if stage == 2:
                        ring_pass(g, stage, kind, by, at, rows).wait_send()

    def list_copy(stage, by):
        order = ("x", "y", "z")
        spot = {axis: 0 for axis in order}
        for axis in order[:stage]:
            spot[axis] = pl.ds(0, SIDE)
        source = list_ref.at[spot["y"], spot["x"], spot["z"]]
        spot[order[stage]] = SIDE - by
        return pltpu.make_async_remote_copy(
            src_ref=source,
            dst_ref=list_ref.at[spot["y"], spot["x"], spot["z"]],
            send_sem=list_send.at[stage, by],
            recv_sem=list_recv.at[stage, by],
            device_id=line[order[stage]][by],
            device_id_type=MESH,
        )

    def list_start(stage):
        for by in range(1, SIDE):
            list_copy(stage, by).start()

    def list_end(stage):
        for by in range(1, SIDE):
            list_copy(stage, by).wait_recv()

    w_rows = D // 2
    w_home = pltpu.make_async_copy(w_hbm, w_ref.at[pl.ds(grp * w_rows, w_rows)], load_sem.at[2])
    w_give = pltpu.make_async_remote_copy(
        src_ref=w_hbm,
        dst_ref=w_ref.at[pl.ds(grp * w_rows, w_rows)],
        send_sem=w_sem.at[0],
        recv_sem=w_sem.at[1],
        device_id=(1 - grp, me),
        device_id_type=MESH,
    )
    w_take = pltpu.make_async_remote_copy(
        src_ref=w_hbm,
        dst_ref=w_ref.at[pl.ds((1 - grp) * w_rows, w_rows)],
        send_sem=w_sem.at[0],
        recv_sem=w_sem.at[1],
        device_id=(1 - grp, me),
        device_id_type=MESH,
    )

    list_start(0)
    ring_start(0, 0)
    part_stat[...] = jnp.zeros(part_stat.shape, jnp.float32)
    for home in homes:
        home.wait()
    list_end(0)
    list_start(1)
    ring_end(0, 0)
    ring_start(0, 1)
    list_end(1)
    list_start(2)
    ring_end(0, 1)
    ring_start(0, 2)
    list_end(2)
    firsts, lasts = [], []
    for n in range(2):
        ids = list_ref[:, :, :, n, :].reshape(OWNERS, LANE)
        key = n * 1024 + lax.broadcasted_iota(jnp.int32, (OWNERS, LANE), 1) * 16 + (ids & 15)
        here = (ids >> 4) == me
        firsts.append(jnp.min(jnp.where(here, key, 1 << 20), axis=1, keepdims=True))
        lasts.append(jnp.max(jnp.where(here, key, -1), axis=1, keepdims=True))
    first, last = jnp.minimum(*firsts), jnp.maximum(*lasts)
    code = jnp.where(last < 0, -1, (first >> 10) + ((first & 15) << 1) + ((last & 15) << 5))
    code_ref[...] = jnp.broadcast_to(code, (OWNERS, LANE)).reshape(OWNERS, 1, LANE)
    code_move = pltpu.make_async_copy(code_ref, code_smem, load_sem.at[3])
    code_move.start()
    w_home.start()
    w_give.start()
    for load in loads:
        load.wait()
    code_move.wait()

    row_head = lax.broadcasted_iota(jnp.int32, (GH * QT, GW), 0) // QT
    lane_head = lax.broadcasted_iota(jnp.int32, (GH * QT, GW), 1) // HD
    diag = (row_head == lane_head).astype(jnp.float32).astype(jnp.bfloat16)
    stat_lane = lax.broadcasted_iota(jnp.int32, (QT, LANE), 1)
    near = stat_lane < HD

    def tree(sources, targets, g, stage, by):
        return [
            pltpu.make_async_remote_copy(
                src_ref=source,
                dst_ref=target,
                send_sem=tree_send.at[stage, g, by, n],
                recv_sem=tree_recv.at[stage, g, by, n],
                device_id=line[order_of(g)[stage]][by],
                device_id_type=MESH,
            )
            for n, (source, target) in enumerate(zip(sources, targets))
        ]

    def one(g, by):
        return tree(
            (part_ref.at[g, by], part_stat.at[g, by]), (near_ref.at[g, by - 1], near_stat.at[g, by - 1]), g, 0, by
        )

    def two(g, by):
        return tree((mid_ref.at[g, by], mid_stat.at[g]), (next_ref.at[g, by - 1], next_stat.at[g, by - 1]), g, 1, by)

    def three(g, by):
        return tree((late_ref.at[g, by], late_stat.at[g]), (last_ref.at[g, by - 1], last_stat.at[g, by - 1]), g, 2, by)

    def tree_start(stage, g):
        for by in range(1, SIDE):
            for copy in stage(g, by):
                copy.start()

    def tree_wait(stage, g):
        for by in range(1, SIDE):
            for copy in stage(g, by):
                copy.wait_send()
                copy.wait_recv()

    stride = {"y": SIDE * SIDE, "x": SIDE, "z": 1}

    def attend(phase, b):
        turn, part_half = b >> 1, b & 1
        items = [(n, g) for n in range(BATCH) for g in PHASES[phase]]
        slots, tags, scores, weights, stats = {}, {}, {}, {}, {}
        if phase < 2:
            third = turn + (turn >> 1) * (1 - 2 * (turn & 1))
            lane = stat_lane - third * GH
            for n, g in items:
                stats[n // SIDE, g] = part_stat[g, part_half * 2 + n // SIDE]
        else:
            delta = (turn + 1) & 3
            lane = stat_lane - part_half * (BATCH * GH)
            for g in PHASES[phase]:
                stats[0, g] = part_stat[g, delta]

        def place(n):
            if phase < 2:
                return part_half * 2 + n // SIDE, n % SIDE, third
            return delta, part_half * 2 + n // SIDE, n % SIDE

        def home(n):
            return (n // SIDE, (n % SIDE) * SIDE) if phase < 2 else (0, n)

        for n, g in items:
            told = code_smem[sum(at * stride[axis] for axis, at in zip(order_of(g), place(n))), 0, 0]
            code = jnp.maximum(told, 0)
            slots[n, g] = (code & 1, (code >> 1) & 15, (code >> 5) & 15)
            tags[n, g] = jnp.where(told < 0, -1.0, jnp.where((code & 1) > 0, 1.0, 0.0))

        def score(n, g):
            which, first, second = slots[n, g]
            cols = slice(g * GW, (g + 1) * GW)
            q = jnp.where(which > 0, q_ref[(g, *place(n), slice(QT, 2 * QT))], q_ref[(g, *place(n), slice(0, QT))])
            lhs = jnp.concatenate([q * jnp.bfloat16(0.125)] * GH, axis=0) * diag
            k = jnp.concatenate([k_ref[first, :, cols], k_ref[second, :, cols]], axis=0)
            scores[n, g] = lax.dot_general(lhs, k, (((1,), (1,)), ((), ())), preferred_element_type=jnp.float32)

        def weigh(n, g):
            which, first, second = slots[n, g]
            values = scores.pop((n, g))
            peak = jnp.max(values, axis=1, keepdims=True)
            shaped = jnp.exp(values - peak)
            total = jnp.sum(shaped, axis=1, keepdims=True)
            lse = peak + jnp.log(total * jnp.where(first == second, 0.5, 1.0))
            tile, at = home(n)
            stat = stats[tile, g]
            for h in range(GH):
                stat = jnp.where(lane == at * GH + h, lse[h * QT : (h + 1) * QT], stat)
            stats[tile, g] = jnp.where(((lane - LANE // 2) >> 2) == at, tags[n, g], stat)
            weights[n, g] = (shaped.astype(jnp.bfloat16), 1.0 / total)

        def apply(n, g):
            which, first, second = slots[n, g]
            cols = slice(g * GW, (g + 1) * GW)
            shaped, inverse = weights.pop((n, g))
            v = jnp.concatenate([v_ref[first, :, cols], v_ref[second, :, cols]], axis=0)
            full = jnp.dot(shaped, v, preferred_element_type=jnp.float32)
            for t in range(GW // LANE):
                lanes = slice(t * LANE, (t + 1) * LANE)
                a, c = (slice((2 * t + e) * QT, (2 * t + e + 1) * QT) for e in (0, 1))
                part = jnp.where(near, full[a, lanes] * inverse[a], full[c, lanes] * inverse[c])
                part_ref[(g, *place(n), slice(None), lanes)] = part.astype(jnp.bfloat16)

        for at in range(len(items) + 4):
            if at < len(items):
                score(*items[at])
            if 2 <= at < len(items) + 2:
                weigh(*items[at - 2])
            if 4 <= at:
                apply(*items[at - 4])
        for (tile, g), stat in stats.items():
            part_stat[g, part_half * 2 + tile if phase < 2 else delta] = stat

    def widen(share, at, t):
        pair = [jnp.broadcast_to(share[:, c : c + 1], (QT, LANE)) for c in (at + 2 * t, at + 2 * t + 1)]
        return jnp.where(near, pair[0], pair[1])

    def tiles(block):
        return [block[:, t * LANE : (t + 1) * LANE].astype(jnp.float32) for t in range(GW // LANE)]

    def blend(shares, at, blocks):
        sums = []
        for t in range(GW // LANE):
            total = widen(shares[0], at, t) * tiles(blocks[0])[t]
            for d in range(1, SIDE):
                total = total + widen(shares[d], at, t) * tiles(blocks[d])[t]
            sums.append(total)
        return jnp.concatenate(sums, axis=1).astype(jnp.bfloat16)

    def merge_one(g):
        tree_wait(one, g)
        packed = [part_stat[g, 0]] + [near_stat[g, d - 1] for d in range(1, SIDE)]
        tags = [pltpu.roll(stat, LANE // 2, 1) for stat in packed]
        tops = []
        for n in range(2):
            kept = [jnp.where(tag == n, stat, DEAD) for stat, tag in zip(packed, tags)]
            tops.append(jnp.maximum(jnp.maximum(kept[0], kept[1]), jnp.maximum(kept[2], kept[3])))
        terms = [
            jnp.exp(jnp.minimum(stat - jnp.where(tag == 1.0, tops[1], tops[0]), 0.0)) for stat, tag in zip(packed, tags)
        ]
        results, inverses = [], []
        for n in range(2):
            kept = [jnp.where(tag == n, term, 0.0) for term, tag in zip(terms, tags)]
            total = jnp.maximum(kept[0] + kept[1] + kept[2] + kept[3], 1e-30)
            results.append(tops[n] + jnp.log(total))
            inverses.append(1.0 / total)
        mid_stat[g] = jnp.where(stat_lane < LANE // 2, results[0], pltpu.roll(results[1], LANE // 2, 1))
        shares = [
            term * jnp.where(tag == 1.0, -inverses[1], jnp.where(tag == 0.0, inverses[0], 0.0))
            for term, tag in zip(terms, tags)
        ]

        def body(j, carry):
            second, third = j >> 2, j & 3
            blocks = [part_ref[g, 0, second, third]] + [near_ref[g, d - 1, second, third] for d in range(1, SIDE)]
            turned = [pltpu.roll(share, (LANE - GH * j) & (LANE - 1), 1) for share in shares]
            for t in range(GW // LANE):
                totals = [jnp.zeros((QT, LANE), jnp.float32)] * 2
                for d in range(SIDE):
                    factor, block = widen(turned[d], 0, t), tiles(blocks[d])[t]
                    totals = [
                        totals[0] + jnp.maximum(factor, 0.0) * block,
                        totals[1] - jnp.minimum(factor, 0.0) * block,
                    ]
                for n in range(2):
                    mid_ref[g, second, third, n, :, t * LANE : (t + 1) * LANE] = totals[n].astype(jnp.bfloat16)
            return carry

        lax.fori_loop(0, SIDE * SIDE, body, 0, unroll=4)
        tree_start(two, g)

    def shares_of(packed):
        top = jnp.maximum(jnp.maximum(packed[0], packed[1]), jnp.maximum(packed[2], packed[3]))
        terms = [jnp.exp(stat - top) for stat in packed]
        total = terms[0] + terms[1] + terms[2] + terms[3]
        inverse = 1.0 / total
        return top + jnp.log(total), [term * inverse for term in terms]

    def merge_two(g):
        tree_wait(two, g)
        packed = [mid_stat[g]] + [pltpu.roll(next_stat[g, d - 1], LANE - 16 * d, 1) for d in range(1, SIDE)]
        late_stat[g], shares = shares_of(packed)
        for third in range(SIDE):
            for n in range(2):
                blocks = [mid_ref[g, 0, third, n]] + [next_ref[g, d - 1, third, n] for d in range(1, SIDE)]
                late_ref[g, third, n] = blend(shares, n * LANE // 2 + third * GH, blocks)
        tree_start(three, g)

    def merge_three(g):
        tree_wait(three, g)
        packed = [late_stat[g]] + [pltpu.roll(last_stat[g, d - 1], LANE - 4 * d, 1) for d in range(1, SIDE)]
        value, shares = shares_of(packed)
        for n in range(2):
            blocks = [late_ref[g, 0, n]] + [last_ref[g, d - 1, n] for d in range(1, SIDE)]
            attended_ref[n * QT : (n + 1) * QT, g * GW : (g + 1) * GW] = blend(shares, n * LANE // 2, blocks)

    def project(phase):
        rows = slice(PHASES[phase][0] * GW, (PHASES[phase][-1] + 1) * GW)
        product = jnp.dot(attended_ref[:, rows], w_ref[rows, :], preferred_element_type=jnp.float32)
        if phase == 0:
            sum_ref[...] = product
        elif phase == 1:
            sum_ref[...] += product
        else:
            out_ref[...] = (sum_ref[...] + product).astype(jnp.bfloat16)

    def send(phase, *offsets):
        for by in offsets:
            for g in PHASES[phase]:
                for copy in one(g, by):
                    copy.start()

    def run(phase, beside):
        def body(b, carry):
            attend(phase, b)
            for at, acts in beside.items():

                @pl.when(b == at)
                def _():
                    for act, *args in acts:
                        act(*args)

            return carry

        lax.fori_loop(0, OWNERS // BATCH, body, 0)

    def each(merge, phase):
        for g in PHASES[phase]:
            merge(g)

    run(
        0,
        {
            1: [(ring_forward, 0, 2), (ring_start, 1, 0)],
            3: [(ring_end, 1, 0), (ring_start, 1, 1)],
            5: [(ring_end, 0, 2)],
            6: [(ring_end, 1, 1), (ring_start, 1, 2)],
        },
    )
    send(0, 2, 1, 3)
    run(
        1,
        {
            0: [(ring_start, 2, 0)],
            1: [(ring_forward, 1, 2)],
            2: [(ring_end, 2, 0), (ring_start, 2, 1)],
            4: [(ring_end, 2, 1), (ring_start, 2, 2)],
            5: [(ring_end, 1, 2)],
            7: [(ring_forward, 2, 2)],
        },
    )
    send(1, 2, 1, 3)
    each(merge_one, 0)
    ring_end(2, 2)
    run(2, {1: [(send, 2, 1)], 3: [(send, 2, 2)], 5: [(send, 2, 3)]})
    each(merge_one, 1)
    each(merge_two, 0)
    each(merge_one, 2)
    each(merge_two, 1)
    each(merge_three, 0)
    w_home.wait()
    w_give.wait_send()
    w_take.wait_recv()
    project(0)
    each(merge_two, 2)
    each(merge_three, 1)
    project(1)
    ring_sent()
    for stage in range(3):
        for by in range(1, SIDE):
            list_copy(stage, by).wait_send()
    each(merge_three, 2)
    project(2)


def on_device(queries, keys, values, counts, passage_ids, out_weight):
    leads = (
        (SIDE, SIDE, SIDE),
        (SIDE - 1, SIDE, SIDE),
        (SIDE, SIDE, 2),
        (SIDE - 1, SIDE, 2),
        (SIDE, 2),
        (SIDE - 1, 2),
    )
    blocks = [pltpu.VMEM((GROUPS, SIDE, SIDE, SIDE, 2 * QT, GW), jnp.bfloat16)]
    blocks += [pltpu.VMEM((GROUPS, *lead, QT, GW), jnp.bfloat16) for lead in leads]
    for lead in ((SIDE,), (SIDE - 1,), (), (SIDE - 1,), (), (SIDE - 1,)):
        blocks.append(pltpu.VMEM((GROUPS, *lead, QT, LANE), jnp.float32))
    return pl.pallas_call(
        torus_kernel,
        out_shape=jax.ShapeDtypeStruct((2 * QT, D), jnp.bfloat16),
        in_specs=[pl.BlockSpec(memory_space=pltpu.SMEM)]
        + [pl.BlockSpec(memory_space=pltpu.VMEM)] * 2
        + [pl.BlockSpec(memory_space=pl.ANY)] * 3,
        out_specs=pl.BlockSpec(memory_space=pltpu.VMEM),
        scratch_shapes=blocks
        + [
            pltpu.VMEM(keys.shape, jnp.bfloat16),
            pltpu.VMEM(values.shape, jnp.bfloat16),
            pltpu.VMEM((D, D), jnp.bfloat16),
            pltpu.VMEM((SIDE, SIDE, SIDE, 2, LANE), jnp.int32),
            pltpu.VMEM((OWNERS, 1, LANE), jnp.int32),
            pltpu.SMEM((OWNERS, 1, LANE), jnp.int32),
            pltpu.VMEM((2 * QT, D), jnp.bfloat16),
            pltpu.VMEM((2 * QT, D), jnp.float32),
            pltpu.SemaphoreType.DMA((4,)),
            pltpu.SemaphoreType.DMA((GROUPS,)),
            pltpu.SemaphoreType.DMA((3, SIDE)),
            pltpu.SemaphoreType.DMA((3, SIDE)),
            pltpu.SemaphoreType.DMA((2,)),
            pltpu.SemaphoreType.DMA((GROUPS, 3, 4)),
            pltpu.SemaphoreType.DMA((GROUPS, 3, 4)),
            pltpu.SemaphoreType.DMA((3, GROUPS, SIDE, 2)),
            pltpu.SemaphoreType.DMA((3, GROUPS, SIDE, 2)),
        ],
        compiler_params=pltpu.CompilerParams(
            vmem_limit_bytes=60 * 2**20, collective_id=0, has_side_effects=True
        ),
        cost_estimate=pl.CostEstimate(flops=40 * 10**9, bytes_accessed=20 * 2**20, transcendentals=4 * 10**6),
        name="torus",
    )(counts, passage_ids, queries, keys, values, out_weight)


def solution(mesh):
    placed = (
        P(("grp", "dev"), None),
        P(("grp", "dev"), None, None),
        P(("grp", "dev"), None, None),
        P(("grp", "dev")),
        P(("grp", "dev"), None),
        P("grp", None),
    )
    return jax.shard_map(
        on_device, mesh=mesh, in_specs=placed, out_specs=P(("grp", "dev"), None), check_vma=False
    )
```

```python
import jax
import jax.numpy as jnp
from jax import lax
from jax.experimental import pallas as pl
from jax.experimental.pallas import tpu as pltpu
from jax.sharding import PartitionSpec as P

D = 2048
H = 32
HD = 64
QT = 16
PT = 64
GW = 256
GH = GW // HD
GROUPS = D // GW
LANE = 128
SIDE = 4
OWNERS = SIDE * SIDE * SIDE
PHASES = ((0, 1, 2), (3, 4, 5), (6, 7))
BATCH = 4

DEAD = -1e30
ORDERS = (("x", "y", "z"), ("y", "z", "x"), ("z", "x", "y"))
MESH = pl.DeviceIdType.MESH


def torus_kernel(
    counts_ref, ids_ref, mine_ref, k_hbm, v_hbm, w_hbm, out_ref,
    q_ref, part_ref, near_ref, mid_ref, next_ref, late_ref, last_ref,
    part_stat, near_stat, mid_stat, next_stat, late_stat, last_stat,
    k_ref, v_ref, w_ref, list_ref, code_ref, code_smem, score_ref, weight_ref, inverse_ref, attended_ref, sum_ref,
    load_sem, home_sem, list_send, list_recv, w_sem, ring_send, ring_recv, tree_send, tree_recv,
):
    me = lax.axis_index("dev")
    grp = lax.axis_index("grp")
    own = {"y": me >> 4, "x": (me >> 2) & 3, "z": me & 3}
    stride = {"y": SIDE * SIDE, "x": SIDE, "z": 1}
    line = {
        axis: {by: (grp, me + ((((own[axis] + by) & 3) - own[axis]) * stride[axis])) for by in range(1, SIDE)}
        for axis in own
    }
    loads = [
        pltpu.make_async_copy(k_hbm, k_ref, load_sem.at[0]),
        pltpu.make_async_copy(v_hbm, v_ref, load_sem.at[1]),
    ]
    for load in loads:
        load.start()
    barrier = pltpu.get_barrier_semaphore()
    for axis in line:
        for by in line[axis]:
            pl.semaphore_signal(barrier, inc=1, device_id=line[axis][by], device_id_type=MESH)
    pl.semaphore_signal(barrier, inc=1, device_id=(1 - grp, me), device_id_type=MESH)
    homes = [
        pltpu.make_async_copy(mine_ref.at[:, pl.ds(g * GW, GW)], q_ref.at[g, 0, 0, 0], home_sem.at[g])
        for g in range(GROUPS)
    ]
    for home in homes:
        home.start()
    list_len = ids_ref.shape[1]
    place = lax.broadcasted_iota(jnp.int32, (2, list_len), 1)
    row = lax.broadcasted_iota(jnp.int32, (2, list_len), 0)
    live = place < jnp.where(row == 0, counts_ref[0], counts_ref[1])
    list_ref[0, 0, 0] = jnp.full((2, LANE), -1, jnp.int32)
    list_ref[0, 0, 0, :, :list_len] = jnp.where(live, ids_ref[...], -1)
    pl.semaphore_wait(barrier, 10)

    whole, lower, upper = (0, 2 * QT), (0, QT), (QT, QT)
    both = ((0, 1, 3, lower), (1, 3, 1, upper))
    straight = both + ((2, 2, 2, whole),)

    def sends(stage):
        return both if stage == 2 else straight

    def order_of(g):
        return ORDERS[g % 3]

    def ring_block(g, stage, at, rows):
        spot = [pl.ds(0, SIDE) if n < stage else at if n == stage else 0 for n in range(3)]
        return q_ref.at[g, spot[0], spot[1], spot[2], pl.ds(*rows), :]

    def ring_own(g, stage, kind, by, at):
        source = ring_block(g, stage, 0, whole) if stage else mine_ref.at[:, pl.ds(g * GW, GW)]
        return pltpu.make_async_remote_copy(
            src_ref=source,
            dst_ref=ring_block(g, stage, at, whole),
            send_sem=ring_send.at[g, stage, kind],
            recv_sem=ring_recv.at[g, stage, kind],
            device_id=line[order_of(g)[stage]][by],
            device_id_type=MESH,
        )

    def ring_pass(g, stage, kind, by, at, rows):
        return pltpu.make_async_remote_copy(
            src_ref=ring_block(g, stage, at, rows),
            dst_ref=ring_block(g, stage, 2, rows),
            send_sem=ring_send.at[g, stage, 2 + kind],
            recv_sem=ring_recv.at[g, stage, 2 + kind],
            device_id=line[order_of(g)[stage]][by],
            device_id_type=MESH,
        )

    def ring_start(phase, stage):
        for g in PHASES[phase]:
            for kind, by, at, rows in sends(stage):
                ring_own(g, stage, kind, by, at).start()

    def ring_forward(phase, stage):
        for kind, by, at, rows in both:
            for g in PHASES[phase]:
                ring_own(g, stage, kind, by, at).wait_recv()
                ring_pass(g, stage, kind, by, at, rows).start()

    def ring_end(phase, stage):
        for g in PHASES[phase]:
            for kind, by, at, rows in sends(stage):
                if stage == 2:
                    ring_pass(g, stage, kind, by, at, rows).wait_recv()
                else:
                    ring_own(g, stage, kind, by, at).wait_recv()

    def ring_sent():
        for g in range(GROUPS):
            for stage in range(3):
                for kind, by, at, rows in sends(stage):
                    ring_own(g, stage, kind, by, at).wait_send()
                    if stage == 2:
                        ring_pass(g, stage, kind, by, at, rows).wait_send()

    def list_copy(stage, by):
        order = ("x", "y", "z")
        spot = {axis: 0 for axis in order}
        for axis in order[:stage]:
            spot[axis] = pl.ds(0, SIDE)
        source = list_ref.at[spot["y"], spot["x"], spot["z"]]
        spot[order[stage]] = SIDE - by
        return pltpu.make_async_remote_copy(
            src_ref=source,
            dst_ref=list_ref.at[spot["y"], spot["x"], spot["z"]],
            send_sem=list_send.at[stage, by],
            recv_sem=list_recv.at[stage, by],
            device_id=line[order[stage]][by],
            device_id_type=MESH,
        )

    def list_start(stage):
        for by in range(1, SIDE):
            list_copy(stage, by).start()

    def list_end(stage):
        for by in range(1, SIDE):
            list_copy(stage, by).wait_recv()

    w_rows = D // 2
    w_home = pltpu.make_async_copy(w_hbm, w_ref.at[pl.ds(grp * w_rows, w_rows)], load_sem.at[2])
    w_give = pltpu.make_async_remote_copy(
        src_ref=w_hbm,
        dst_ref=w_ref.at[pl.ds(grp * w_rows, w_rows)],
        send_sem=w_sem.at[0],
        recv_sem=w_sem.at[1],
        device_id=(1 - grp, me),
        device_id_type=MESH,
    )
    w_take = pltpu.make_async_remote_copy(
        src_ref=w_hbm,
        dst_ref=w_ref.at[pl.ds((1 - grp) * w_rows, w_rows)],
        send_sem=w_sem.at[0],
        recv_sem=w_sem.at[1],
        device_id=(1 - grp, me),
        device_id_type=MESH,
    )

    list_start(0)
    ring_start(0, 0)
    part_stat[...] = jnp.zeros(part_stat.shape, jnp.float32)
    for home in homes:
        home.wait()
    list_end(0)
    list_start(1)
    ring_end(0, 0)
    ring_start(0, 1)
    list_end(1)
    list_start(2)
    ring_end(0, 1)
    ring_start(0, 2)
    list_end(2)
    firsts, lasts = [], []
    for n in range(2):
        ids = list_ref[:, :, :, n, :].reshape(OWNERS, LANE)
        key = n * 1024 + lax.broadcasted_iota(jnp.int32, (OWNERS, LANE), 1) * 16 + (ids & 15)
        here = (ids >> 4) == me
        firsts.append(jnp.min(jnp.where(here, key, 1 << 20), axis=1, keepdims=True))
        lasts.append(jnp.max(jnp.where(here, key, -1), axis=1, keepdims=True))
    first, last = jnp.minimum(*firsts), jnp.maximum(*lasts)
    code = jnp.where(last < 0, -1, (first >> 10) + ((first & 15) << 1) + ((last & 15) << 5))
    code_ref[...] = jnp.broadcast_to(code, (OWNERS, LANE)).reshape(OWNERS, 1, LANE)
    code_move = pltpu.make_async_copy(code_ref, code_smem, load_sem.at[3])
    code_move.start()
    w_home.start()
    w_give.start()
    for load in loads:
        load.wait()
    code_move.wait()

    row_head = lax.broadcasted_iota(jnp.int32, (GH * QT, GW), 0) // QT
    lane_head = lax.broadcasted_iota(jnp.int32, (GH * QT, GW), 1) // HD
    diag = jnp.where(row_head == lane_head, 0.125, 0.0).astype(jnp.bfloat16)
    stat_lane = lax.broadcasted_iota(jnp.int32, (QT, LANE), 1)
    near = stat_lane < HD

    def tree(sources, targets, g, stage, by):
        return [
            pltpu.make_async_remote_copy(
                src_ref=source,
                dst_ref=target,
                send_sem=tree_send.at[stage, g, by, n],
                recv_sem=tree_recv.at[stage, g, by, n],
                device_id=line[order_of(g)[stage]][by],
                device_id_type=MESH,
            )
            for n, (source, target) in enumerate(zip(sources, targets))
        ]

    def one(g, by):
        return tree(
            (part_ref.at[g, by], part_stat.at[g, by]), (near_ref.at[g, by - 1], near_stat.at[g, by - 1]), g, 0, by
        )

    def two(g, by):
        return tree((mid_ref.at[g, by], mid_stat.at[g]), (next_ref.at[g, by - 1], next_stat.at[g, by - 1]), g, 1, by)

    def three(g, by):
        return tree((late_ref.at[g, by], late_stat.at[g]), (last_ref.at[g, by - 1], last_stat.at[g, by - 1]), g, 2, by)

    def tree_start(stage, g):
        for by in range(1, SIDE):
            for copy in stage(g, by):
                copy.start()

    def tree_wait(stage, g):
        for by in range(1, SIDE):
            for copy in stage(g, by):
                copy.wait_send()
                copy.wait_recv()

    stride = {"y": SIDE * SIDE, "x": SIDE, "z": 1}

    def place(phase, b, n):
        turn, quarter = b >> 2, b & 3
        if phase < 2:
            return quarter, n, turn + (turn >> 1) * (1 - 2 * (turn & 1))
        return (turn + 1) & 3, quarter, n

    def told(phase, b, n, g):
        return code_smem[sum(at * stride[axis] for axis, at in zip(order_of(g), place(phase, b, n))), 0, 0]

    def passages(code):
        code = jnp.maximum(code, 0)
        return code & 1, (code >> 1) & 15, (code >> 5) & 15

    def items_of(phase):
        return [(n, g) for n in range(BATCH) for g in PHASES[phase]]

    def score(phase, b, at):
        n, g = items_of(phase)[at]
        which, first, second = passages(told(phase, b, n, g))
        cols = slice(g * GW, (g + 1) * GW)
        spot = place(phase, b, n)
        q = jnp.where(which > 0, q_ref[(g, *spot, slice(QT, 2 * QT))], q_ref[(g, *spot, slice(0, QT))])
        lhs = jnp.concatenate([q] * GH, axis=0) * diag
        k = jnp.concatenate([k_ref[first, :, cols], k_ref[second, :, cols]], axis=0)
        score_ref[at] = lax.dot_general(lhs, k, (((1,), (1,)), ((), ())), preferred_element_type=jnp.float32)

    def weigh(phase, b, at, packed):
        n, g = items_of(phase)[at]
        code = told(phase, b, n, g)
        which, first, second = passages(code)
        values = score_ref[at]
        peak = jnp.max(values, axis=1, keepdims=True)
        shaped = jnp.exp(values - peak)
        total = jnp.sum(shaped, axis=1, keepdims=True)
        weight_ref[at] = shaped.astype(jnp.bfloat16)
        rows = [slice(h * QT, (h + 1) * QT) for h in range(GH)]
        for t in range(GW // LANE):
            pair = jnp.where(near, total[rows[2 * t]], total[rows[2 * t + 1]])
            inverse_ref[at, :, t * LANE : (t + 1) * LANE] = 1.0 / pair
        lane, peaks, totals, tags = packed[g]
        spot = n * SIDE if phase < 2 else n
        for h in range(GH):
            here = lane == spot * GH + h
            peaks = jnp.where(here, peak[rows[h]], peaks)
            totals = jnp.where(here, total[rows[h]], totals)
        share = jnp.where(first == second, 0.5, 1.0)
        totals = jnp.where((lane >> 2) == spot, totals * share, totals)
        tag = jnp.where(code < 0, -1.0, jnp.where(which > 0, 1.0, 0.0))
        tags = jnp.where(((lane - LANE // 2) >> 2) == spot, tag, tags)
        packed[g] = (lane, peaks, totals, tags)

    def apply(phase, b, at):
        n, g = items_of(phase)[at]
        which, first, second = passages(told(phase, b, n, g))
        cols = slice(g * GW, (g + 1) * GW)
        v = jnp.concatenate([v_ref[first, :, cols], v_ref[second, :, cols]], axis=0)
        full = jnp.dot(weight_ref[at], v, preferred_element_type=jnp.float32)
        for t in range(GW // LANE):
            lanes = slice(t * LANE, (t + 1) * LANE)
            a, c = (slice((2 * t + e) * QT, (2 * t + e + 1) * QT) for e in (0, 1))
            part = jnp.where(near, full[a, lanes], full[c, lanes]) * inverse_ref[at, :, lanes]
            part_ref[(g, *place(phase, b, n), slice(None), lanes)] = part.astype(jnp.bfloat16)

    def pack_open(phase, b):
        first, second, third = place(phase, b, 0)
        lane = stat_lane - (third * GH if phase < 2 else second * GH * SIDE)
        zero = jnp.zeros((QT, LANE), jnp.float32)
        return {g: (lane, zero, zero + 1.0, zero) for g in PHASES[phase]}

    def pack_close(phase, b, packed):
        first, second, third = place(phase, b, 0)
        for g, (lane, peaks, totals, tags) in packed.items():
            if phase < 2:
                mine = (lane & 15) < GH
            else:
                mine = ((stat_lane & 63) >> 4) == second
            value = jnp.where(stat_lane < LANE // 2, peaks + jnp.log(totals), tags)
            part_stat[g, first] = jnp.where(mine, value, part_stat[g, first])

    def attend(phase, b):
        later, latest = jnp.minimum(b + 1, OWNERS // BATCH - 1), jnp.minimum(b + 2, OWNERS // BATCH - 1)
        packed = pack_open(phase, later)
        for at in range(len(items_of(phase))):
            apply(phase, b, at)
            weigh(phase, later, at, packed)
            score(phase, latest, at)
        pack_close(phase, later, packed)

    def prepare(phase):
        for at in range(len(items_of(phase))):
            score(phase, 0, at)
        packed = pack_open(phase, 0)
        for at in range(len(items_of(phase))):
            weigh(phase, 0, at, packed)
            score(phase, 1, at)
        pack_close(phase, 0, packed)

    def widen(share, at, t):
        pair = [jnp.broadcast_to(share[:, c : c + 1], (QT, LANE)) for c in (at + 2 * t, at + 2 * t + 1)]
        return jnp.where(near, pair[0], pair[1])

    def tiles(block):
        return [block[:, t * LANE : (t + 1) * LANE].astype(jnp.float32) for t in range(GW // LANE)]

    def blend(shares, at, blocks):
        sums = []
        for t in range(GW // LANE):
            total = widen(shares[0], at, t) * tiles(blocks[0])[t]
            for d in range(1, SIDE):
                total = total + widen(shares[d], at, t) * tiles(blocks[d])[t]
            sums.append(total)
        return jnp.concatenate(sums, axis=1).astype(jnp.bfloat16)

    def merge_one(g):
        tree_wait(one, g)
        packed = [part_stat[g, 0]] + [near_stat[g, d - 1] for d in range(1, SIDE)]
        tags = [pltpu.roll(stat, LANE // 2, 1) for stat in packed]
        tops = []
        for n in range(2):
            kept = [jnp.where(tag == n, stat, DEAD) for stat, tag in zip(packed, tags)]
            tops.append(jnp.maximum(jnp.maximum(kept[0], kept[1]), jnp.maximum(kept[2], kept[3])))
        terms = [
            jnp.exp(jnp.minimum(stat - jnp.where(tag == 1.0, tops[1], tops[0]), 0.0)) for stat, tag in zip(packed, tags)
        ]
        results, inverses = [], []
        for n in range(2):
            kept = [jnp.where(tag == n, term, 0.0) for term, tag in zip(terms, tags)]
            total = jnp.maximum(kept[0] + kept[1] + kept[2] + kept[3], 1e-30)
            results.append(tops[n] + jnp.log(total))
            inverses.append(1.0 / total)
        mid_stat[g] = jnp.where(stat_lane < LANE // 2, results[0], pltpu.roll(results[1], LANE // 2, 1))
        shares = [
            term * jnp.where(tag == 1.0, -inverses[1], jnp.where(tag == 0.0, inverses[0], 0.0))
            for term, tag in zip(terms, tags)
        ]

        def body(j, carry):
            second, third = j >> 2, j & 3
            blocks = [part_ref[g, 0, second, third]] + [near_ref[g, d - 1, second, third] for d in range(1, SIDE)]
            turned = [pltpu.roll(share, (LANE - GH * j) & (LANE - 1), 1) for share in shares]
            for t in range(GW // LANE):
                totals = [jnp.zeros((QT, LANE), jnp.float32)] * 2
                for d in range(SIDE):
                    factor, block = widen(turned[d], 0, t), tiles(blocks[d])[t]
                    totals = [
                        totals[0] + jnp.maximum(factor, 0.0) * block,
                        totals[1] - jnp.minimum(factor, 0.0) * block,
                    ]
                for n in range(2):
                    mid_ref[g, second, third, n, :, t * LANE : (t + 1) * LANE] = totals[n].astype(jnp.bfloat16)
            return carry

        lax.fori_loop(0, SIDE * SIDE, body, 0, unroll=4)
        tree_start(two, g)

    def shares_of(packed):
        top = jnp.maximum(jnp.maximum(packed[0], packed[1]), jnp.maximum(packed[2], packed[3]))
        terms = [jnp.exp(stat - top) for stat in packed]
        total = terms[0] + terms[1] + terms[2] + terms[3]
        inverse = 1.0 / total
        return top + jnp.log(total), [term * inverse for term in terms]

    def merge_two(g):
        tree_wait(two, g)
        packed = [mid_stat[g]] + [pltpu.roll(next_stat[g, d - 1], LANE - 16 * d, 1) for d in range(1, SIDE)]
        late_stat[g], shares = shares_of(packed)
        for third in range(SIDE):
            for n in range(2):
                blocks = [mid_ref[g, 0, third, n]] + [next_ref[g, d - 1, third, n] for d in range(1, SIDE)]
                late_ref[g, third, n] = blend(shares, n * LANE // 2 + third * GH, blocks)
        tree_start(three, g)

    def merge_three(g):
        tree_wait(three, g)
        packed = [late_stat[g]] + [pltpu.roll(last_stat[g, d - 1], LANE - 4 * d, 1) for d in range(1, SIDE)]
        value, shares = shares_of(packed)
        for n in range(2):
            blocks = [late_ref[g, 0, n]] + [last_ref[g, d - 1, n] for d in range(1, SIDE)]
            attended_ref[n * QT : (n + 1) * QT, g * GW : (g + 1) * GW] = blend(shares, n * LANE // 2, blocks)

    def project(phase):
        rows = slice(PHASES[phase][0] * GW, (PHASES[phase][-1] + 1) * GW)
        product = jnp.dot(attended_ref[:, rows], w_ref[rows, :], preferred_element_type=jnp.float32)
        if phase == 0:
            sum_ref[...] = product
        elif phase == 1:
            sum_ref[...] += product
        else:
            out_ref[...] = (sum_ref[...] + product).astype(jnp.bfloat16)

    def send(phase, *offsets):
        for by in offsets:
            for g in PHASES[phase]:
                for copy in one(g, by):
                    copy.start()

    def run(phase, beside):
        prepare(phase)

        def body(b, carry):
            attend(phase, b)
            for at, acts in beside.items():

                @pl.when(b == at)
                def _():
                    for act, *args in acts:
                        act(*args)

            return carry

        lax.fori_loop(0, OWNERS // BATCH, body, 0)

    def each(merge, phase):
        for g in PHASES[phase]:
            merge(g)

    run(
        0,
        {
            1: [(ring_forward, 0, 2), (ring_start, 1, 0)],
            5: [(ring_end, 1, 0), (ring_start, 1, 1)],
            9: [(ring_end, 0, 2)],
            10: [(ring_end, 1, 1), (ring_start, 1, 2)],
        },
    )
    send(0, 2, 1, 3)
    run(
        1,
        {
            0: [(ring_start, 2, 0)],
            1: [(ring_forward, 1, 2)],
            4: [(ring_end, 2, 0), (ring_start, 2, 1)],
            8: [(ring_end, 2, 1), (ring_start, 2, 2)],
            9: [(ring_end, 1, 2)],
            14: [(ring_forward, 2, 2)],
        },
    )
    send(1, 2, 1, 3)
    each(merge_one, 0)
    ring_end(2, 2)
    run(2, {3: [(send, 2, 1)], 7: [(send, 2, 2)], 11: [(send, 2, 3)]})
    each(merge_one, 1)
    each(merge_two, 0)
    each(merge_one, 2)
    each(merge_two, 1)
    each(merge_three, 0)
    w_home.wait()
    w_give.wait_send()
    w_take.wait_recv()
    project(0)
    each(merge_two, 2)
    each(merge_three, 1)
    project(1)
    ring_sent()
    for stage in range(3):
        for by in range(1, SIDE):
            list_copy(stage, by).wait_send()
    each(merge_three, 2)
    project(2)


def on_device(queries, keys, values, counts, passage_ids, out_weight):
    leads = (
        (SIDE, SIDE, SIDE),
        (SIDE - 1, SIDE, SIDE),
        (SIDE, SIDE, 2),
        (SIDE - 1, SIDE, 2),
        (SIDE, 2),
        (SIDE - 1, 2),
    )
    blocks = [pltpu.VMEM((GROUPS, SIDE, SIDE, SIDE, 2 * QT, GW), jnp.bfloat16)]
    blocks += [pltpu.VMEM((GROUPS, *lead, QT, GW), jnp.bfloat16) for lead in leads]
    for lead in ((SIDE,), (SIDE - 1,), (), (SIDE - 1,), (), (SIDE - 1,)):
        blocks.append(pltpu.VMEM((GROUPS, *lead, QT, LANE), jnp.float32))
    return pl.pallas_call(
        torus_kernel,
        out_shape=jax.ShapeDtypeStruct((2 * QT, D), jnp.bfloat16),
        in_specs=[pl.BlockSpec(memory_space=pltpu.SMEM)]
        + [pl.BlockSpec(memory_space=pltpu.VMEM)] * 2
        + [pl.BlockSpec(memory_space=pl.ANY)] * 3,
        out_specs=pl.BlockSpec(memory_space=pltpu.VMEM),
        scratch_shapes=blocks
        + [
            pltpu.VMEM(keys.shape, jnp.bfloat16),
            pltpu.VMEM(values.shape, jnp.bfloat16),
            pltpu.VMEM((D, D), jnp.bfloat16),
            pltpu.VMEM((SIDE, SIDE, SIDE, 2, LANE), jnp.int32),
            pltpu.VMEM((OWNERS, 1, LANE), jnp.int32),
            pltpu.SMEM((OWNERS, 1, LANE), jnp.int32),
            pltpu.VMEM((3 * BATCH, GH * QT, 2 * PT), jnp.float32),
            pltpu.VMEM((3 * BATCH, GH * QT, 2 * PT), jnp.bfloat16),
            pltpu.VMEM((3 * BATCH, QT, GW), jnp.float32),
            pltpu.VMEM((2 * QT, D), jnp.bfloat16),
            pltpu.VMEM((2 * QT, D), jnp.float32),
            pltpu.SemaphoreType.DMA((4,)),
            pltpu.SemaphoreType.DMA((GROUPS,)),
            pltpu.SemaphoreType.DMA((3, SIDE)),
            pltpu.SemaphoreType.DMA((3, SIDE)),
            pltpu.SemaphoreType.DMA((2,)),
            pltpu.SemaphoreType.DMA((GROUPS, 3, 4)),
            pltpu.SemaphoreType.DMA((GROUPS, 3, 4)),
            pltpu.SemaphoreType.DMA((3, GROUPS, SIDE, 2)),
            pltpu.SemaphoreType.DMA((3, GROUPS, SIDE, 2)),
        ],
        compiler_params=pltpu.CompilerParams(
            vmem_limit_bytes=60 * 2**20, collective_id=0, has_side_effects=True
        ),
        cost_estimate=pl.CostEstimate(flops=40 * 10**9, bytes_accessed=20 * 2**20, transcendentals=4 * 10**6),
        name="torus",
    )(counts, passage_ids, queries, keys, values, out_weight)


def solution(mesh):
    placed = (
        P(("grp", "dev"), None),
        P(("grp", "dev"), None, None),
        P(("grp", "dev"), None, None),
        P(("grp", "dev")),
        P(("grp", "dev"), None),
        P("grp", None),
    )
    return jax.shard_map(
        on_device, mesh=mesh, in_specs=placed, out_specs=P(("grp", "dev"), None), check_vma=False
    )
```

```python
import jax
import jax.numpy as jnp
from jax import lax
from jax.experimental import pallas as pl
from jax.experimental.pallas import tpu as pltpu
from jax.sharding import PartitionSpec as P

D = 2048
H = 32
HD = 64
QT = 16
PT = 64
GW = 256
GH = GW // HD
GROUPS = D // GW
LANE = 128
SIDE = 4
OWNERS = SIDE * SIDE * SIDE
PHASES = ((0, 1, 2), (3, 4, 5), (6, 7))
BATCH = 4

DEAD = -1e30
ORDERS = (("x", "y", "z"), ("y", "z", "x"), ("z", "x", "y"))
MESH = pl.DeviceIdType.MESH


def torus_kernel(
    counts_ref, ids_ref, mine_ref, k_hbm, v_hbm, w_hbm, out_ref,
    q_ref, part_ref, near_ref, mid_ref, next_ref, late_ref, last_ref,
    part_stat, near_stat, mid_stat, next_stat, late_stat, last_stat,
    k_ref, v_ref, w_ref, list_ref, code_ref, code_smem, score_ref, weight_ref, inverse_ref, attended_ref, sum_ref,
    load_sem, home_sem, list_send, list_recv, w_sem, ring_send, ring_recv, tree_send, tree_recv,
):
    me = lax.axis_index("dev")
    grp = lax.axis_index("grp")
    own = {"y": me >> 4, "x": (me >> 2) & 3, "z": me & 3}
    stride = {"y": SIDE * SIDE, "x": SIDE, "z": 1}
    line = {
        axis: {by: (grp, me + ((((own[axis] + by) & 3) - own[axis]) * stride[axis])) for by in range(1, SIDE)}
        for axis in own
    }
    loads = [
        pltpu.make_async_copy(k_hbm, k_ref, load_sem.at[0]),
        pltpu.make_async_copy(v_hbm, v_ref, load_sem.at[1]),
    ]
    for load in loads:
        load.start()
    barrier = pltpu.get_barrier_semaphore()
    for axis in line:
        for by in line[axis]:
            pl.semaphore_signal(barrier, inc=1, device_id=line[axis][by], device_id_type=MESH)
    pl.semaphore_signal(barrier, inc=1, device_id=(1 - grp, me), device_id_type=MESH)
    homes = [
        pltpu.make_async_copy(mine_ref.at[:, pl.ds(g * GW, GW)], q_ref.at[g, 0, 0, 0], home_sem.at[g])
        for g in range(GROUPS)
    ]
    for home in homes:
        home.start()
    list_len = ids_ref.shape[1]
    place = lax.broadcasted_iota(jnp.int32, (2, list_len), 1)
    row = lax.broadcasted_iota(jnp.int32, (2, list_len), 0)
    live = place < jnp.where(row == 0, counts_ref[0], counts_ref[1])
    list_ref[0, 0, 0] = jnp.full((2, LANE), -1, jnp.int32)
    list_ref[0, 0, 0, :, :list_len] = jnp.where(live, ids_ref[...], -1)
    pl.semaphore_wait(barrier, 10)

    whole, lower, upper = (0, 2 * QT), (0, QT), (QT, QT)
    both = ((0, 1, 3, lower), (1, 3, 1, upper))
    straight = both + ((2, 2, 2, whole),)

    def sends(stage):
        return both if stage == 2 else straight

    def order_of(g):
        return ORDERS[g % 3]

    def ring_block(g, stage, at, rows):
        spot = [pl.ds(0, SIDE) if n < stage else at if n == stage else 0 for n in range(3)]
        return q_ref.at[g, spot[0], spot[1], spot[2], pl.ds(*rows), :]

    def ring_own(g, stage, kind, by, at):
        source = ring_block(g, stage, 0, whole) if stage else mine_ref.at[:, pl.ds(g * GW, GW)]
        return pltpu.make_async_remote_copy(
            src_ref=source,
            dst_ref=ring_block(g, stage, at, whole),
            send_sem=ring_send.at[g, stage, kind],
            recv_sem=ring_recv.at[g, stage, kind],
            device_id=line[order_of(g)[stage]][by],
            device_id_type=MESH,
        )

    def ring_pass(g, stage, kind, by, at, rows):
        return pltpu.make_async_remote_copy(
            src_ref=ring_block(g, stage, at, rows),
            dst_ref=ring_block(g, stage, 2, rows),
            send_sem=ring_send.at[g, stage, 2 + kind],
            recv_sem=ring_recv.at[g, stage, 2 + kind],
            device_id=line[order_of(g)[stage]][by],
            device_id_type=MESH,
        )

    def ring_start(phase, stage):
        for g in PHASES[phase]:
            for kind, by, at, rows in sends(stage):
                ring_own(g, stage, kind, by, at).start()

    def ring_forward(phase, stage):
        for kind, by, at, rows in both:
            for g in PHASES[phase]:
                ring_own(g, stage, kind, by, at).wait_recv()
                ring_pass(g, stage, kind, by, at, rows).start()

    def ring_end(phase, stage):
        for g in PHASES[phase]:
            for kind, by, at, rows in sends(stage):
                if stage == 2:
                    ring_pass(g, stage, kind, by, at, rows).wait_recv()
                else:
                    ring_own(g, stage, kind, by, at).wait_recv()

    def ring_sent():
        for g in range(GROUPS):
            for stage in range(3):
                for kind, by, at, rows in sends(stage):
                    ring_own(g, stage, kind, by, at).wait_send()
                    if stage == 2:
                        ring_pass(g, stage, kind, by, at, rows).wait_send()

    def list_copy(stage, by):
        order = ("x", "y", "z")
        spot = {axis: 0 for axis in order}
        for axis in order[:stage]:
            spot[axis] = pl.ds(0, SIDE)
        source = list_ref.at[spot["y"], spot["x"], spot["z"]]
        spot[order[stage]] = SIDE - by
        return pltpu.make_async_remote_copy(
            src_ref=source,
            dst_ref=list_ref.at[spot["y"], spot["x"], spot["z"]],
            send_sem=list_send.at[stage, by],
            recv_sem=list_recv.at[stage, by],
            device_id=line[order[stage]][by],
            device_id_type=MESH,
        )

    def list_start(stage):
        for by in range(1, SIDE):
            list_copy(stage, by).start()

    def list_end(stage):
        for by in range(1, SIDE):
            list_copy(stage, by).wait_recv()

    w_rows = D // 2
    w_home = pltpu.make_async_copy(w_hbm, w_ref.at[pl.ds(grp * w_rows, w_rows)], load_sem.at[2])
    w_give = pltpu.make_async_remote_copy(
        src_ref=w_hbm,
        dst_ref=w_ref.at[pl.ds(grp * w_rows, w_rows)],
        send_sem=w_sem.at[0],
        recv_sem=w_sem.at[1],
        device_id=(1 - grp, me),
        device_id_type=MESH,
    )
    w_take = pltpu.make_async_remote_copy(
        src_ref=w_hbm,
        dst_ref=w_ref.at[pl.ds((1 - grp) * w_rows, w_rows)],
        send_sem=w_sem.at[0],
        recv_sem=w_sem.at[1],
        device_id=(1 - grp, me),
        device_id_type=MESH,
    )

    list_start(0)
    ring_start(0, 0)
    part_stat[...] = jnp.zeros(part_stat.shape, jnp.float32)
    for home in homes:
        home.wait()
    list_end(0)
    list_start(1)
    ring_end(0, 0)
    ring_start(0, 1)
    list_end(1)
    list_start(2)
    ring_end(0, 1)
    ring_start(0, 2)
    list_end(2)
    firsts, lasts = [], []
    for n in range(2):
        ids = list_ref[:, :, :, n, :].reshape(OWNERS, LANE)
        key = n * 1024 + lax.broadcasted_iota(jnp.int32, (OWNERS, LANE), 1) * 16 + (ids & 15)
        here = (ids >> 4) == me
        firsts.append(jnp.min(jnp.where(here, key, 1 << 20), axis=1, keepdims=True))
        lasts.append(jnp.max(jnp.where(here, key, -1), axis=1, keepdims=True))
    first, last = jnp.minimum(*firsts), jnp.maximum(*lasts)
    code = jnp.where(last < 0, -1, (first >> 10) + ((first & 15) << 1) + ((last & 15) << 5))
    code_ref[...] = jnp.broadcast_to(code, (OWNERS, LANE)).reshape(OWNERS, 1, LANE)
    code_move = pltpu.make_async_copy(code_ref, code_smem, load_sem.at[3])
    code_move.start()
    w_home.start()
    w_give.start()
    for load in loads:
        load.wait()
    code_move.wait()

    row_head = lax.broadcasted_iota(jnp.int32, (GH * QT, GW), 0) // QT
    lane_head = lax.broadcasted_iota(jnp.int32, (GH * QT, GW), 1) // HD
    diag = jnp.where(row_head == lane_head, 0.125, 0.0).astype(jnp.bfloat16)
    stat_lane = lax.broadcasted_iota(jnp.int32, (QT, LANE), 1)
    near = stat_lane < HD

    def tree(sources, targets, g, stage, by):
        return [
            pltpu.make_async_remote_copy(
                src_ref=source,
                dst_ref=target,
                send_sem=tree_send.at[stage, g, by, n],
                recv_sem=tree_recv.at[stage, g, by, n],
                device_id=line[order_of(g)[stage]][by],
                device_id_type=MESH,
            )
            for n, (source, target) in enumerate(zip(sources, targets))
        ]

    def one(g, by):
        return tree(
            (part_ref.at[g, by], part_stat.at[g, by]), (near_ref.at[g, by - 1], near_stat.at[g, by - 1]), g, 0, by
        )

    def two(g, by):
        return tree((mid_ref.at[g, by], mid_stat.at[g]), (next_ref.at[g, by - 1], next_stat.at[g, by - 1]), g, 1, by)

    def three(g, by):
        return tree((late_ref.at[g, by], late_stat.at[g]), (last_ref.at[g, by - 1], last_stat.at[g, by - 1]), g, 2, by)

    def tree_start(stage, g):
        for by in range(1, SIDE):
            for copy in stage(g, by):
                copy.start()

    def tree_wait(stage, g):
        for by in range(1, SIDE):
            for copy in stage(g, by):
                copy.wait_send()
                copy.wait_recv()

    stride = {"y": SIDE * SIDE, "x": SIDE, "z": 1}

    def place(phase, b, n):
        turn, quarter = b >> 2, b & 3
        if phase < 2:
            return quarter, n, turn + (turn >> 1) * (1 - 2 * (turn & 1))
        return (turn + 1) & 3, quarter, n

    def told(phase, b, n, g):
        return code_smem[sum(at * stride[axis] for axis, at in zip(order_of(g), place(phase, b, n))), 0, 0]

    def passages(code):
        code = jnp.maximum(code, 0)
        return code & 1, (code >> 1) & 15, (code >> 5) & 15

    def items_of(phase):
        return [(n, g) for n in range(BATCH) for g in PHASES[phase]]

    def score(phase, b, at):
        n, g = items_of(phase)[at]
        which, first, second = passages(told(phase, b, n, g))
        cols = slice(g * GW, (g + 1) * GW)
        spot = place(phase, b, n)
        q = jnp.where(which > 0, q_ref[(g, *spot, slice(QT, 2 * QT))], q_ref[(g, *spot, slice(0, QT))])
        lhs = jnp.concatenate([q] * GH, axis=0) * diag
        k = jnp.concatenate([k_ref[first, :, cols], k_ref[second, :, cols]], axis=0)
        score_ref[at] = lax.dot_general(lhs, k, (((1,), (1,)), ((), ())), preferred_element_type=jnp.float32)

    def weigh(phase, b, at, packed):
        n, g = items_of(phase)[at]
        code = told(phase, b, n, g)
        which, first, second = passages(code)
        values = score_ref[at]
        peak = jnp.max(values, axis=1, keepdims=True)
        shaped = jnp.exp(values - peak)
        total = jnp.sum(shaped, axis=1, keepdims=True)
        weight_ref[at] = shaped.astype(jnp.bfloat16)
        rows = [slice(h * QT, (h + 1) * QT) for h in range(GH)]
        for t in range(GW // LANE):
            pair = jnp.where(near, total[rows[2 * t]], total[rows[2 * t + 1]])
            inverse_ref[at, :, t * LANE : (t + 1) * LANE] = 1.0 / pair
        lane, peaks, totals, tags = packed[g]
        spot = n * SIDE if phase < 2 else n
        for h in range(GH):
            here = lane == spot * GH + h
            peaks = jnp.where(here, peak[rows[h]], peaks)
            totals = jnp.where(here, total[rows[h]], totals)
        share = jnp.where(first == second, 0.5, 1.0)
        totals = jnp.where((lane >> 2) == spot, totals * share, totals)
        tag = jnp.where(code < 0, -1.0, jnp.where(which > 0, 1.0, 0.0))
        tags = jnp.where(((lane - LANE // 2) >> 2) == spot, tag, tags)
        packed[g] = (lane, peaks, totals, tags)

    def apply(phase, b, at):
        n, g = items_of(phase)[at]
        which, first, second = passages(told(phase, b, n, g))
        cols = slice(g * GW, (g + 1) * GW)
        v = jnp.concatenate([v_ref[first, :, cols], v_ref[second, :, cols]], axis=0)
        full = jnp.dot(weight_ref[at], v, preferred_element_type=jnp.float32)
        for t in range(GW // LANE):
            lanes = slice(t * LANE, (t + 1) * LANE)
            a, c = (slice((2 * t + e) * QT, (2 * t + e + 1) * QT) for e in (0, 1))
            part = jnp.where(near, full[a, lanes], full[c, lanes]) * inverse_ref[at, :, lanes]
            part_ref[(g, *place(phase, b, n), slice(None), lanes)] = part.astype(jnp.bfloat16)

    def pack_open(phase, b):
        first, second, third = place(phase, b, 0)
        lane = stat_lane - (third * GH if phase < 2 else second * GH * SIDE)
        zero = jnp.zeros((QT, LANE), jnp.float32)
        return {g: (lane, zero, zero + 1.0, zero) for g in PHASES[phase]}

    def pack_close(phase, b, packed):
        first, second, third = place(phase, b, 0)
        for g, (lane, peaks, totals, tags) in packed.items():
            if phase < 2:
                mine = (lane & 15) < GH
            else:
                mine = ((stat_lane & 63) >> 4) == second
            value = jnp.where(stat_lane < LANE // 2, peaks + jnp.log(totals), tags)
            part_stat[g, first] = jnp.where(mine, value, part_stat[g, first])

    def attend(phase, b):
        later, latest = jnp.minimum(b + 1, OWNERS // BATCH - 1), jnp.minimum(b + 2, OWNERS // BATCH - 1)
        packed = pack_open(phase, later)
        for at in range(len(items_of(phase))):
            apply(phase, b, at)
            weigh(phase, later, at, packed)
            score(phase, latest, at)
        pack_close(phase, later, packed)

    def prepare(phase):
        for at in range(len(items_of(phase))):
            score(phase, 0, at)
        packed = pack_open(phase, 0)
        for at in range(len(items_of(phase))):
            weigh(phase, 0, at, packed)
            score(phase, 1, at)
        pack_close(phase, 0, packed)

    def widen(share, at, t):
        pair = [jnp.broadcast_to(share[:, c : c + 1], (QT, LANE)) for c in (at + 2 * t, at + 2 * t + 1)]
        return jnp.where(near, pair[0], pair[1])

    def tiles(block):
        return [block[:, t * LANE : (t + 1) * LANE].astype(jnp.float32) for t in range(GW // LANE)]

    def blend(shares, at, blocks):
        sums = []
        for t in range(GW // LANE):
            total = widen(shares[0], at, t) * tiles(blocks[0])[t]
            for d in range(1, SIDE):
                total = total + widen(shares[d], at, t) * tiles(blocks[d])[t]
            sums.append(total)
        return jnp.concatenate(sums, axis=1).astype(jnp.bfloat16)

    def merge_one(g):
        tree_wait(one, g)
        packed = [part_stat[g, 0]] + [near_stat[g, d - 1] for d in range(1, SIDE)]
        tags = [pltpu.roll(stat, LANE // 2, 1) for stat in packed]
        tops = []
        for n in range(2):
            kept = [jnp.where(tag == n, stat, DEAD) for stat, tag in zip(packed, tags)]
            tops.append(jnp.maximum(jnp.maximum(kept[0], kept[1]), jnp.maximum(kept[2], kept[3])))
        terms = [
            jnp.exp(jnp.minimum(stat - jnp.where(tag == 1.0, tops[1], tops[0]), 0.0)) for stat, tag in zip(packed, tags)
        ]
        results, inverses = [], []
        for n in range(2):
            kept = [jnp.where(tag == n, term, 0.0) for term, tag in zip(terms, tags)]
            total = jnp.maximum(kept[0] + kept[1] + kept[2] + kept[3], 1e-30)
            results.append(tops[n] + jnp.log(total))
            inverses.append(1.0 / total)
        mid_stat[g] = jnp.where(stat_lane < LANE // 2, results[0], pltpu.roll(results[1], LANE // 2, 1))
        shares = [
            term * jnp.where(tag == 1.0, -inverses[1], jnp.where(tag == 0.0, inverses[0], 0.0))
            for term, tag in zip(terms, tags)
        ]

        def body(j, carry):
            second, third = j >> 2, j & 3
            blocks = [part_ref[g, 0, second, third]] + [near_ref[g, d - 1, second, third] for d in range(1, SIDE)]
            turned = [pltpu.roll(share, (LANE - GH * j) & (LANE - 1), 1) for share in shares]
            for t in range(GW // LANE):
                totals = [jnp.zeros((QT, LANE), jnp.float32)] * 2
                for d in range(SIDE):
                    factor, block = widen(turned[d], 0, t), tiles(blocks[d])[t]
                    totals = [
                        totals[0] + jnp.maximum(factor, 0.0) * block,
                        totals[1] - jnp.minimum(factor, 0.0) * block,
                    ]
                for n in range(2):
                    mid_ref[g, second, third, n, :, t * LANE : (t + 1) * LANE] = totals[n].astype(jnp.bfloat16)
            return carry

        lax.fori_loop(0, SIDE * SIDE, body, 0, unroll=4)
        tree_start(two, g)

    def shares_of(packed):
        top = jnp.maximum(jnp.maximum(packed[0], packed[1]), jnp.maximum(packed[2], packed[3]))
        terms = [jnp.exp(stat - top) for stat in packed]
        total = terms[0] + terms[1] + terms[2] + terms[3]
        inverse = 1.0 / total
        return top + jnp.log(total), [term * inverse for term in terms]

    def merge_two(g):
        tree_wait(two, g)
        packed = [mid_stat[g]] + [pltpu.roll(next_stat[g, d - 1], LANE - 16 * d, 1) for d in range(1, SIDE)]
        late_stat[g], shares = shares_of(packed)
        for third in range(SIDE):
            for n in range(2):
                blocks = [mid_ref[g, 0, third, n]] + [next_ref[g, d - 1, third, n] for d in range(1, SIDE)]
                late_ref[g, third, n] = blend(shares, n * LANE // 2 + third * GH, blocks)
        tree_start(three, g)

    def merge_three(g):
        tree_wait(three, g)
        packed = [late_stat[g]] + [pltpu.roll(last_stat[g, d - 1], LANE - 4 * d, 1) for d in range(1, SIDE)]
        value, shares = shares_of(packed)
        for n in range(2):
            blocks = [late_ref[g, 0, n]] + [last_ref[g, d - 1, n] for d in range(1, SIDE)]
            attended_ref[n * QT : (n + 1) * QT, g * GW : (g + 1) * GW] = blend(shares, n * LANE // 2, blocks)

    def project(phase):
        rows = slice(PHASES[phase][0] * GW, (PHASES[phase][-1] + 1) * GW)
        product = jnp.dot(attended_ref[:, rows], w_ref[rows, :], preferred_element_type=jnp.float32)
        if phase == 0:
            sum_ref[...] = product
        elif phase == 1:
            sum_ref[...] += product
        else:
            out_ref[...] = (sum_ref[...] + product).astype(jnp.bfloat16)

    def send(phase, *offsets):
        for by in offsets:
            for g in PHASES[phase]:
                for copy in one(g, by):
                    copy.start()

    def run(phase, beside):
        prepare(phase)

        def body(b, carry):
            attend(phase, b)
            for at, acts in beside.items():

                @pl.when(b == at)
                def _():
                    for act, *args in acts:
                        act(*args)

            return carry

        lax.fori_loop(0, OWNERS // BATCH, body, 0)

    def each(merge, phase):
        for g in PHASES[phase]:
            merge(g)

    run(
        0,
        {
            1: [(ring_forward, 0, 2), (ring_start, 1, 0)],
            5: [(ring_end, 1, 0), (ring_start, 1, 1)],
            9: [(ring_end, 0, 2)],
            10: [(ring_end, 1, 1), (ring_start, 1, 2)],
        },
    )
    run(
        1,
        {
            0: [(ring_start, 2, 0)],
            1: [(ring_forward, 1, 2), (send, 0, 2)],
            3: [(send, 0, 1)],
            4: [(ring_end, 2, 0), (ring_start, 2, 1)],
            5: [(send, 0, 3)],
            8: [(ring_end, 2, 1), (ring_start, 2, 2)],
            9: [(ring_end, 1, 2)],
            14: [(ring_forward, 2, 2)],
        },
    )
    send(1, 2, 1, 3)
    each(merge_one, 0)
    ring_end(2, 2)
    run(2, {3: [(send, 2, 1)], 7: [(send, 2, 2)], 10: [(each, merge_two, 0)], 11: [(send, 2, 3)]})
    each(merge_three, 0)
    w_home.wait()
    w_give.wait_send()
    w_take.wait_recv()
    project(0)
    each(merge_one, 1)
    each(merge_one, 2)
    each(merge_two, 1)
    ring_sent()
    for stage in range(3):
        for by in range(1, SIDE):
            list_copy(stage, by).wait_send()
    each(merge_two, 2)
    each(merge_three, 1)
    project(1)
    each(merge_three, 2)
    project(2)


def on_device(queries, keys, values, counts, passage_ids, out_weight):
    leads = (
        (SIDE, SIDE, SIDE),
        (SIDE - 1, SIDE, SIDE),
        (SIDE, SIDE, 2),
        (SIDE - 1, SIDE, 2),
        (SIDE, 2),
        (SIDE - 1, 2),
    )
    blocks = [pltpu.VMEM((GROUPS, SIDE, SIDE, SIDE, 2 * QT, GW), jnp.bfloat16)]
    blocks += [pltpu.VMEM((GROUPS, *lead, QT, GW), jnp.bfloat16) for lead in leads]
    for lead in ((SIDE,), (SIDE - 1,), (), (SIDE - 1,), (), (SIDE - 1,)):
        blocks.append(pltpu.VMEM((GROUPS, *lead, QT, LANE), jnp.float32))
    return pl.pallas_call(
        torus_kernel,
        out_shape=jax.ShapeDtypeStruct((2 * QT, D), jnp.bfloat16),
        in_specs=[pl.BlockSpec(memory_space=pltpu.SMEM)]
        + [pl.BlockSpec(memory_space=pltpu.VMEM)] * 2
        + [pl.BlockSpec(memory_space=pl.ANY)] * 3,
        out_specs=pl.BlockSpec(memory_space=pltpu.VMEM),
        scratch_shapes=blocks
        + [
            pltpu.VMEM(keys.shape, jnp.bfloat16),
            pltpu.VMEM(values.shape, jnp.bfloat16),
            pltpu.VMEM((D, D), jnp.bfloat16),
            pltpu.VMEM((SIDE, SIDE, SIDE, 2, LANE), jnp.int32),
            pltpu.VMEM((OWNERS, 1, LANE), jnp.int32),
            pltpu.SMEM((OWNERS, 1, LANE), jnp.int32),
            pltpu.VMEM((3 * BATCH, GH * QT, 2 * PT), jnp.float32),
            pltpu.VMEM((3 * BATCH, GH * QT, 2 * PT), jnp.bfloat16),
            pltpu.VMEM((3 * BATCH, QT, GW), jnp.float32),
            pltpu.VMEM((2 * QT, D), jnp.bfloat16),
            pltpu.VMEM((2 * QT, D), jnp.float32),
            pltpu.SemaphoreType.DMA((4,)),
            pltpu.SemaphoreType.DMA((GROUPS,)),
            pltpu.SemaphoreType.DMA((3, SIDE)),
            pltpu.SemaphoreType.DMA((3, SIDE)),
            pltpu.SemaphoreType.DMA((2,)),
            pltpu.SemaphoreType.DMA((GROUPS, 3, 4)),
            pltpu.SemaphoreType.DMA((GROUPS, 3, 4)),
            pltpu.SemaphoreType.DMA((3, GROUPS, SIDE, 2)),
            pltpu.SemaphoreType.DMA((3, GROUPS, SIDE, 2)),
        ],
        compiler_params=pltpu.CompilerParams(
            vmem_limit_bytes=60 * 2**20, collective_id=0, has_side_effects=True
        ),
        cost_estimate=pl.CostEstimate(flops=40 * 10**9, bytes_accessed=20 * 2**20, transcendentals=4 * 10**6),
        name="torus",
    )(counts, passage_ids, queries, keys, values, out_weight)


def solution(mesh):
    placed = (
        P(("grp", "dev"), None),
        P(("grp", "dev"), None, None),
        P(("grp", "dev"), None, None),
        P(("grp", "dev")),
        P(("grp", "dev"), None),
        P("grp", None),
    )
    return jax.shard_map(
        on_device, mesh=mesh, in_specs=placed, out_specs=P(("grp", "dev"), None), check_vma=False
    )
```

```python
import jax
import jax.numpy as jnp
from jax import lax
from jax.experimental import pallas as pl
from jax.experimental.pallas import tpu as pltpu
from jax.sharding import PartitionSpec as P

D = 2048
H = 32
HD = 64
QT = 16
PT = 64
GW = 256
GH = GW // HD
GROUPS = D // GW
LANE = 128
SIDE = 4
OWNERS = SIDE * SIDE * SIDE
PHASES = ((0, 1, 2), (3, 4, 5), (6, 7))
BATCH = 4

DEAD = -1e30
ORDERS = (("x", "y", "z"), ("y", "z", "x"), ("z", "x", "y"))
MESH = pl.DeviceIdType.MESH


def torus_kernel(
    counts_ref, ids_ref, mine_ref, k_hbm, v_hbm, w_hbm, out_ref,
    q_ref, part_ref, near_ref, mid_ref, next_ref, late_ref, last_ref,
    part_stat, mid_stat, late_stat,
    k_ref, v_ref, w_ref, list_ref, code_ref, code_smem, score_ref, weight_ref, inverse_ref, attended_ref, sum_ref,
    load_sem, home_sem, list_send, list_recv, w_sem, ring_send, ring_recv, tree_send, tree_recv,
):
    me = lax.axis_index("dev")
    grp = lax.axis_index("grp")
    own = {"y": me >> 4, "x": (me >> 2) & 3, "z": me & 3}
    stride = {"y": SIDE * SIDE, "x": SIDE, "z": 1}
    line = {
        axis: {by: (grp, me + ((((own[axis] + by) & 3) - own[axis]) * stride[axis])) for by in range(1, SIDE)}
        for axis in own
    }
    loads = [
        pltpu.make_async_copy(k_hbm, k_ref, load_sem.at[0]),
        pltpu.make_async_copy(v_hbm, v_ref, load_sem.at[1]),
    ]
    for load in loads:
        load.start()
    barrier = pltpu.get_barrier_semaphore()
    for axis in line:
        for by in line[axis]:
            pl.semaphore_signal(barrier, inc=1, device_id=line[axis][by], device_id_type=MESH)
    pl.semaphore_signal(barrier, inc=1, device_id=(1 - grp, me), device_id_type=MESH)
    homes = [
        pltpu.make_async_copy(mine_ref.at[:, pl.ds(g * GW, GW)], q_ref.at[g, 0, 0, 0], home_sem.at[g])
        for g in range(GROUPS)
    ]
    for home in homes:
        home.start()
    list_len = ids_ref.shape[1]
    place = lax.broadcasted_iota(jnp.int32, (2, list_len), 1)
    row = lax.broadcasted_iota(jnp.int32, (2, list_len), 0)
    live = place < jnp.where(row == 0, counts_ref[0], counts_ref[1])
    list_ref[0, 0, 0] = jnp.full((2, LANE), -1, jnp.int32)
    list_ref[0, 0, 0, :, :list_len] = jnp.where(live, ids_ref[...], -1)
    pl.semaphore_wait(barrier, 10)

    whole, lower, upper = (0, 2 * QT), (0, QT), (QT, QT)
    both = ((0, 1, 3, lower), (1, 3, 1, upper))
    straight = both + ((2, 2, 2, whole),)

    def sends(stage):
        return both if stage == 2 else straight

    def order_of(g):
        return ORDERS[g % 3]

    def ring_block(g, stage, at, rows):
        spot = [pl.ds(0, SIDE) if n < stage else at if n == stage else 0 for n in range(3)]
        return q_ref.at[g, spot[0], spot[1], spot[2], pl.ds(*rows), :]

    def ring_own(g, stage, kind, by, at):
        source = ring_block(g, stage, 0, whole) if stage else mine_ref.at[:, pl.ds(g * GW, GW)]
        return pltpu.make_async_remote_copy(
            src_ref=source,
            dst_ref=ring_block(g, stage, at, whole),
            send_sem=ring_send.at[g, stage],
            recv_sem=ring_recv.at[g, stage + kind if stage == 2 else stage],
            device_id=line[order_of(g)[stage]][by],
            device_id_type=MESH,
        )

    def ring_pass(g, stage, kind, by, at, rows):
        return pltpu.make_async_remote_copy(
            src_ref=ring_block(g, stage, at, rows),
            dst_ref=ring_block(g, stage, 2, rows),
            send_sem=ring_send.at[g, stage],
            recv_sem=ring_recv.at[g, 4],
            device_id=line[order_of(g)[stage]][by],
            device_id_type=MESH,
        )

    def ring_start(phase, stage):
        for g in PHASES[phase]:
            for kind, by, at, rows in sends(stage):
                ring_own(g, stage, kind, by, at).start()

    def ring_forward(phase, stage):
        for kind, by, at, rows in both:
            for g in PHASES[phase]:
                taken(ring_block(g, stage, at, whole), ring_recv.at[g, stage + kind])
                ring_pass(g, stage, kind, by, at, rows).start()

    def taken(ref, sem):
        pltpu.make_async_copy(ref, ref, sem).wait()

    def ring_all(g, stage):
        spot = [pl.ds(0, SIDE) if n < stage else pl.ds(1, 3) if n == stage else 0 for n in range(3)]
        return q_ref.at[g, spot[0], spot[1], spot[2]]

    def ring_end(phase, stage):
        for g in PHASES[phase]:
            if stage == 2:
                taken(ring_block(g, stage, 2, whole), ring_recv.at[g, 4])
            else:
                taken(ring_all(g, stage), ring_recv.at[g, stage])

    def ring_sent():
        for g in range(GROUPS):
            for stage in range(3):
                taken(ring_all(g, stage), ring_send.at[g, stage])

    def list_copy(stage, by):
        order = ("x", "y", "z")
        spot = {axis: 0 for axis in order}
        for axis in order[:stage]:
            spot[axis] = pl.ds(0, SIDE)
        source = list_ref.at[spot["y"], spot["x"], spot["z"]]
        spot[order[stage]] = SIDE - by
        return pltpu.make_async_remote_copy(
            src_ref=source,
            dst_ref=list_ref.at[spot["y"], spot["x"], spot["z"]],
            send_sem=list_send.at[stage, by],
            recv_sem=list_recv.at[stage, by],
            device_id=line[order[stage]][by],
            device_id_type=MESH,
        )

    def list_start(stage):
        for by in range(1, SIDE):
            list_copy(stage, by).start()

    def list_end(stage):
        for by in range(1, SIDE):
            list_copy(stage, by).wait_recv()

    w_rows = D // 2
    w_home = pltpu.make_async_copy(w_hbm, w_ref.at[pl.ds(grp * w_rows, w_rows)], load_sem.at[2])
    w_give = pltpu.make_async_remote_copy(
        src_ref=w_hbm,
        dst_ref=w_ref.at[pl.ds(grp * w_rows, w_rows)],
        send_sem=w_sem.at[0],
        recv_sem=w_sem.at[1],
        device_id=(1 - grp, me),
        device_id_type=MESH,
    )
    w_take = pltpu.make_async_remote_copy(
        src_ref=w_hbm,
        dst_ref=w_ref.at[pl.ds((1 - grp) * w_rows, w_rows)],
        send_sem=w_sem.at[0],
        recv_sem=w_sem.at[1],
        device_id=(1 - grp, me),
        device_id_type=MESH,
    )

    list_start(0)
    ring_start(0, 0)
    part_stat[...] = jnp.zeros(part_stat.shape, jnp.float32)
    for home in homes:
        home.wait()
    list_end(0)
    list_start(1)
    ring_end(0, 0)
    ring_start(0, 1)
    list_end(1)
    list_start(2)
    ring_end(0, 1)
    ring_start(0, 2)
    list_end(2)
    firsts, lasts = [], []
    for n in range(2):
        ids = list_ref[:, :, :, n, :].reshape(OWNERS, LANE)
        key = n * 1024 + lax.broadcasted_iota(jnp.int32, (OWNERS, LANE), 1) * 16 + (ids & 15)
        here = (ids >> 4) == me
        firsts.append(jnp.min(jnp.where(here, key, 1 << 20), axis=1, keepdims=True))
        lasts.append(jnp.max(jnp.where(here, key, -1), axis=1, keepdims=True))
    first, last = jnp.minimum(*firsts), jnp.maximum(*lasts)
    code = jnp.where(last < 0, -1, (first >> 10) + ((first & 15) << 1) + ((last & 15) << 5))
    code_ref[...] = jnp.broadcast_to(code, (OWNERS, LANE)).reshape(OWNERS, 1, LANE)
    code_move = pltpu.make_async_copy(code_ref, code_smem, load_sem.at[3])
    code_move.start()
    w_home.start()
    w_give.start()
    for load in loads:
        load.wait()
    code_move.wait()

    row_head = lax.broadcasted_iota(jnp.int32, (GH * QT, GW), 0) // QT
    lane_head = lax.broadcasted_iota(jnp.int32, (GH * QT, GW), 1) // HD
    diag = jnp.where(row_head == lane_head, 0.125, 0.0).astype(jnp.bfloat16)
    stat_lane = lax.broadcasted_iota(jnp.int32, (QT, LANE), 1)
    near = stat_lane < HD

    trees = ((part_ref, near_ref), (mid_ref, next_ref), (late_ref, last_ref))

    def tree_start(stage, g, by):
        source, target = trees[stage]
        pltpu.make_async_remote_copy(
            src_ref=source.at[g, by],
            dst_ref=target.at[g, by - 1],
            send_sem=tree_send.at[stage, g],
            recv_sem=tree_recv.at[stage, g],
            device_id=line[order_of(g)[stage]][by],
            device_id_type=MESH,
        ).start()

    def tree_wait(stage, g):
        target = trees[stage][1]
        taken(target.at[g], tree_send.at[stage, g])
        taken(target.at[g], tree_recv.at[stage, g])

    def put_stat(ref, g, by, value):
        high = value.astype(jnp.bfloat16).astype(jnp.float32)
        rest = value - high
        middle = rest.astype(jnp.bfloat16).astype(jnp.float32)
        blocks = ref.shape[2] - 2
        ref[g, by, blocks] = jnp.concatenate([high, middle], axis=1).astype(jnp.bfloat16)
        ref[g, by, blocks + 1] = jnp.concatenate([rest - middle, jnp.zeros_like(high)], axis=1).astype(jnp.bfloat16)

    def get_stat(ref, g, d):
        blocks = ref.shape[2] - 2
        first = ref[g, d - 1, blocks].astype(jnp.float32)
        return first[:, :LANE] + first[:, LANE:] + ref[g, d - 1, blocks + 1, :, :LANE].astype(jnp.float32)

    stride = {"y": SIDE * SIDE, "x": SIDE, "z": 1}

    def place(phase, b, n):
        turn, quarter = b >> 2, b & 3
        if phase < 2:
            return quarter, n, turn + (turn >> 1) * (1 - 2 * (turn & 1))
        return (turn + 1) & 3, quarter, n

    def block_of(g, spot):
        return g, spot[0], spot[1] * SIDE + spot[2]

    def told(phase, b, n, g):
        return code_smem[sum(at * stride[axis] for axis, at in zip(order_of(g), place(phase, b, n))), 0, 0]

    def passages(code):
        code = jnp.maximum(code, 0)
        return code & 1, (code >> 1) & 15, (code >> 5) & 15

    def items_of(phase):
        return [(n, g) for n in range(BATCH) for g in PHASES[phase]]

    def score(phase, b, at):
        n, g = items_of(phase)[at]
        which, first, second = passages(told(phase, b, n, g))
        cols = slice(g * GW, (g + 1) * GW)
        spot = place(phase, b, n)
        q = jnp.where(which > 0, q_ref[(g, *spot, slice(QT, 2 * QT))], q_ref[(g, *spot, slice(0, QT))])
        lhs = jnp.concatenate([q] * GH, axis=0) * diag
        k = jnp.concatenate([k_ref[first, :, cols], k_ref[second, :, cols]], axis=0)
        score_ref[at] = lax.dot_general(lhs, k, (((1,), (1,)), ((), ())), preferred_element_type=jnp.float32)

    def weigh(phase, b, at, packed):
        n, g = items_of(phase)[at]
        code = told(phase, b, n, g)
        which, first, second = passages(code)
        values = score_ref[at]
        peak = jnp.max(values, axis=1, keepdims=True)
        shaped = jnp.exp(values - peak)
        total = jnp.sum(shaped, axis=1, keepdims=True)
        weight_ref[at] = shaped.astype(jnp.bfloat16)
        rows = [slice(h * QT, (h + 1) * QT) for h in range(GH)]
        for t in range(GW // LANE):
            pair = jnp.where(near, total[rows[2 * t]], total[rows[2 * t + 1]])
            inverse_ref[at, :, t * LANE : (t + 1) * LANE] = 1.0 / pair
        lane, peaks, totals, tags = packed[g]
        spot = n * SIDE if phase < 2 else n
        for h in range(GH):
            here = lane == spot * GH + h
            peaks = jnp.where(here, peak[rows[h]], peaks)
            totals = jnp.where(here, total[rows[h]], totals)
        share = jnp.where(first == second, 0.5, 1.0)
        totals = jnp.where((lane >> 2) == spot, totals * share, totals)
        tag = jnp.where(code < 0, -1.0, jnp.where(which > 0, 1.0, 0.0))
        tags = jnp.where(((lane - LANE // 2) >> 2) == spot, tag, tags)
        packed[g] = (lane, peaks, totals, tags)

    def apply(phase, b, at):
        n, g = items_of(phase)[at]
        which, first, second = passages(told(phase, b, n, g))
        cols = slice(g * GW, (g + 1) * GW)
        v = jnp.concatenate([v_ref[first, :, cols], v_ref[second, :, cols]], axis=0)
        full = jnp.dot(weight_ref[at], v, preferred_element_type=jnp.float32)
        for t in range(GW // LANE):
            lanes = slice(t * LANE, (t + 1) * LANE)
            a, c = (slice((2 * t + e) * QT, (2 * t + e + 1) * QT) for e in (0, 1))
            part = jnp.where(near, full[a, lanes], full[c, lanes]) * inverse_ref[at, :, lanes]
            part_ref[(*block_of(g, place(phase, b, n)), slice(None), lanes)] = part.astype(jnp.bfloat16)

    def pack_open(phase, b):
        first, second, third = place(phase, b, 0)
        lane = stat_lane - (third * GH if phase < 2 else second * GH * SIDE)
        zero = jnp.zeros((QT, LANE), jnp.float32)
        return {g: (lane, zero, zero + 1.0, zero) for g in PHASES[phase]}

    def pack_close(phase, b, packed):
        first, second, third = place(phase, b, 0)
        for g, (lane, peaks, totals, tags) in packed.items():
            if phase < 2:
                mine = (lane & 15) < GH
            else:
                mine = ((stat_lane & 63) >> 4) == second
            value = jnp.where(stat_lane < LANE // 2, peaks + jnp.log(totals), tags)
            part_stat[g, first] = jnp.where(mine, value, part_stat[g, first])

    def attend(phase, b):
        later, latest = jnp.minimum(b + 1, OWNERS // BATCH - 1), jnp.minimum(b + 2, OWNERS // BATCH - 1)
        packed = pack_open(phase, later)
        for at in range(len(items_of(phase))):
            apply(phase, b, at)
            weigh(phase, later, at, packed)
            score(phase, latest, at)
        pack_close(phase, later, packed)

    def prepare(phase):
        for at in range(len(items_of(phase))):
            score(phase, 0, at)
        packed = pack_open(phase, 0)
        for at in range(len(items_of(phase))):
            weigh(phase, 0, at, packed)
            score(phase, 1, at)
        pack_close(phase, 0, packed)

    def widen(share, at, t):
        pair = [jnp.broadcast_to(share[:, c : c + 1], (QT, LANE)) for c in (at + 2 * t, at + 2 * t + 1)]
        return jnp.where(near, pair[0], pair[1])

    def tiles(block):
        return [block[:, t * LANE : (t + 1) * LANE].astype(jnp.float32) for t in range(GW // LANE)]

    def blend(shares, at, blocks):
        sums = []
        for t in range(GW // LANE):
            total = widen(shares[0], at, t) * tiles(blocks[0])[t]
            for d in range(1, SIDE):
                total = total + widen(shares[d], at, t) * tiles(blocks[d])[t]
            sums.append(total)
        return jnp.concatenate(sums, axis=1).astype(jnp.bfloat16)

    def merge_one(g):
        tree_wait(0, g)
        packed = [part_stat[g, 0]] + [get_stat(near_ref, g, d) for d in range(1, SIDE)]
        tags = [pltpu.roll(stat, LANE // 2, 1) for stat in packed]
        tops = []
        for n in range(2):
            kept = [jnp.where(tag == n, stat, DEAD) for stat, tag in zip(packed, tags)]
            tops.append(jnp.maximum(jnp.maximum(kept[0], kept[1]), jnp.maximum(kept[2], kept[3])))
        terms = [
            jnp.exp(jnp.minimum(stat - jnp.where(tag == 1.0, tops[1], tops[0]), 0.0)) for stat, tag in zip(packed, tags)
        ]
        results, inverses = [], []
        for n in range(2):
            kept = [jnp.where(tag == n, term, 0.0) for term, tag in zip(terms, tags)]
            total = jnp.maximum(kept[0] + kept[1] + kept[2] + kept[3], 1e-30)
            results.append(tops[n] + jnp.log(total))
            inverses.append(1.0 / total)
        stat = jnp.where(stat_lane < LANE // 2, results[0], pltpu.roll(results[1], LANE // 2, 1))
        shares = [
            term * jnp.where(tag == 1.0, -inverses[1], jnp.where(tag == 0.0, inverses[0], 0.0))
            for term, tag in zip(terms, tags)
        ]

        def body(j, carry):
            second, third = j >> 2, j & 3
            blocks = [part_ref[g, 0, j]] + [near_ref[g, d - 1, j] for d in range(1, SIDE)]
            turned = [pltpu.roll(share, (LANE - GH * j) & (LANE - 1), 1) for share in shares]
            for t in range(GW // LANE):
                totals = [jnp.zeros((QT, LANE), jnp.float32)] * 2
                for d in range(SIDE):
                    factor, block = widen(turned[d], 0, t), tiles(blocks[d])[t]
                    totals = [
                        totals[0] + jnp.maximum(factor, 0.0) * block,
                        totals[1] - jnp.minimum(factor, 0.0) * block,
                    ]
                for n in range(2):
                    mid_ref[g, second, third * 2 + n, :, t * LANE : (t + 1) * LANE] = totals[n].astype(jnp.bfloat16)
            return carry

        lax.fori_loop(0, SIDE * SIDE, body, 0, unroll=4)
        mid_stat[g] = stat
        for by in range(1, SIDE):
            put_stat(mid_ref, g, by, stat)
            tree_start(1, g, by)

    def shares_of(packed):
        top = jnp.maximum(jnp.maximum(packed[0], packed[1]), jnp.maximum(packed[2], packed[3]))
        terms = [jnp.exp(stat - top) for stat in packed]
        total = terms[0] + terms[1] + terms[2] + terms[3]
        inverse = 1.0 / total
        return top + jnp.log(total), [term * inverse for term in terms]

    def merge_two(g):
        tree_wait(1, g)
        packed = [mid_stat[g]] + [pltpu.roll(get_stat(next_ref, g, d), LANE - 16 * d, 1) for d in range(1, SIDE)]
        stat, shares = shares_of(packed)
        for third in range(SIDE):
            for n in range(2):
                blocks = [mid_ref[g, 0, third * 2 + n]] + [next_ref[g, d - 1, third * 2 + n] for d in range(1, SIDE)]
                late_ref[g, third, n] = blend(shares, n * LANE // 2 + third * GH, blocks)
        late_stat[g] = stat
        for by in range(1, SIDE):
            put_stat(late_ref, g, by, stat)
            tree_start(2, g, by)

    def merge_three(g):
        tree_wait(2, g)
        packed = [late_stat[g]] + [pltpu.roll(get_stat(last_ref, g, d), LANE - 4 * d, 1) for d in range(1, SIDE)]
        value, shares = shares_of(packed)
        for n in range(2):
            blocks = [late_ref[g, 0, n]] + [last_ref[g, d - 1, n] for d in range(1, SIDE)]
            attended_ref[n * QT : (n + 1) * QT, g * GW : (g + 1) * GW] = blend(shares, n * LANE // 2, blocks)

    def project(phase):
        rows = slice(PHASES[phase][0] * GW, (PHASES[phase][-1] + 1) * GW)
        product = jnp.dot(attended_ref[:, rows], w_ref[rows, :], preferred_element_type=jnp.float32)
        if phase == 0:
            sum_ref[...] = product
        elif phase == 1:
            sum_ref[...] += product
        else:
            out_ref[...] = (sum_ref[...] + product).astype(jnp.bfloat16)

    def send(phase, *offsets):
        for by in offsets:
            for g in PHASES[phase]:
                put_stat(part_ref, g, by, part_stat[g, by])
                tree_start(0, g, by)

    def run(phase, beside):
        prepare(phase)

        def body(b, carry):
            attend(phase, b)
            for at, acts in beside.items():

                @pl.when(b == at)
                def _():
                    for act, *args in acts:
                        act(*args)

            return carry

        lax.fori_loop(0, OWNERS // BATCH, body, 0)

    def each(merge, phase):
        for g in PHASES[phase]:
            merge(g)

    run(
        0,
        {
            1: [(ring_forward, 0, 2), (ring_start, 1, 0)],
            5: [(ring_end, 1, 0), (ring_start, 1, 1)],
            9: [(ring_end, 0, 2)],
            10: [(ring_end, 1, 1), (ring_start, 1, 2)],
        },
    )
    send(0, 2, 1, 3)
    run(
        1,
        {
            0: [(ring_start, 2, 0)],
            1: [(ring_forward, 1, 2)],
            4: [(ring_end, 2, 0), (ring_start, 2, 1)],
            8: [(ring_end, 2, 1), (ring_start, 2, 2)],
            9: [(ring_end, 1, 2)],
            14: [(ring_forward, 2, 2)],
        },
    )
    send(1, 2, 1, 3)
    each(merge_one, 0)
    ring_end(2, 2)
    run(2, {3: [(send, 2, 1)], 7: [(send, 2, 2)], 11: [(send, 2, 3)]})
    each(merge_two, 0)
    each(merge_one, 1)
    each(merge_one, 2)
    each(merge_two, 1)
    each(merge_three, 0)
    w_home.wait()
    w_give.wait_send()
    w_take.wait_recv()
    project(0)
    each(merge_two, 2)
    each(merge_three, 1)
    project(1)
    ring_sent()
    for stage in range(3):
        for by in range(1, SIDE):
            list_copy(stage, by).wait_send()
    each(merge_three, 2)
    project(2)


def on_device(queries, keys, values, counts, passage_ids, out_weight):
    blocks = [pltpu.VMEM((GROUPS, SIDE, SIDE, SIDE, 2 * QT, GW), jnp.bfloat16)]
    for count in (SIDE * SIDE, 2 * SIDE, 2):
        for lead in (SIDE, SIDE - 1):
            blocks.append(pltpu.VMEM((GROUPS, lead, count + 2, QT, GW), jnp.bfloat16))
    for lead in ((SIDE,), (), ()):
        blocks.append(pltpu.VMEM((GROUPS, *lead, QT, LANE), jnp.float32))
    return pl.pallas_call(
        torus_kernel,
        out_shape=jax.ShapeDtypeStruct((2 * QT, D), jnp.bfloat16),
        in_specs=[pl.BlockSpec(memory_space=pltpu.SMEM)]
        + [pl.BlockSpec(memory_space=pltpu.VMEM)] * 2
        + [pl.BlockSpec(memory_space=pl.ANY)] * 3,
        out_specs=pl.BlockSpec(memory_space=pltpu.VMEM),
        scratch_shapes=blocks
        + [
            pltpu.VMEM(keys.shape, jnp.bfloat16),
            pltpu.VMEM(values.shape, jnp.bfloat16),
            pltpu.VMEM((D, D), jnp.bfloat16),
            pltpu.VMEM((SIDE, SIDE, SIDE, 2, LANE), jnp.int32),
            pltpu.VMEM((OWNERS, 1, LANE), jnp.int32),
            pltpu.SMEM((OWNERS, 1, LANE), jnp.int32),
            pltpu.VMEM((3 * BATCH, GH * QT, 2 * PT), jnp.float32),
            pltpu.VMEM((3 * BATCH, GH * QT, 2 * PT), jnp.bfloat16),
            pltpu.VMEM((3 * BATCH, QT, GW), jnp.float32),
            pltpu.VMEM((2 * QT, D), jnp.bfloat16),
            pltpu.VMEM((2 * QT, D), jnp.float32),
            pltpu.SemaphoreType.DMA((4,)),
            pltpu.SemaphoreType.DMA((GROUPS,)),
            pltpu.SemaphoreType.DMA((3, SIDE)),
            pltpu.SemaphoreType.DMA((3, SIDE)),
            pltpu.SemaphoreType.DMA((2,)),
            pltpu.SemaphoreType.DMA((GROUPS, 3)),
            pltpu.SemaphoreType.DMA((GROUPS, 5)),
            pltpu.SemaphoreType.DMA((3, GROUPS)),
            pltpu.SemaphoreType.DMA((3, GROUPS)),
        ],
        compiler_params=pltpu.CompilerParams(
            vmem_limit_bytes=60 * 2**20, collective_id=0, has_side_effects=True
        ),
        cost_estimate=pl.CostEstimate(flops=40 * 10**9, bytes_accessed=20 * 2**20, transcendentals=4 * 10**6),
        name="torus",
    )(counts, passage_ids, queries, keys, values, out_weight)


def solution(mesh):
    placed = (
        P(("grp", "dev"), None),
        P(("grp", "dev"), None, None),
        P(("grp", "dev"), None, None),
        P(("grp", "dev")),
        P(("grp", "dev"), None),
        P("grp", None),
    )
    return jax.shard_map(
        on_device, mesh=mesh, in_specs=placed, out_specs=P(("grp", "dev"), None), check_vma=False
    )
```

```python
import jax
import jax.numpy as jnp
from jax import lax
from jax.experimental import pallas as pl
from jax.experimental.pallas import tpu as pltpu
from jax.sharding import PartitionSpec as P

D = 2048
H = 32
HD = 64
QT = 16
PT = 64
GW = 256
GH = GW // HD
GROUPS = D // GW
LANE = 128
SIDE = 4
OWNERS = SIDE * SIDE * SIDE
PHASES = ((0, 1, 2), (3, 4, 5), (6, 7))
BATCH = 4

DEAD = -1e30
ORDERS = (("x", "y", "z"), ("y", "z", "x"), ("z", "x", "y"))
MESH = pl.DeviceIdType.MESH


def torus_kernel(
    counts_ref, ids_ref, mine_ref, k_hbm, v_hbm, w_hbm, out_ref,
    q_ref, part_ref, near_ref, mid_ref, next_ref, late_ref, last_ref,
    part_stat, mid_stat, late_stat,
    k_ref, v_ref, w_ref, list_ref, code_ref, code_smem, score_ref, weight_ref, inverse_ref, attended_ref, sum_ref,
    load_sem, list_send, list_recv, w_sem, early_send, early_recv, ring_send, ring_recv, tree_send, tree_recv,
):
    me = lax.axis_index("dev")
    grp = lax.axis_index("grp")
    own = {"y": me >> 4, "x": (me >> 2) & 3, "z": me & 3}
    stride = {"y": SIDE * SIDE, "x": SIDE, "z": 1}
    line = {
        axis: {by: (grp, me + ((((own[axis] + by) & 3) - own[axis]) * stride[axis])) for by in range(1, SIDE)}
        for axis in own
    }
    loads = [
        pltpu.make_async_copy(k_hbm, k_ref, load_sem.at[0]),
        pltpu.make_async_copy(v_hbm, v_ref, load_sem.at[1]),
    ]
    for load in loads:
        load.start()
    barrier = pltpu.get_barrier_semaphore()
    for axis in line:
        for by in line[axis]:
            pl.semaphore_signal(barrier, inc=1, device_id=line[axis][by], device_id_type=MESH)
    pl.semaphore_signal(barrier, inc=1, device_id=(1 - grp, me), device_id_type=MESH)
    for g in range(GROUPS):
        q_ref[g % 3, g // 3, 0, 0, 0] = mine_ref[:, g * GW : (g + 1) * GW]
    list_len = ids_ref.shape[1]
    place = lax.broadcasted_iota(jnp.int32, (2, list_len), 1)
    row = lax.broadcasted_iota(jnp.int32, (2, list_len), 0)
    live = place < jnp.where(row == 0, counts_ref[0], counts_ref[1])
    list_ref[0, 0, 0] = jnp.full((2, LANE), -1, jnp.int32)
    list_ref[0, 0, 0, :, :list_len] = jnp.where(live, ids_ref[...], -1)
    pl.semaphore_wait(barrier, 10)

    whole, lower, upper = (0, 2 * QT), (0, QT), (QT, QT)
    both = ((0, 1, 3, lower), (1, 3, 1, upper))
    def order_of(g):
        return ORDERS[g % 3]

    def taken(ref, sem):
        pltpu.make_async_copy(ref, ref, sem).wait()

    def early_part(step, k, at):
        count = len(range(k, GROUPS, 3))
        if step == 0:
            return q_ref.at[k, pl.ds(0, count), at, 0, 0]
        which = pl.ds(0, 1) if step == 1 else pl.ds(1, count - 1)
        return q_ref.at[k, which, :, at, 0]

    def early_start(step):
        for k in range(3):
            for by in range(1, SIDE):
                pltpu.make_async_remote_copy(
                    src_ref=early_part(step, k, 0),
                    dst_ref=early_part(step, k, SIDE - by),
                    send_sem=early_send.at[k, step],
                    recv_sem=early_recv.at[k, step],
                    device_id=line[ORDERS[k][min(step, 1)]][by],
                    device_id_type=MESH,
                ).start()

    def early_end(step, sem):
        for k in range(3):
            taken(early_part(step, k, pl.ds(1, 3)), sem.at[k, step])

    def ring_block(g, at, rows):
        return q_ref.at[g % 3, g // 3, :, :, at, pl.ds(*rows), :]

    def ring_start(phase):
        for g in PHASES[phase]:
            for kind, by, at, rows in both:
                pltpu.make_async_remote_copy(
                    src_ref=ring_block(g, 0, whole),
                    dst_ref=ring_block(g, at, whole),
                    send_sem=ring_send.at[g],
                    recv_sem=ring_recv.at[g, kind],
                    device_id=line[order_of(g)[2]][by],
                    device_id_type=MESH,
                ).start()

    def ring_forward(phase):
        for kind, by, at, rows in both:
            for g in PHASES[phase]:
                taken(ring_block(g, at, whole), ring_recv.at[g, kind])
                pltpu.make_async_remote_copy(
                    src_ref=ring_block(g, at, rows),
                    dst_ref=ring_block(g, 2, rows),
                    send_sem=ring_send.at[g],
                    recv_sem=ring_recv.at[g, 2],
                    device_id=line[order_of(g)[2]][by],
                    device_id_type=MESH,
                ).start()

    def ring_end(phase):
        for g in PHASES[phase]:
            taken(ring_block(g, 2, whole), ring_recv.at[g, 2])

    def ring_sent():
        for step in range(3):
            early_end(step, early_send)
        for g in range(GROUPS):
            taken(q_ref.at[g % 3, g // 3, :, :, pl.ds(1, 3)], ring_send.at[g])

    def list_copy(stage, by):
        order = ("x", "y", "z")
        spot = {axis: 0 for axis in order}
        for axis in order[:stage]:
            spot[axis] = pl.ds(0, SIDE)
        source = list_ref.at[spot["y"], spot["x"], spot["z"]]
        spot[order[stage]] = SIDE - by
        return pltpu.make_async_remote_copy(
            src_ref=source,
            dst_ref=list_ref.at[spot["y"], spot["x"], spot["z"]],
            send_sem=list_send.at[stage, by],
            recv_sem=list_recv.at[stage, by],
            device_id=line[order[stage]][by],
            device_id_type=MESH,
        )

    def list_start(stage):
        for by in range(1, SIDE):
            list_copy(stage, by).start()

    def list_end(stage):
        for by in range(1, SIDE):
            list_copy(stage, by).wait_recv()

    w_rows = D // 2
    w_home = pltpu.make_async_copy(w_hbm, w_ref.at[pl.ds(grp * w_rows, w_rows)], load_sem.at[2])
    w_give = pltpu.make_async_remote_copy(
        src_ref=w_hbm,
        dst_ref=w_ref.at[pl.ds(grp * w_rows, w_rows)],
        send_sem=w_sem.at[0],
        recv_sem=w_sem.at[1],
        device_id=(1 - grp, me),
        device_id_type=MESH,
    )
    w_take = pltpu.make_async_remote_copy(
        src_ref=w_hbm,
        dst_ref=w_ref.at[pl.ds((1 - grp) * w_rows, w_rows)],
        send_sem=w_sem.at[0],
        recv_sem=w_sem.at[1],
        device_id=(1 - grp, me),
        device_id_type=MESH,
    )

    list_start(0)
    early_start(0)
    part_stat[...] = jnp.zeros(part_stat.shape, jnp.float32)
    list_end(0)
    list_start(1)
    early_end(0, early_recv)
    early_start(1)
    list_end(1)
    list_start(2)
    early_end(1, early_recv)
    ring_start(0)
    early_start(2)
    list_end(2)
    firsts, lasts = [], []
    for n in range(2):
        ids = list_ref[:, :, :, n, :].reshape(OWNERS, LANE)
        key = n * 1024 + lax.broadcasted_iota(jnp.int32, (OWNERS, LANE), 1) * 16 + (ids & 15)
        here = (ids >> 4) == me
        firsts.append(jnp.min(jnp.where(here, key, 1 << 20), axis=1, keepdims=True))
        lasts.append(jnp.max(jnp.where(here, key, -1), axis=1, keepdims=True))
    first, last = jnp.minimum(*firsts), jnp.maximum(*lasts)
    code = jnp.where(last < 0, -1, (first >> 10) + ((first & 15) << 1) + ((last & 15) << 5))
    code_ref[...] = jnp.broadcast_to(code, (OWNERS, LANE)).reshape(OWNERS, 1, LANE)
    code_move = pltpu.make_async_copy(code_ref, code_smem, load_sem.at[3])
    code_move.start()
    w_home.start()
    w_give.start()
    for load in loads:
        load.wait()
    code_move.wait()

    row_head = lax.broadcasted_iota(jnp.int32, (GH * QT, GW), 0) // QT
    lane_head = lax.broadcasted_iota(jnp.int32, (GH * QT, GW), 1) // HD
    diag = jnp.where(row_head == lane_head, 0.125, 0.0).astype(jnp.bfloat16)
    stat_lane = lax.broadcasted_iota(jnp.int32, (QT, LANE), 1)
    near = stat_lane < HD

    trees = ((part_ref, near_ref), (mid_ref, next_ref), (late_ref, last_ref))

    def tree_start(stage, g, by):
        source, target = trees[stage]
        pltpu.make_async_remote_copy(
            src_ref=source.at[g, by],
            dst_ref=target.at[g, by - 1],
            send_sem=tree_send.at[stage, g],
            recv_sem=tree_recv.at[stage, g],
            device_id=line[order_of(g)[stage]][by],
            device_id_type=MESH,
        ).start()

    def tree_wait(stage, g):
        target = trees[stage][1]
        taken(target.at[g], tree_send.at[stage, g])
        taken(target.at[g], tree_recv.at[stage, g])

    def put_stat(ref, g, by, value):
        high = value.astype(jnp.bfloat16).astype(jnp.float32)
        rest = value - high
        middle = rest.astype(jnp.bfloat16).astype(jnp.float32)
        blocks = ref.shape[2] - 2
        ref[g, by, blocks] = jnp.concatenate([high, middle], axis=1).astype(jnp.bfloat16)
        ref[g, by, blocks + 1] = jnp.concatenate([rest - middle, jnp.zeros_like(high)], axis=1).astype(jnp.bfloat16)

    def get_stat(ref, g, d):
        blocks = ref.shape[2] - 2
        first = ref[g, d - 1, blocks].astype(jnp.float32)
        return first[:, :LANE] + first[:, LANE:] + ref[g, d - 1, blocks + 1, :, :LANE].astype(jnp.float32)

    stride = {"y": SIDE * SIDE, "x": SIDE, "z": 1}

    def place(phase, b, n):
        turn, quarter = b >> 2, b & 3
        if phase < 2:
            return quarter, n, turn + (turn >> 1) * (1 - 2 * (turn & 1))
        return (turn + 1) & 3, quarter, n

    def block_of(g, spot):
        return g, spot[0], spot[1] * SIDE + spot[2]

    def told(phase, b, n, g):
        return code_smem[sum(at * stride[axis] for axis, at in zip(order_of(g), place(phase, b, n))), 0, 0]

    def passages(code):
        code = jnp.maximum(code, 0)
        return code & 1, (code >> 1) & 15, (code >> 5) & 15

    def items_of(phase):
        return [(n, g) for n in range(BATCH) for g in PHASES[phase]]

    def score(phase, b, at):
        n, g = items_of(phase)[at]
        which, first, second = passages(told(phase, b, n, g))
        cols = slice(g * GW, (g + 1) * GW)
        spot = place(phase, b, n)
        q = jnp.where(which > 0, q_ref[(g % 3, g // 3, *spot, slice(QT, 2 * QT))], q_ref[(g % 3, g // 3, *spot, slice(0, QT))])
        lhs = jnp.concatenate([q] * GH, axis=0) * diag
        k = jnp.concatenate([k_ref[first, :, cols], k_ref[second, :, cols]], axis=0)
        score_ref[at] = lax.dot_general(lhs, k, (((1,), (1,)), ((), ())), preferred_element_type=jnp.float32)

    def weigh(phase, b, at, packed):
        n, g = items_of(phase)[at]
        code = told(phase, b, n, g)
        which, first, second = passages(code)
        values = score_ref[at]
        peak = jnp.max(values, axis=1, keepdims=True)
        shaped = jnp.exp(values - peak)
        total = jnp.sum(shaped, axis=1, keepdims=True)
        weight_ref[at] = shaped.astype(jnp.bfloat16)
        rows = [slice(h * QT, (h + 1) * QT) for h in range(GH)]
        for t in range(GW // LANE):
            pair = jnp.where(near, total[rows[2 * t]], total[rows[2 * t + 1]])
            inverse_ref[at, :, t * LANE : (t + 1) * LANE] = 1.0 / pair
        lane, peaks, totals, tags = packed[g]
        spot = n * SIDE if phase < 2 else n
        for h in range(GH):
            here = lane == spot * GH + h
            peaks = jnp.where(here, peak[rows[h]], peaks)
            totals = jnp.where(here, total[rows[h]], totals)
        share = jnp.where(first == second, 0.5, 1.0)
        totals = jnp.where((lane >> 2) == spot, totals * share, totals)
        tag = jnp.where(code < 0, -1.0, jnp.where(which > 0, 1.0, 0.0))
        tags = jnp.where(((lane - LANE // 2) >> 2) == spot, tag, tags)
        packed[g] = (lane, peaks, totals, tags)

    def apply(phase, b, at):
        n, g = items_of(phase)[at]
        which, first, second = passages(told(phase, b, n, g))
        cols = slice(g * GW, (g + 1) * GW)
        v = jnp.concatenate([v_ref[first, :, cols], v_ref[second, :, cols]], axis=0)
        full = jnp.dot(weight_ref[at], v, preferred_element_type=jnp.float32)
        for t in range(GW // LANE):
            lanes = slice(t * LANE, (t + 1) * LANE)
            a, c = (slice((2 * t + e) * QT, (2 * t + e + 1) * QT) for e in (0, 1))
            part = jnp.where(near, full[a, lanes], full[c, lanes]) * inverse_ref[at, :, lanes]
            part_ref[(*block_of(g, place(phase, b, n)), slice(None), lanes)] = part.astype(jnp.bfloat16)

    def pack_open(phase, b):
        first, second, third = place(phase, b, 0)
        lane = stat_lane - (third * GH if phase < 2 else second * GH * SIDE)
        zero = jnp.zeros((QT, LANE), jnp.float32)
        return {g: (lane, zero, zero + 1.0, zero) for g in PHASES[phase]}

    def pack_close(phase, b, packed):
        first, second, third = place(phase, b, 0)
        for g, (lane, peaks, totals, tags) in packed.items():
            if phase < 2:
                mine = (lane & 15) < GH
            else:
                mine = ((stat_lane & 63) >> 4) == second
            value = jnp.where(stat_lane < LANE // 2, peaks + jnp.log(totals), tags)
            part_stat[g, first] = jnp.where(mine, value, part_stat[g, first])

    def attend(phase, b):
        later, latest = jnp.minimum(b + 1, OWNERS // BATCH - 1), jnp.minimum(b + 2, OWNERS // BATCH - 1)
        packed = pack_open(phase, later)
        for at in range(len(items_of(phase))):
            apply(phase, b, at)
            weigh(phase, later, at, packed)
            score(phase, latest, at)
        pack_close(phase, later, packed)

    def prepare(phase):
        for at in range(len(items_of(phase))):
            score(phase, 0, at)
        packed = pack_open(phase, 0)
        for at in range(len(items_of(phase))):
            weigh(phase, 0, at, packed)
            score(phase, 1, at)
        pack_close(phase, 0, packed)

    def widen(share, at, t):
        pair = [jnp.broadcast_to(share[:, c : c + 1], (QT, LANE)) for c in (at + 2 * t, at + 2 * t + 1)]
        return jnp.where(near, pair[0], pair[1])

    def tiles(block):
        return [block[:, t * LANE : (t + 1) * LANE].astype(jnp.float32) for t in range(GW // LANE)]

    def blend(shares, at, blocks):
        sums = []
        for t in range(GW // LANE):
            total = widen(shares[0], at, t) * tiles(blocks[0])[t]
            for d in range(1, SIDE):
                total = total + widen(shares[d], at, t) * tiles(blocks[d])[t]
            sums.append(total)
        return jnp.concatenate(sums, axis=1).astype(jnp.bfloat16)

    def merge_one(g):
        tree_wait(0, g)
        packed = [part_stat[g, 0]] + [get_stat(near_ref, g, d) for d in range(1, SIDE)]
        tags = [pltpu.roll(stat, LANE // 2, 1) for stat in packed]
        tops = []
        for n in range(2):
            kept = [jnp.where(tag == n, stat, DEAD) for stat, tag in zip(packed, tags)]
            tops.append(jnp.maximum(jnp.maximum(kept[0], kept[1]), jnp.maximum(kept[2], kept[3])))
        terms = [
            jnp.exp(jnp.minimum(stat - jnp.where(tag == 1.0, tops[1], tops[0]), 0.0)) for stat, tag in zip(packed, tags)
        ]
        results, inverses = [], []
        for n in range(2):
            kept = [jnp.where(tag == n, term, 0.0) for term, tag in zip(terms, tags)]
            total = jnp.maximum(kept[0] + kept[1] + kept[2] + kept[3], 1e-30)
            results.append(tops[n] + jnp.log(total))
            inverses.append(1.0 / total)
        stat = jnp.where(stat_lane < LANE // 2, results[0], pltpu.roll(results[1], LANE // 2, 1))
        shares = [
            term * jnp.where(tag == 1.0, -inverses[1], jnp.where(tag == 0.0, inverses[0], 0.0))
            for term, tag in zip(terms, tags)
        ]

        def body(j, carry):
            second, third = j >> 2, j & 3
            blocks = [part_ref[g, 0, j]] + [near_ref[g, d - 1, j] for d in range(1, SIDE)]
            turned = [pltpu.roll(share, (LANE - GH * j) & (LANE - 1), 1) for share in shares]
            for t in range(GW // LANE):
                totals = [jnp.zeros((QT, LANE), jnp.float32)] * 2
                for d in range(SIDE):
                    factor, block = widen(turned[d], 0, t), tiles(blocks[d])[t]
                    totals = [
                        totals[0] + jnp.maximum(factor, 0.0) * block,
                        totals[1] - jnp.minimum(factor, 0.0) * block,
                    ]
                for n in range(2):
                    mid_ref[g, second, third * 2 + n, :, t * LANE : (t + 1) * LANE] = totals[n].astype(jnp.bfloat16)
            return carry

        lax.fori_loop(0, SIDE * SIDE, body, 0, unroll=4)
        mid_stat[g] = stat
        for by in range(1, SIDE):
            put_stat(mid_ref, g, by, stat)
            tree_start(1, g, by)

    def shares_of(packed):
        top = jnp.maximum(jnp.maximum(packed[0], packed[1]), jnp.maximum(packed[2], packed[3]))
        terms = [jnp.exp(stat - top) for stat in packed]
        total = terms[0] + terms[1] + terms[2] + terms[3]
        inverse = 1.0 / total
        return top + jnp.log(total), [term * inverse for term in terms]

    def merge_two(g):
        tree_wait(1, g)
        packed = [mid_stat[g]] + [pltpu.roll(get_stat(next_ref, g, d), LANE - 16 * d, 1) for d in range(1, SIDE)]
        stat, shares = shares_of(packed)
        for third in range(SIDE):
            for n in range(2):
                blocks = [mid_ref[g, 0, third * 2 + n]] + [next_ref[g, d - 1, third * 2 + n] for d in range(1, SIDE)]
                late_ref[g, third, n] = blend(shares, n * LANE // 2 + third * GH, blocks)
        late_stat[g] = stat
        for by in range(1, SIDE):
            put_stat(late_ref, g, by, stat)
            tree_start(2, g, by)

    def merge_three(g):
        tree_wait(2, g)
        packed = [late_stat[g]] + [pltpu.roll(get_stat(last_ref, g, d), LANE - 4 * d, 1) for d in range(1, SIDE)]
        value, shares = shares_of(packed)
        for n in range(2):
            blocks = [late_ref[g, 0, n]] + [last_ref[g, d - 1, n] for d in range(1, SIDE)]
            attended_ref[n * QT : (n + 1) * QT, g * GW : (g + 1) * GW] = blend(shares, n * LANE // 2, blocks)

    def project(phase):
        rows = slice(PHASES[phase][0] * GW, (PHASES[phase][-1] + 1) * GW)
        product = jnp.dot(attended_ref[:, rows], w_ref[rows, :], preferred_element_type=jnp.float32)
        if phase == 0:
            sum_ref[...] = product
        elif phase == 1:
            sum_ref[...] += product
        else:
            out_ref[...] = (sum_ref[...] + product).astype(jnp.bfloat16)

    def send(phase, *offsets):
        for by in offsets:
            for g in PHASES[phase]:
                put_stat(part_ref, g, by, part_stat[g, by])
                tree_start(0, g, by)

    def run(phase, beside):
        prepare(phase)

        def body(b, carry):
            attend(phase, b)
            for at, acts in beside.items():

                @pl.when(b == at)
                def _():
                    for act, *args in acts:
                        act(*args)

            return carry

        lax.fori_loop(0, OWNERS // BATCH, body, 0)

    def each(merge, phase):
        for g in PHASES[phase]:
            merge(g)

    run(
        0,
        {
            1: [(ring_forward, 0)],
            4: [(early_end, 2, early_recv), (ring_start, 1)],
            9: [(ring_end, 0)],
            13: [(ring_forward, 1), (ring_start, 2)],
        },
    )
    send(0, 2, 1, 3)
    run(1, {6: [(ring_forward, 2)], 9: [(ring_end, 1)]})
    send(1, 2, 1, 3)
    each(merge_one, 0)
    ring_end(2)
    run(2, {3: [(send, 2, 1)], 7: [(send, 2, 2)], 11: [(send, 2, 3)]})
    each(merge_two, 0)
    each(merge_one, 1)
    each(merge_one, 2)
    each(merge_two, 1)
    each(merge_three, 0)
    w_home.wait()
    w_give.wait_send()
    w_take.wait_recv()
    project(0)
    each(merge_two, 2)
    each(merge_three, 1)
    project(1)
    ring_sent()
    for stage in range(3):
        for by in range(1, SIDE):
            list_copy(stage, by).wait_send()
    each(merge_three, 2)
    project(2)


def on_device(queries, keys, values, counts, passage_ids, out_weight):
    blocks = [pltpu.VMEM((3, 3, SIDE, SIDE, SIDE, 2 * QT, GW), jnp.bfloat16)]
    for count in (SIDE * SIDE, 2 * SIDE, 2):
        for lead in (SIDE, SIDE - 1):
            blocks.append(pltpu.VMEM((GROUPS, lead, count + 2, QT, GW), jnp.bfloat16))
    for lead in ((SIDE,), (), ()):
        blocks.append(pltpu.VMEM((GROUPS, *lead, QT, LANE), jnp.float32))
    return pl.pallas_call(
        torus_kernel,
        out_shape=jax.ShapeDtypeStruct((2 * QT, D), jnp.bfloat16),
        in_specs=[pl.BlockSpec(memory_space=pltpu.SMEM)]
        + [pl.BlockSpec(memory_space=pltpu.VMEM)] * 2
        + [pl.BlockSpec(memory_space=pl.ANY)] * 3,
        out_specs=pl.BlockSpec(memory_space=pltpu.VMEM),
        scratch_shapes=blocks
        + [
            pltpu.VMEM(keys.shape, jnp.bfloat16),
            pltpu.VMEM(values.shape, jnp.bfloat16),
            pltpu.VMEM((D, D), jnp.bfloat16),
            pltpu.VMEM((SIDE, SIDE, SIDE, 2, LANE), jnp.int32),
            pltpu.VMEM((OWNERS, 1, LANE), jnp.int32),
            pltpu.SMEM((OWNERS, 1, LANE), jnp.int32),
            pltpu.VMEM((3 * BATCH, GH * QT, 2 * PT), jnp.float32),
            pltpu.VMEM((3 * BATCH, GH * QT, 2 * PT), jnp.bfloat16),
            pltpu.VMEM((3 * BATCH, QT, GW), jnp.float32),
            pltpu.VMEM((2 * QT, D), jnp.bfloat16),
            pltpu.VMEM((2 * QT, D), jnp.float32),
            pltpu.SemaphoreType.DMA((4,)),
            pltpu.SemaphoreType.DMA((3, SIDE)),
            pltpu.SemaphoreType.DMA((3, SIDE)),
            pltpu.SemaphoreType.DMA((2,)),
            pltpu.SemaphoreType.DMA((3, 3)),
            pltpu.SemaphoreType.DMA((3, 3)),
            pltpu.SemaphoreType.DMA((GROUPS,)),
            pltpu.SemaphoreType.DMA((GROUPS, 3)),
            pltpu.SemaphoreType.DMA((3, GROUPS)),
            pltpu.SemaphoreType.DMA((3, GROUPS)),
        ],
        compiler_params=pltpu.CompilerParams(
            vmem_limit_bytes=60 * 2**20, collective_id=0, has_side_effects=True
        ),
        cost_estimate=pl.CostEstimate(flops=40 * 10**9, bytes_accessed=20 * 2**20, transcendentals=4 * 10**6),
        name="torus",
    )(counts, passage_ids, queries, keys, values, out_weight)


def solution(mesh):
    placed = (
        P(("grp", "dev"), None),
        P(("grp", "dev"), None, None),
        P(("grp", "dev"), None, None),
        P(("grp", "dev")),
        P(("grp", "dev"), None),
        P("grp", None),
    )
    return jax.shard_map(
        on_device, mesh=mesh, in_specs=placed, out_specs=P(("grp", "dev"), None), check_vma=False
    )
```

```python
import jax
import jax.numpy as jnp
from jax import lax
from jax.experimental import pallas as pl
from jax.experimental.pallas import tpu as pltpu
from jax.sharding import PartitionSpec as P

D = 2048
H = 32
HD = 64
QT = 16
PT = 64
GW = 256
GH = GW // HD
GROUPS = D // GW
LANE = 128
SIDE = 4
OWNERS = SIDE * SIDE * SIDE
PHASES = ((0, 1, 2), (3, 4, 5), (6, 7))
BATCH = 4

GRAY = (0, 1, 3, 2)
DEAD = -1e30
ORDERS = (("x", "y", "z"), ("y", "z", "x"), ("z", "x", "y"))
MESH = pl.DeviceIdType.MESH


def torus_kernel(
    counts_ref, ids_ref, mine_ref, k_hbm, v_hbm, w_hbm, out_ref,
    q_ref, part_ref, near_ref, mid_ref, next_ref, late_ref, last_ref,
    part_stat, mid_stat, late_stat,
    k_ref, v_ref, w_ref, list_ref, code_ref, code_smem, score_ref, weight_ref, inverse_ref, attended_ref, sum_ref,
    load_sem, list_send, list_recv, w_sem, early_send, early_recv, ring_send, ring_recv, tree_send, tree_recv,
):
    me = lax.axis_index("dev")
    grp = lax.axis_index("grp")
    own = {"y": me >> 4, "x": (me >> 2) & 3, "z": me & 3}
    stride = {"y": SIDE * SIDE, "x": SIDE, "z": 1}
    line = {
        axis: {by: (grp, me + ((((own[axis] + by) & 3) - own[axis]) * stride[axis])) for by in range(1, SIDE)}
        for axis in own
    }
    loads = [
        pltpu.make_async_copy(k_hbm, k_ref, load_sem.at[0]),
        pltpu.make_async_copy(v_hbm, v_ref, load_sem.at[1]),
    ]
    for load in loads:
        load.start()
    barrier = pltpu.get_barrier_semaphore()
    for axis in line:
        for by in line[axis]:
            pl.semaphore_signal(barrier, inc=1, device_id=line[axis][by], device_id_type=MESH)
    pl.semaphore_signal(barrier, inc=1, device_id=(1 - grp, me), device_id_type=MESH)
    for g in range(GROUPS):
        q_ref[g % 3, g // 3, 0, 0, 0] = mine_ref[:, g * GW : (g + 1) * GW]
    list_len = ids_ref.shape[1]
    place = lax.broadcasted_iota(jnp.int32, (2, list_len), 1)
    row = lax.broadcasted_iota(jnp.int32, (2, list_len), 0)
    live = place < jnp.where(row == 0, counts_ref[0], counts_ref[1])
    list_ref[0, 0, 0] = jnp.full((2, LANE), -1, jnp.int32)
    list_ref[0, 0, 0, :, :list_len] = jnp.where(live, ids_ref[...], -1)
    pl.semaphore_wait(barrier, 10)

    whole, lower, upper = (0, 2 * QT), (0, QT), (QT, QT)
    both = ((0, 1, 3, lower), (1, 3, 1, upper))
    def order_of(g):
        return ORDERS[g % 3]

    def taken(ref, sem):
        pltpu.make_async_copy(ref, ref, sem).wait()

    def early_part(step, k, at):
        count = len(range(k, GROUPS, 3))
        if step == 0:
            return q_ref.at[k, pl.ds(0, count), at, 0, 0]
        which = pl.ds(0, 1) if step == 1 else pl.ds(1, count - 1)
        return q_ref.at[k, which, :, at, 0]

    def early_start(step):
        for k in range(3):
            for by in range(1, SIDE):
                pltpu.make_async_remote_copy(
                    src_ref=early_part(step, k, 0),
                    dst_ref=early_part(step, k, SIDE - by),
                    send_sem=early_send.at[k, step],
                    recv_sem=early_recv.at[k, step],
                    device_id=line[ORDERS[k][min(step, 1)]][by],
                    device_id_type=MESH,
                ).start()

    def early_end(step, sem):
        for k in range(3):
            taken(early_part(step, k, pl.ds(1, 3)), sem.at[k, step])

    def ring_block(g, at, rows):
        return q_ref.at[g % 3, g // 3, :, :, at, pl.ds(*rows), :]

    def ring_start(phase):
        for g in PHASES[phase]:
            for kind, by, at, rows in both:
                pltpu.make_async_remote_copy(
                    src_ref=ring_block(g, 0, whole),
                    dst_ref=ring_block(g, at, whole),
                    send_sem=ring_send.at[g],
                    recv_sem=ring_recv.at[g, kind],
                    device_id=line[order_of(g)[2]][by],
                    device_id_type=MESH,
                ).start()

    def ring_forward(phase):
        for kind, by, at, rows in both:
            for g in PHASES[phase]:
                taken(ring_block(g, at, whole), ring_recv.at[g, kind])
                pltpu.make_async_remote_copy(
                    src_ref=ring_block(g, at, rows),
                    dst_ref=ring_block(g, 2, rows),
                    send_sem=ring_send.at[g],
                    recv_sem=ring_recv.at[g, 2],
                    device_id=line[order_of(g)[2]][by],
                    device_id_type=MESH,
                ).start()

    def ring_end(phase):
        for g in PHASES[phase]:
            taken(ring_block(g, 2, whole), ring_recv.at[g, 2])

    def ring_sent():
        for step in range(3):
            early_end(step, early_send)
        for g in range(GROUPS):
            taken(q_ref.at[g % 3, g // 3, :, :, pl.ds(1, 3)], ring_send.at[g])

    def list_copy(stage, by):
        order = ("x", "y", "z")
        spot = {axis: 0 for axis in order}
        for axis in order[:stage]:
            spot[axis] = pl.ds(0, SIDE)
        source = list_ref.at[spot["y"], spot["x"], spot["z"]]
        spot[order[stage]] = SIDE - by
        return pltpu.make_async_remote_copy(
            src_ref=source,
            dst_ref=list_ref.at[spot["y"], spot["x"], spot["z"]],
            send_sem=list_send.at[stage, by],
            recv_sem=list_recv.at[stage, by],
            device_id=line[order[stage]][by],
            device_id_type=MESH,
        )

    def list_start(stage):
        for by in range(1, SIDE):
            list_copy(stage, by).start()

    def list_end(stage):
        for by in range(1, SIDE):
            list_copy(stage, by).wait_recv()

    w_rows = D // 2
    w_home = pltpu.make_async_copy(w_hbm, w_ref.at[pl.ds(grp * w_rows, w_rows)], load_sem.at[2])
    w_give = pltpu.make_async_remote_copy(
        src_ref=w_hbm,
        dst_ref=w_ref.at[pl.ds(grp * w_rows, w_rows)],
        send_sem=w_sem.at[0],
        recv_sem=w_sem.at[1],
        device_id=(1 - grp, me),
        device_id_type=MESH,
    )
    w_take = pltpu.make_async_remote_copy(
        src_ref=w_hbm,
        dst_ref=w_ref.at[pl.ds((1 - grp) * w_rows, w_rows)],
        send_sem=w_sem.at[0],
        recv_sem=w_sem.at[1],
        device_id=(1 - grp, me),
        device_id_type=MESH,
    )

    list_start(0)
    early_start(0)
    part_stat[...] = jnp.zeros(part_stat.shape, jnp.float32)
    list_end(0)
    list_start(1)
    early_end(0, early_recv)
    early_start(1)
    list_end(1)
    list_start(2)
    early_end(1, early_recv)
    ring_start(0)
    early_start(2)
    list_end(2)
    firsts, lasts = [], []
    for n in range(2):
        ids = list_ref[:, :, :, n, :].reshape(OWNERS, LANE)
        key = n * 1024 + lax.broadcasted_iota(jnp.int32, (OWNERS, LANE), 1) * 16 + (ids & 15)
        here = (ids >> 4) == me
        firsts.append(jnp.min(jnp.where(here, key, 1 << 20), axis=1, keepdims=True))
        lasts.append(jnp.max(jnp.where(here, key, -1), axis=1, keepdims=True))
    first, last = jnp.minimum(*firsts), jnp.maximum(*lasts)
    code = jnp.where(last < 0, -1, (first >> 10) + ((first & 15) << 1) + ((last & 15) << 5))
    code_ref[...] = jnp.broadcast_to(code, (OWNERS, LANE)).reshape(OWNERS, 1, LANE)
    code_move = pltpu.make_async_copy(code_ref, code_smem, load_sem.at[3])
    code_move.start()
    w_home.start()
    w_give.start()
    for load in loads:
        load.wait()
    code_move.wait()

    row_head = lax.broadcasted_iota(jnp.int32, (GH * QT, GW), 0) // QT
    lane_head = lax.broadcasted_iota(jnp.int32, (GH * QT, GW), 1) // HD
    diag = jnp.where(row_head == lane_head, 0.125, 0.0).astype(jnp.bfloat16)
    stat_lane = lax.broadcasted_iota(jnp.int32, (QT, LANE), 1)
    near = stat_lane < HD

    trees = ((part_ref, near_ref), (mid_ref, next_ref), (late_ref, last_ref))

    def tree_start(stage, g, by, rows=None):
        source, target = (ref.at[g, at] for ref, at in zip(trees[stage], (by, by - 1)))
        if rows is not None:
            source, target = source.at[pl.ds(*rows)], target.at[pl.ds(*rows)]
        pltpu.make_async_remote_copy(
            src_ref=source,
            dst_ref=target,
            send_sem=tree_send.at[stage, g],
            recv_sem=tree_recv.at[stage, g],
            device_id=line[order_of(g)[stage]][by],
            device_id_type=MESH,
        ).start()

    def tree_wait(stage, g):
        target = trees[stage][1]
        taken(target.at[g], tree_send.at[stage, g])
        taken(target.at[g], tree_recv.at[stage, g])

    def put_stat(ref, g, by, value):
        high = value.astype(jnp.bfloat16).astype(jnp.float32)
        rest = value - high
        middle = rest.astype(jnp.bfloat16).astype(jnp.float32)
        blocks = ref.shape[2] - 2
        ref[g, by, blocks] = jnp.concatenate([high, middle], axis=1).astype(jnp.bfloat16)
        ref[g, by, blocks + 1] = jnp.concatenate([rest - middle, jnp.zeros_like(high)], axis=1).astype(jnp.bfloat16)

    def get_stat(ref, g, d):
        blocks = ref.shape[2] - 2
        first = ref[g, d - 1, blocks].astype(jnp.float32)
        return first[:, :LANE] + first[:, LANE:] + ref[g, d - 1, blocks + 1, :, :LANE].astype(jnp.float32)

    stride = {"y": SIDE * SIDE, "x": SIDE, "z": 1}

    def place(phase, b, n):
        turn, quarter = b >> 2, b & 3
        if phase < 2:
            return quarter, n, turn + (turn >> 1) * (1 - 2 * (turn & 1))
        return (turn + 1) & 3, quarter, n

    def block_of(g, phase, b, n):
        if phase < 2:
            return g, b & 3, (b >> 2) * SIDE + n
        return g, ((b >> 2) + 1) & 3, GRAY[n] * SIDE + (b & 3)

    def told(phase, b, n, g):
        return code_smem[sum(at * stride[axis] for axis, at in zip(order_of(g), place(phase, b, n))), 0, 0]

    def passages(code):
        code = jnp.maximum(code, 0)
        return code & 1, (code >> 1) & 15, (code >> 5) & 15

    def items_of(phase):
        return [(n, g) for n in range(BATCH) for g in PHASES[phase]]

    def score(phase, b, at):
        n, g = items_of(phase)[at]
        which, first, second = passages(told(phase, b, n, g))
        cols = slice(g * GW, (g + 1) * GW)
        spot = place(phase, b, n)
        q = jnp.where(which > 0, q_ref[(g % 3, g // 3, *spot, slice(QT, 2 * QT))], q_ref[(g % 3, g // 3, *spot, slice(0, QT))])
        lhs = jnp.concatenate([q] * GH, axis=0) * diag
        k = jnp.concatenate([k_ref[first, :, cols], k_ref[second, :, cols]], axis=0)
        score_ref[at] = lax.dot_general(lhs, k, (((1,), (1,)), ((), ())), preferred_element_type=jnp.float32)

    def weigh(phase, b, at, packed):
        n, g = items_of(phase)[at]
        code = told(phase, b, n, g)
        which, first, second = passages(code)
        values = score_ref[at]
        peak = jnp.max(values, axis=1, keepdims=True)
        shaped = jnp.exp(values - peak)
        total = jnp.sum(shaped, axis=1, keepdims=True)
        weight_ref[at] = shaped.astype(jnp.bfloat16)
        rows = [slice(h * QT, (h + 1) * QT) for h in range(GH)]
        for t in range(GW // LANE):
            pair = jnp.where(near, total[rows[2 * t]], total[rows[2 * t + 1]])
            inverse_ref[at, :, t * LANE : (t + 1) * LANE] = 1.0 / pair
        lane, peaks, totals, tags = packed[g]
        spot = n * SIDE if phase < 2 else n
        for h in range(GH):
            here = lane == spot * GH + h
            peaks = jnp.where(here, peak[rows[h]], peaks)
            totals = jnp.where(here, total[rows[h]], totals)
        share = jnp.where(first == second, 0.5, 1.0)
        totals = jnp.where((lane >> 2) == spot, totals * share, totals)
        tag = jnp.where(code < 0, -1.0, jnp.where(which > 0, 1.0, 0.0))
        tags = jnp.where(((lane - LANE // 2) >> 2) == spot, tag, tags)
        packed[g] = (lane, peaks, totals, tags)

    def apply(phase, b, at):
        n, g = items_of(phase)[at]
        which, first, second = passages(told(phase, b, n, g))
        cols = slice(g * GW, (g + 1) * GW)
        v = jnp.concatenate([v_ref[first, :, cols], v_ref[second, :, cols]], axis=0)
        full = jnp.dot(weight_ref[at], v, preferred_element_type=jnp.float32)
        for t in range(GW // LANE):
            lanes = slice(t * LANE, (t + 1) * LANE)
            a, c = (slice((2 * t + e) * QT, (2 * t + e + 1) * QT) for e in (0, 1))
            part = jnp.where(near, full[a, lanes], full[c, lanes]) * inverse_ref[at, :, lanes]
            part_ref[(*block_of(g, phase, b, n), slice(None), lanes)] = part.astype(jnp.bfloat16)

    def pack_open(phase, b):
        first, second, third = place(phase, b, 0)
        lane = stat_lane - (third * GH if phase < 2 else second * GH * SIDE)
        zero = jnp.zeros((QT, LANE), jnp.float32)
        return {g: (lane, zero, zero + 1.0, zero) for g in PHASES[phase]}

    def pack_close(phase, b, packed):
        first, second, third = place(phase, b, 0)
        for g, (lane, peaks, totals, tags) in packed.items():
            if phase < 2:
                mine = (lane & 15) < GH
            else:
                mine = ((stat_lane & 63) >> 4) == second
            value = jnp.where(stat_lane < LANE // 2, peaks + jnp.log(totals), tags)
            part_stat[g, first] = jnp.where(mine, value, part_stat[g, first])

    def attend(phase, b):
        later, latest = jnp.minimum(b + 1, OWNERS // BATCH - 1), jnp.minimum(b + 2, OWNERS // BATCH - 1)
        packed = pack_open(phase, later)
        for at in range(len(items_of(phase))):
            apply(phase, b, at)
            weigh(phase, later, at, packed)
            score(phase, latest, at)
        pack_close(phase, later, packed)

    def prepare(phase):
        for at in range(len(items_of(phase))):
            score(phase, 0, at)
        packed = pack_open(phase, 0)
        for at in range(len(items_of(phase))):
            weigh(phase, 0, at, packed)
            score(phase, 1, at)
        pack_close(phase, 0, packed)

    def widen(share, at, t):
        pair = [jnp.broadcast_to(share[:, c : c + 1], (QT, LANE)) for c in (at + 2 * t, at + 2 * t + 1)]
        return jnp.where(near, pair[0], pair[1])

    def tiles(block):
        return [block[:, t * LANE : (t + 1) * LANE].astype(jnp.float32) for t in range(GW // LANE)]

    def blend(shares, at, blocks):
        sums = []
        for t in range(GW // LANE):
            total = widen(shares[0], at, t) * tiles(blocks[0])[t]
            for d in range(1, SIDE):
                total = total + widen(shares[d], at, t) * tiles(blocks[d])[t]
            sums.append(total)
        return jnp.concatenate(sums, axis=1).astype(jnp.bfloat16)

    def merge_one(g):
        tree_wait(0, g)
        packed = [part_stat[g, 0]] + [get_stat(near_ref, g, d) for d in range(1, SIDE)]
        tags = [pltpu.roll(stat, LANE // 2, 1) for stat in packed]
        tops = []
        for n in range(2):
            kept = [jnp.where(tag == n, stat, DEAD) for stat, tag in zip(packed, tags)]
            tops.append(jnp.maximum(jnp.maximum(kept[0], kept[1]), jnp.maximum(kept[2], kept[3])))
        terms = [
            jnp.exp(jnp.minimum(stat - jnp.where(tag == 1.0, tops[1], tops[0]), 0.0)) for stat, tag in zip(packed, tags)
        ]
        results, inverses = [], []
        for n in range(2):
            kept = [jnp.where(tag == n, term, 0.0) for term, tag in zip(terms, tags)]
            total = jnp.maximum(kept[0] + kept[1] + kept[2] + kept[3], 1e-30)
            results.append(tops[n] + jnp.log(total))
            inverses.append(1.0 / total)
        stat = jnp.where(stat_lane < LANE // 2, results[0], pltpu.roll(results[1], LANE // 2, 1))
        shares = [
            term * jnp.where(tag == 1.0, -inverses[1], jnp.where(tag == 0.0, inverses[0], 0.0))
            for term, tag in zip(terms, tags)
        ]

        def body(j, carry):
            second, turn = j & 3, j >> 2
            third = turn + (turn >> 1) * (1 - 2 * (turn & 1))
            blocks = [part_ref[g, 0, j]] + [near_ref[g, d - 1, j] for d in range(1, SIDE)]
            turned = [pltpu.roll(share, (LANE - GH * (second * SIDE + third)) & (LANE - 1), 1) for share in shares]
            for t in range(GW // LANE):
                totals = [jnp.zeros((QT, LANE), jnp.float32)] * 2
                for d in range(SIDE):
                    factor, block = widen(turned[d], 0, t), tiles(blocks[d])[t]
                    totals = [
                        totals[0] + jnp.maximum(factor, 0.0) * block,
                        totals[1] - jnp.minimum(factor, 0.0) * block,
                    ]
                for n in range(2):
                    mid_ref[g, second, third * 2 + n, :, t * LANE : (t + 1) * LANE] = totals[n].astype(jnp.bfloat16)
            return carry

        lax.fori_loop(0, SIDE * SIDE, body, 0, unroll=4)
        mid_stat[g] = stat
        for by in range(1, SIDE):
            put_stat(mid_ref, g, by, stat)
            tree_start(1, g, by)

    def shares_of(packed):
        top = jnp.maximum(jnp.maximum(packed[0], packed[1]), jnp.maximum(packed[2], packed[3]))
        terms = [jnp.exp(stat - top) for stat in packed]
        total = terms[0] + terms[1] + terms[2] + terms[3]
        inverse = 1.0 / total
        return top + jnp.log(total), [term * inverse for term in terms]

    def merge_two(g):
        tree_wait(1, g)
        packed = [mid_stat[g]] + [pltpu.roll(get_stat(next_ref, g, d), LANE - 16 * d, 1) for d in range(1, SIDE)]
        stat, shares = shares_of(packed)
        for third in range(SIDE):
            for n in range(2):
                blocks = [mid_ref[g, 0, third * 2 + n]] + [next_ref[g, d - 1, third * 2 + n] for d in range(1, SIDE)]
                late_ref[g, third, n] = blend(shares, n * LANE // 2 + third * GH, blocks)
        late_stat[g] = stat
        for by in range(1, SIDE):
            put_stat(late_ref, g, by, stat)
            tree_start(2, g, by)

    def merge_three(g):
        tree_wait(2, g)
        packed = [late_stat[g]] + [pltpu.roll(get_stat(last_ref, g, d), LANE - 4 * d, 1) for d in range(1, SIDE)]
        value, shares = shares_of(packed)
        for n in range(2):
            blocks = [late_ref[g, 0, n]] + [last_ref[g, d - 1, n] for d in range(1, SIDE)]
            attended_ref[n * QT : (n + 1) * QT, g * GW : (g + 1) * GW] = blend(shares, n * LANE // 2, blocks)

    def project(phase):
        rows = slice(PHASES[phase][0] * GW, (PHASES[phase][-1] + 1) * GW)
        product = jnp.dot(attended_ref[:, rows], w_ref[rows, :], preferred_element_type=jnp.float32)
        if phase == 0:
            sum_ref[...] = product
        elif phase == 1:
            sum_ref[...] += product
        else:
            out_ref[...] = (sum_ref[...] + product).astype(jnp.bfloat16)

    def send(phase, *offsets):
        for by in offsets:
            for g in PHASES[phase]:
                put_stat(part_ref, g, by, part_stat[g, by])
                tree_start(0, g, by)

    def send_turn(phase, turn):
        for by in (2, 1, 3):
            for g in PHASES[phase]:
                if turn == SIDE - 1:
                    put_stat(part_ref, g, by, part_stat[g, by])
                tree_start(0, g, by, (turn * SIDE, SIDE + 2 if turn == SIDE - 1 else SIDE))

    def run(phase, beside):
        prepare(phase)

        def body(b, carry):
            attend(phase, b)
            for at, acts in beside.items():

                @pl.when(b == at)
                def _():
                    for act, *args in acts:
                        act(*args)

            return carry

        lax.fori_loop(0, OWNERS // BATCH, body, 0)

    def each(merge, phase):
        for g in PHASES[phase]:
            merge(g)

    run(
        0,
        {
            1: [(ring_forward, 0)],
            4: [(early_end, 2, early_recv), (ring_start, 1)],
            9: [(ring_end, 0)],
            13: [(ring_forward, 1), (ring_start, 2)],
        },
    )
    send(0, 2, 1, 3)
    run(
        1,
        {
            3: [(send_turn, 1, 0)],
            6: [(ring_forward, 2)],
            7: [(send_turn, 1, 1)],
            9: [(ring_end, 1)],
            11: [(send_turn, 1, 2)],
        },
    )
    send_turn(1, 3)
    each(merge_one, 0)
    ring_end(2)
    run(2, {3: [(send, 2, 1)], 7: [(send, 2, 2)], 11: [(send, 2, 3)]})
    each(merge_two, 0)
    each(merge_one, 1)
    each(merge_one, 2)
    each(merge_two, 1)
    each(merge_three, 0)
    w_home.wait()
    w_give.wait_send()
    w_take.wait_recv()
    project(0)
    each(merge_two, 2)
    each(merge_three, 1)
    project(1)
    ring_sent()
    for stage in range(3):
        for by in range(1, SIDE):
            list_copy(stage, by).wait_send()
    each(merge_three, 2)
    project(2)


def on_device(queries, keys, values, counts, passage_ids, out_weight):
    blocks = [pltpu.VMEM((3, 3, SIDE, SIDE, SIDE, 2 * QT, GW), jnp.bfloat16)]
    for count in (SIDE * SIDE, 2 * SIDE, 2):
        for lead in (SIDE, SIDE - 1):
            blocks.append(pltpu.VMEM((GROUPS, lead, count + 2, QT, GW), jnp.bfloat16))
    for lead in ((SIDE,), (), ()):
        blocks.append(pltpu.VMEM((GROUPS, *lead, QT, LANE), jnp.float32))
    return pl.pallas_call(
        torus_kernel,
        out_shape=jax.ShapeDtypeStruct((2 * QT, D), jnp.bfloat16),
        in_specs=[pl.BlockSpec(memory_space=pltpu.SMEM)]
        + [pl.BlockSpec(memory_space=pltpu.VMEM)] * 2
        + [pl.BlockSpec(memory_space=pl.ANY)] * 3,
        out_specs=pl.BlockSpec(memory_space=pltpu.VMEM),
        scratch_shapes=blocks
        + [
            pltpu.VMEM(keys.shape, jnp.bfloat16),
            pltpu.VMEM(values.shape, jnp.bfloat16),
            pltpu.VMEM((D, D), jnp.bfloat16),
            pltpu.VMEM((SIDE, SIDE, SIDE, 2, LANE), jnp.int32),
            pltpu.VMEM((OWNERS, 1, LANE), jnp.int32),
            pltpu.SMEM((OWNERS, 1, LANE), jnp.int32),
            pltpu.VMEM((3 * BATCH, GH * QT, 2 * PT), jnp.float32),
            pltpu.VMEM((3 * BATCH, GH * QT, 2 * PT), jnp.bfloat16),
            pltpu.VMEM((3 * BATCH, QT, GW), jnp.float32),
            pltpu.VMEM((2 * QT, D), jnp.bfloat16),
            pltpu.VMEM((2 * QT, D), jnp.float32),
            pltpu.SemaphoreType.DMA((4,)),
            pltpu.SemaphoreType.DMA((3, SIDE)),
            pltpu.SemaphoreType.DMA((3, SIDE)),
            pltpu.SemaphoreType.DMA((2,)),
            pltpu.SemaphoreType.DMA((3, 3)),
            pltpu.SemaphoreType.DMA((3, 3)),
            pltpu.SemaphoreType.DMA((GROUPS,)),
            pltpu.SemaphoreType.DMA((GROUPS, 3)),
            pltpu.SemaphoreType.DMA((3, GROUPS)),
            pltpu.SemaphoreType.DMA((3, GROUPS)),
        ],
        compiler_params=pltpu.CompilerParams(
            vmem_limit_bytes=60 * 2**20, collective_id=0, has_side_effects=True
        ),
        cost_estimate=pl.CostEstimate(flops=40 * 10**9, bytes_accessed=20 * 2**20, transcendentals=4 * 10**6),
        name="torus",
    )(counts, passage_ids, queries, keys, values, out_weight)


def solution(mesh):
    placed = (
        P(("grp", "dev"), None),
        P(("grp", "dev"), None, None),
        P(("grp", "dev"), None, None),
        P(("grp", "dev")),
        P(("grp", "dev"), None),
        P("grp", None),
    )
    return jax.shard_map(
        on_device, mesh=mesh, in_specs=placed, out_specs=P(("grp", "dev"), None), check_vma=False
    )
```

```python
import jax
import jax.numpy as jnp
from jax import lax
from jax.experimental import pallas as pl
from jax.experimental.pallas import tpu as pltpu
from jax.sharding import PartitionSpec as P

D = 2048
H = 32
HD = 64
QT = 16
PT = 64
GW = 256
GH = GW // HD
GROUPS = D // GW
LANE = 128
SIDE = 4
OWNERS = SIDE * SIDE * SIDE
PHASES = ((0, 1, 2), (3, 4, 5), (6, 7))
BATCH = 4

DEAD = -1e30
ORDERS = (("x", "y", "z"), ("y", "z", "x"), ("z", "x", "y"))
MESH = pl.DeviceIdType.MESH


def torus_kernel(
    counts_ref, ids_ref, mine_ref, k_hbm, v_hbm, w_hbm, out_ref,
    q_ref, part_ref, near_ref, mid_ref, next_ref, late_ref, last_ref,
    part_stat, mid_stat, late_stat,
    k_ref, v_ref, w_ref, list_ref, code_ref, code_smem, score_ref, weight_ref, inverse_ref, attended_ref, sum_ref,
    load_sem, list_send, list_recv, w_sem, early_send, early_recv, ring_send, ring_recv, tree_send, tree_recv,
):
    me = lax.axis_index("dev")
    grp = lax.axis_index("grp")
    own = {"y": me >> 4, "x": (me >> 2) & 3, "z": me & 3}
    stride = {"y": SIDE * SIDE, "x": SIDE, "z": 1}
    line = {
        axis: {by: (grp, me + ((((own[axis] + by) & 3) - own[axis]) * stride[axis])) for by in range(1, SIDE)}
        for axis in own
    }
    loads = [
        pltpu.make_async_copy(k_hbm, k_ref, load_sem.at[0]),
        pltpu.make_async_copy(v_hbm, v_ref, load_sem.at[1]),
    ]
    for load in loads:
        load.start()
    barrier = pltpu.get_barrier_semaphore()
    for axis in line:
        for by in line[axis]:
            pl.semaphore_signal(barrier, inc=1, device_id=line[axis][by], device_id_type=MESH)
    pl.semaphore_signal(barrier, inc=1, device_id=(1 - grp, me), device_id_type=MESH)
    for g in range(GROUPS):
        q_ref[g % 3, g // 3, 0, 0, 0] = mine_ref[:, g * GW : (g + 1) * GW]
    list_len = ids_ref.shape[1]
    place = lax.broadcasted_iota(jnp.int32, (2, list_len), 1)
    row = lax.broadcasted_iota(jnp.int32, (2, list_len), 0)
    live = place < jnp.where(row == 0, counts_ref[0], counts_ref[1])
    list_ref[0, 0, 0] = jnp.full((2, LANE), -1, jnp.int32)
    list_ref[0, 0, 0, :, :list_len] = jnp.where(live, ids_ref[...], -1)
    pl.semaphore_wait(barrier, 10)

    whole, lower, upper = (0, 2 * QT), (0, QT), (QT, QT)
    both = ((0, 1, 3, lower), (1, 3, 1, upper))
    def order_of(g):
        return ORDERS[g % 3]

    def taken(ref, sem):
        pltpu.make_async_copy(ref, ref, sem).wait()

    def early_part(step, k, at):
        count = len(range(k, GROUPS, 3))
        if step == 0:
            return q_ref.at[k, pl.ds(0, count), at, 0, 0]
        which = pl.ds(0, 1) if step == 1 else pl.ds(1, count - 1)
        return q_ref.at[k, which, :, at, 0]

    def early_start(step):
        for k in range(3):
            for by in range(1, SIDE):
                pltpu.make_async_remote_copy(
                    src_ref=early_part(step, k, 0),
                    dst_ref=early_part(step, k, SIDE - by),
                    send_sem=early_send.at[k, step],
                    recv_sem=early_recv.at[k, step],
                    device_id=line[ORDERS[k][min(step, 1)]][by],
                    device_id_type=MESH,
                ).start()

    def early_end(step, sem):
        for k in range(3):
            taken(early_part(step, k, pl.ds(1, 3)), sem.at[k, step])

    def ring_block(g, at, rows):
        return q_ref.at[g % 3, g // 3, :, :, at, pl.ds(*rows), :]

    def ring_start(phase):
        for g in PHASES[phase]:
            for kind, by, at, rows in both:
                pltpu.make_async_remote_copy(
                    src_ref=ring_block(g, 0, whole),
                    dst_ref=ring_block(g, at, whole),
                    send_sem=ring_send.at[g],
                    recv_sem=ring_recv.at[g, kind],
                    device_id=line[order_of(g)[2]][by],
                    device_id_type=MESH,
                ).start()

    def ring_forward(phase):
        for kind, by, at, rows in both:
            for g in PHASES[phase]:
                taken(ring_block(g, at, whole), ring_recv.at[g, kind])
                pltpu.make_async_remote_copy(
                    src_ref=ring_block(g, at, rows),
                    dst_ref=ring_block(g, 2, rows),
                    send_sem=ring_send.at[g],
                    recv_sem=ring_recv.at[g, 2],
                    device_id=line[order_of(g)[2]][by],
                    device_id_type=MESH,
                ).start()

    def ring_end(phase):
        for g in PHASES[phase]:
            taken(ring_block(g, 2, whole), ring_recv.at[g, 2])

    def ring_sent():
        for step in range(3):
            early_end(step, early_send)
        for g in range(GROUPS):
            taken(q_ref.at[g % 3, g // 3, :, :, pl.ds(1, 3)], ring_send.at[g])

    def list_copy(stage, by):
        order = ("x", "y", "z")
        spot = {axis: 0 for axis in order}
        for axis in order[:stage]:
            spot[axis] = pl.ds(0, SIDE)
        source = list_ref.at[spot["y"], spot["x"], spot["z"]]
        spot[order[stage]] = SIDE - by
        return pltpu.make_async_remote_copy(
            src_ref=source,
            dst_ref=list_ref.at[spot["y"], spot["x"], spot["z"]],
            send_sem=list_send.at[stage, by],
            recv_sem=list_recv.at[stage, by],
            device_id=line[order[stage]][by],
            device_id_type=MESH,
        )

    def list_start(stage):
        for by in range(1, SIDE):
            list_copy(stage, by).start()

    def list_end(stage):
        for by in range(1, SIDE):
            list_copy(stage, by).wait_recv()

    w_rows = D // 2
    w_home = pltpu.make_async_copy(w_hbm, w_ref.at[pl.ds(grp * w_rows, w_rows)], load_sem.at[2])
    w_give = pltpu.make_async_remote_copy(
        src_ref=w_hbm,
        dst_ref=w_ref.at[pl.ds(grp * w_rows, w_rows)],
        send_sem=w_sem.at[0],
        recv_sem=w_sem.at[1],
        device_id=(1 - grp, me),
        device_id_type=MESH,
    )
    w_take = pltpu.make_async_remote_copy(
        src_ref=w_hbm,
        dst_ref=w_ref.at[pl.ds((1 - grp) * w_rows, w_rows)],
        send_sem=w_sem.at[0],
        recv_sem=w_sem.at[1],
        device_id=(1 - grp, me),
        device_id_type=MESH,
    )

    list_start(0)
    early_start(0)
    part_stat[...] = jnp.zeros(part_stat.shape, jnp.float32)
    list_end(0)
    list_start(1)
    early_end(0, early_recv)
    early_start(1)
    list_end(1)
    list_start(2)
    early_end(1, early_recv)
    ring_start(0)
    list_end(2)
    firsts, lasts = [], []
    for n in range(2):
        ids = list_ref[:, :, :, n, :].reshape(OWNERS, LANE)
        key = n * 1024 + lax.broadcasted_iota(jnp.int32, (OWNERS, LANE), 1) * 16 + (ids & 15)
        here = (ids >> 4) == me
        firsts.append(jnp.min(jnp.where(here, key, 1 << 20), axis=1, keepdims=True))
        lasts.append(jnp.max(jnp.where(here, key, -1), axis=1, keepdims=True))
    first, last = jnp.minimum(*firsts), jnp.maximum(*lasts)
    code = jnp.where(last < 0, -1, (first >> 10) + ((first & 15) << 1) + ((last & 15) << 5))
    code_ref[...] = jnp.broadcast_to(code, (OWNERS, LANE)).reshape(OWNERS, 1, LANE)
    code_move = pltpu.make_async_copy(code_ref, code_smem, load_sem.at[3])
    code_move.start()
    for load in loads:
        load.wait()
    code_move.wait()

    row_head = lax.broadcasted_iota(jnp.int32, (GH * QT, GW), 0) // QT
    lane_head = lax.broadcasted_iota(jnp.int32, (GH * QT, GW), 1) // HD
    diag = jnp.where(row_head == lane_head, 0.125, 0.0).astype(jnp.bfloat16)
    stat_lane = lax.broadcasted_iota(jnp.int32, (QT, LANE), 1)
    near = stat_lane < HD

    trees = ((part_ref, near_ref), (mid_ref, next_ref), (late_ref, last_ref))

    def tree_start(stage, g, by):
        source, target = trees[stage]
        pltpu.make_async_remote_copy(
            src_ref=source.at[g, by],
            dst_ref=target.at[g, by - 1],
            send_sem=tree_send.at[stage, g],
            recv_sem=tree_recv.at[stage, g],
            device_id=line[order_of(g)[stage]][by],
            device_id_type=MESH,
        ).start()

    def tree_wait(stage, g):
        target = trees[stage][1]
        taken(target.at[g], tree_send.at[stage, g])
        taken(target.at[g], tree_recv.at[stage, g])

    def put_stat(ref, g, by, value):
        high = value.astype(jnp.bfloat16).astype(jnp.float32)
        rest = value - high
        middle = rest.astype(jnp.bfloat16).astype(jnp.float32)
        blocks = ref.shape[2] - 2
        ref[g, by, blocks] = jnp.concatenate([high, middle], axis=1).astype(jnp.bfloat16)
        ref[g, by, blocks + 1] = jnp.concatenate([rest - middle, jnp.zeros_like(high)], axis=1).astype(jnp.bfloat16)

    def get_stat(ref, g, d):
        blocks = ref.shape[2] - 2
        first = ref[g, d - 1, blocks].astype(jnp.float32)
        return first[:, :LANE] + first[:, LANE:] + ref[g, d - 1, blocks + 1, :, :LANE].astype(jnp.float32)

    stride = {"y": SIDE * SIDE, "x": SIDE, "z": 1}

    def place(phase, b, n):
        turn, quarter = b >> 2, b & 3
        if phase < 2:
            return quarter, n, turn + (turn >> 1) * (1 - 2 * (turn & 1))
        return (turn + 1) & 3, quarter, n

    def block_of(g, spot):
        return g, spot[0], spot[1] * SIDE + spot[2]

    def told(phase, b, n, g):
        return code_smem[sum(at * stride[axis] for axis, at in zip(order_of(g), place(phase, b, n))), 0, 0]

    def passages(code):
        code = jnp.maximum(code, 0)
        return code & 1, (code >> 1) & 15, (code >> 5) & 15

    def items_of(phase):
        return [(n, g) for n in range(BATCH) for g in PHASES[phase]]

    def score(phase, b, at):
        n, g = items_of(phase)[at]
        which, first, second = passages(told(phase, b, n, g))
        cols = slice(g * GW, (g + 1) * GW)
        spot = place(phase, b, n)
        q = jnp.where(which > 0, q_ref[(g % 3, g // 3, *spot, slice(QT, 2 * QT))], q_ref[(g % 3, g // 3, *spot, slice(0, QT))])
        lhs = jnp.concatenate([q] * GH, axis=0) * diag
        k = jnp.concatenate([k_ref[first, :, cols], k_ref[second, :, cols]], axis=0)
        score_ref[at] = lax.dot_general(lhs, k, (((1,), (1,)), ((), ())), preferred_element_type=jnp.float32)

    def weigh(phase, b, at, packed):
        n, g = items_of(phase)[at]
        code = told(phase, b, n, g)
        which, first, second = passages(code)
        values = score_ref[at]
        peak = jnp.max(values, axis=1, keepdims=True)
        shaped = jnp.exp(values - peak)
        total = jnp.sum(shaped, axis=1, keepdims=True)
        weight_ref[at] = shaped.astype(jnp.bfloat16)
        rows = [slice(h * QT, (h + 1) * QT) for h in range(GH)]
        for t in range(GW // LANE):
            pair = jnp.where(near, total[rows[2 * t]], total[rows[2 * t + 1]])
            inverse_ref[at, :, t * LANE : (t + 1) * LANE] = 1.0 / pair
        lane, peaks, totals, tags = packed[g]
        spot = n * SIDE if phase < 2 else n
        for h in range(GH):
            here = lane == spot * GH + h
            peaks = jnp.where(here, peak[rows[h]], peaks)
            totals = jnp.where(here, total[rows[h]], totals)
        share = jnp.where(first == second, 0.5, 1.0)
        totals = jnp.where((lane >> 2) == spot, totals * share, totals)
        tag = jnp.where(code < 0, -1.0, jnp.where(which > 0, 1.0, 0.0))
        tags = jnp.where(((lane - LANE // 2) >> 2) == spot, tag, tags)
        packed[g] = (lane, peaks, totals, tags)

    def apply(phase, b, at):
        n, g = items_of(phase)[at]
        which, first, second = passages(told(phase, b, n, g))
        cols = slice(g * GW, (g + 1) * GW)
        v = jnp.concatenate([v_ref[first, :, cols], v_ref[second, :, cols]], axis=0)
        full = jnp.dot(weight_ref[at], v, preferred_element_type=jnp.float32)
        for t in range(GW // LANE):
            lanes = slice(t * LANE, (t + 1) * LANE)
            a, c = (slice((2 * t + e) * QT, (2 * t + e + 1) * QT) for e in (0, 1))
            part = jnp.where(near, full[a, lanes], full[c, lanes]) * inverse_ref[at, :, lanes]
            part_ref[(*block_of(g, place(phase, b, n)), slice(None), lanes)] = part.astype(jnp.bfloat16)

    def pack_open(phase, b):
        first, second, third = place(phase, b, 0)
        lane = stat_lane - (third * GH if phase < 2 else second * GH * SIDE)
        zero = jnp.zeros((QT, LANE), jnp.float32)
        return {g: (lane, zero, zero + 1.0, zero) for g in PHASES[phase]}

    def pack_close(phase, b, packed):
        first, second, third = place(phase, b, 0)
        for g, (lane, peaks, totals, tags) in packed.items():
            if phase < 2:
                mine = (lane & 15) < GH
            else:
                mine = ((stat_lane & 63) >> 4) == second
            value = jnp.where(stat_lane < LANE // 2, peaks + jnp.log(totals), tags)
            part_stat[g, first] = jnp.where(mine, value, part_stat[g, first])

    def attend(phase, b):
        later, latest = jnp.minimum(b + 1, OWNERS // BATCH - 1), jnp.minimum(b + 2, OWNERS // BATCH - 1)
        packed = pack_open(phase, later)
        for at in range(len(items_of(phase))):
            apply(phase, b, at)
            weigh(phase, later, at, packed)
            score(phase, latest, at)
        pack_close(phase, later, packed)

    def prepare(phase):
        for at in range(len(items_of(phase))):
            score(phase, 0, at)
        packed = pack_open(phase, 0)
        for at in range(len(items_of(phase))):
            weigh(phase, 0, at, packed)
            score(phase, 1, at)
        pack_close(phase, 0, packed)

    def widen(share, at, t):
        pair = [jnp.broadcast_to(share[:, c : c + 1], (QT, LANE)) for c in (at + 2 * t, at + 2 * t + 1)]
        return jnp.where(near, pair[0], pair[1])

    def tiles(block):
        return [block[:, t * LANE : (t + 1) * LANE].astype(jnp.float32) for t in range(GW // LANE)]

    def blend(shares, at, blocks):
        sums = []
        for t in range(GW // LANE):
            total = widen(shares[0], at, t) * tiles(blocks[0])[t]
            for d in range(1, SIDE):
                total = total + widen(shares[d], at, t) * tiles(blocks[d])[t]
            sums.append(total)
        return jnp.concatenate(sums, axis=1).astype(jnp.bfloat16)

    def merge_one(g):
        tree_wait(0, g)
        packed = [part_stat[g, 0]] + [get_stat(near_ref, g, d) for d in range(1, SIDE)]
        tags = [pltpu.roll(stat, LANE // 2, 1) for stat in packed]
        tops = []
        for n in range(2):
            kept = [jnp.where(tag == n, stat, DEAD) for stat, tag in zip(packed, tags)]
            tops.append(jnp.maximum(jnp.maximum(kept[0], kept[1]), jnp.maximum(kept[2], kept[3])))
        terms = [
            jnp.exp(jnp.minimum(stat - jnp.where(tag == 1.0, tops[1], tops[0]), 0.0)) for stat, tag in zip(packed, tags)
        ]
        results, inverses = [], []
        for n in range(2):
            kept = [jnp.where(tag == n, term, 0.0) for term, tag in zip(terms, tags)]
            total = jnp.maximum(kept[0] + kept[1] + kept[2] + kept[3], 1e-30)
            results.append(tops[n] + jnp.log(total))
            inverses.append(1.0 / total)
        stat = jnp.where(stat_lane < LANE // 2, results[0], pltpu.roll(results[1], LANE // 2, 1))
        shares = [
            term * jnp.where(tag == 1.0, -inverses[1], jnp.where(tag == 0.0, inverses[0], 0.0))
            for term, tag in zip(terms, tags)
        ]

        def body(j, carry):
            second, third = j >> 2, j & 3
            blocks = [part_ref[g, 0, j]] + [near_ref[g, d - 1, j] for d in range(1, SIDE)]
            turned = [pltpu.roll(share, (LANE - GH * j) & (LANE - 1), 1) for share in shares]
            for t in range(GW // LANE):
                totals = [jnp.zeros((QT, LANE), jnp.float32)] * 2
                for d in range(SIDE):
                    factor, block = widen(turned[d], 0, t), tiles(blocks[d])[t]
                    totals = [
                        totals[0] + jnp.maximum(factor, 0.0) * block,
                        totals[1] - jnp.minimum(factor, 0.0) * block,
                    ]
                for n in range(2):
                    mid_ref[g, second, third * 2 + n, :, t * LANE : (t + 1) * LANE] = totals[n].astype(jnp.bfloat16)
            return carry

        lax.fori_loop(0, SIDE * SIDE, body, 0, unroll=4)
        mid_stat[g] = stat
        for by in range(1, SIDE):
            put_stat(mid_ref, g, by, stat)
            tree_start(1, g, by)

    def shares_of(packed):
        top = jnp.maximum(jnp.maximum(packed[0], packed[1]), jnp.maximum(packed[2], packed[3]))
        terms = [jnp.exp(stat - top) for stat in packed]
        total = terms[0] + terms[1] + terms[2] + terms[3]
        inverse = 1.0 / total
        return top + jnp.log(total), [term * inverse for term in terms]

    def merge_two(g):
        tree_wait(1, g)
        packed = [mid_stat[g]] + [pltpu.roll(get_stat(next_ref, g, d), LANE - 16 * d, 1) for d in range(1, SIDE)]
        stat, shares = shares_of(packed)
        for third in range(SIDE):
            for n in range(2):
                blocks = [mid_ref[g, 0, third * 2 + n]] + [next_ref[g, d - 1, third * 2 + n] for d in range(1, SIDE)]
                late_ref[g, third, n] = blend(shares, n * LANE // 2 + third * GH, blocks)
        late_stat[g] = stat
        for by in range(1, SIDE):
            put_stat(late_ref, g, by, stat)
            tree_start(2, g, by)

    def merge_three(g):
        tree_wait(2, g)
        packed = [late_stat[g]] + [pltpu.roll(get_stat(last_ref, g, d), LANE - 4 * d, 1) for d in range(1, SIDE)]
        value, shares = shares_of(packed)
        for n in range(2):
            blocks = [late_ref[g, 0, n]] + [last_ref[g, d - 1, n] for d in range(1, SIDE)]
            attended_ref[n * QT : (n + 1) * QT, g * GW : (g + 1) * GW] = blend(shares, n * LANE // 2, blocks)

    def project(phase):
        rows = slice(PHASES[phase][0] * GW, (PHASES[phase][-1] + 1) * GW)
        product = jnp.dot(attended_ref[:, rows], w_ref[rows, :], preferred_element_type=jnp.float32)
        if phase == 0:
            sum_ref[...] = product
        elif phase == 1:
            sum_ref[...] += product
        else:
            out_ref[...] = (sum_ref[...] + product).astype(jnp.bfloat16)

    def send(phase, *offsets):
        for by in offsets:
            for g in PHASES[phase]:
                put_stat(part_ref, g, by, part_stat[g, by])
                tree_start(0, g, by)

    def run(phase, beside):
        prepare(phase)

        def body(b, carry):
            attend(phase, b)
            for at, acts in beside.items():

                @pl.when(b == at)
                def _():
                    for act, *args in acts:
                        act(*args)

            return carry

        lax.fori_loop(0, OWNERS // BATCH, body, 0)

    def each(merge, phase):
        for g in PHASES[phase]:
            merge(g)

    def weights_start():
        w_home.start()
        w_give.start()

    run(
        0,
        {
            1: [(ring_forward, 0), (early_start, 2)],
            6: [(early_end, 2, early_recv), (ring_start, 1)],
            9: [(ring_end, 0)],
            14: [(ring_forward, 1), (ring_start, 2)],
        },
    )
    send(0, 2, 1, 3)
    run(1, {6: [(ring_forward, 2)], 9: [(ring_end, 1)], 10: [(weights_start,)]})
    send(1, 2, 1, 3)
    each(merge_one, 0)
    ring_end(2)
    run(2, {3: [(send, 2, 1)], 7: [(send, 2, 2)], 11: [(send, 2, 3)]})
    each(merge_two, 0)
    each(merge_one, 1)
    each(merge_one, 2)
    each(merge_two, 1)
    each(merge_three, 0)
    w_home.wait()
    w_give.wait_send()
    w_take.wait_recv()
    project(0)
    each(merge_two, 2)
    each(merge_three, 1)
    project(1)
    ring_sent()
    for stage in range(3):
        for by in range(1, SIDE):
            list_copy(stage, by).wait_send()
    each(merge_three, 2)
    project(2)


def on_device(queries, keys, values, counts, passage_ids, out_weight):
    blocks = [pltpu.VMEM((3, 3, SIDE, SIDE, SIDE, 2 * QT, GW), jnp.bfloat16)]
    for count in (SIDE * SIDE, 2 * SIDE, 2):
        for lead in (SIDE, SIDE - 1):
            blocks.append(pltpu.VMEM((GROUPS, lead, count + 2, QT, GW), jnp.bfloat16))
    for lead in ((SIDE,), (), ()):
        blocks.append(pltpu.VMEM((GROUPS, *lead, QT, LANE), jnp.float32))
    return pl.pallas_call(
        torus_kernel,
        out_shape=jax.ShapeDtypeStruct((2 * QT, D), jnp.bfloat16),
        in_specs=[pl.BlockSpec(memory_space=pltpu.SMEM)]
        + [pl.BlockSpec(memory_space=pltpu.VMEM)] * 2
        + [pl.BlockSpec(memory_space=pl.ANY)] * 3,
        out_specs=pl.BlockSpec(memory_space=pltpu.VMEM),
        scratch_shapes=blocks
        + [
            pltpu.VMEM(keys.shape, jnp.bfloat16),
            pltpu.VMEM(values.shape, jnp.bfloat16),
            pltpu.VMEM((D, D), jnp.bfloat16),
            pltpu.VMEM((SIDE, SIDE, SIDE, 2, LANE), jnp.int32),
            pltpu.VMEM((OWNERS, 1, LANE), jnp.int32),
            pltpu.SMEM((OWNERS, 1, LANE), jnp.int32),
            pltpu.VMEM((3 * BATCH, GH * QT, 2 * PT), jnp.float32),
            pltpu.VMEM((3 * BATCH, GH * QT, 2 * PT), jnp.bfloat16),
            pltpu.VMEM((3 * BATCH, QT, GW), jnp.float32),
            pltpu.VMEM((2 * QT, D), jnp.bfloat16),
            pltpu.VMEM((2 * QT, D), jnp.float32),
            pltpu.SemaphoreType.DMA((4,)),
            pltpu.SemaphoreType.DMA((3, SIDE)),
            pltpu.SemaphoreType.DMA((3, SIDE)),
            pltpu.SemaphoreType.DMA((2,)),
            pltpu.SemaphoreType.DMA((3, 3)),
            pltpu.SemaphoreType.DMA((3, 3)),
            pltpu.SemaphoreType.DMA((GROUPS,)),
            pltpu.SemaphoreType.DMA((GROUPS, 3)),
            pltpu.SemaphoreType.DMA((3, GROUPS)),
            pltpu.SemaphoreType.DMA((3, GROUPS)),
        ],
        compiler_params=pltpu.CompilerParams(
            vmem_limit_bytes=60 * 2**20, collective_id=0, has_side_effects=True
        ),
        cost_estimate=pl.CostEstimate(flops=40 * 10**9, bytes_accessed=20 * 2**20, transcendentals=4 * 10**6),
        name="torus",
    )(counts, passage_ids, queries, keys, values, out_weight)


def solution(mesh):
    placed = (
        P(("grp", "dev"), None),
        P(("grp", "dev"), None, None),
        P(("grp", "dev"), None, None),
        P(("grp", "dev")),
        P(("grp", "dev"), None),
        P("grp", None),
    )
    return jax.shard_map(
        on_device, mesh=mesh, in_specs=placed, out_specs=P(("grp", "dev"), None), check_vma=False
    )
```
